32 devices in a mesh: ctx: 16 (over z, y, x), fsdp: 2 (over core).
Axes of the slice: x: 2, y: 2, z: 4, core: 2. Of those that a mesh axis runs over, the one named last changes fastest.
Arguments:
- inputs: bfloat16 [2, 8192, 1024], P('fsdp', 'ctx'), may hold values from -6 to 6
- segments: int32 [2, 8192], P('fsdp'), may hold values from 0 to 8, as said below
- cotangent: bfloat16 [2, 8192, 1024], P('fsdp', 'ctx'), may hold values from -6 to 6
- qkv_weight: bfloat16 [1024, 3072], P(('ctx', 'fsdp')), may hold values from -0.25 to 0.25
- query_bias: bfloat16 [1024], P(('ctx', 'fsdp')), may hold values from -3 to 3
- value_bias: bfloat16 [1024], P(('ctx', 'fsdp')), may hold values from -3 to 3
- out_weight: bfloat16 [1024, 1024], P(('ctx', 'fsdp')), may hold values from -0.75 to 0.75
- out_bias: bfloat16 [1024], P(('ctx', 'fsdp')), may hold values from -3 to 3
- first_gain: bfloat16 [1024], P(('ctx', 'fsdp')), may hold values from 0.099609375 to 1.8984375
- first_shift: bfloat16 [1024], P(('ctx', 'fsdp')), may hold values from -3 to 3
- up_weight: bfloat16 [1024, 4096], P(('ctx', 'fsdp')), may hold values from -0.1875 to 0.1875
- up_bias: bfloat16 [4096], P(('ctx', 'fsdp')), may hold values from -3 to 3
- down_weight: bfloat16 [4096, 1024], P(('ctx', 'fsdp')), may hold values from -0.125 to 0.125
- down_bias: bfloat16 [1024], P(('ctx', 'fsdp')), may hold values from -3 to 3
- second_gain: bfloat16 [1024], P(('ctx', 'fsdp')), may hold values from 0.099609375 to 1.8984375
- second_shift: bfloat16 [1024], P(('ctx', 'fsdp')), may hold values from -3 to 3
Outputs:
- result: bfloat16 [2, 8192, 1024], P('fsdp', 'ctx')
- inputs_grad: bfloat16 [2, 8192, 1024], P('fsdp', 'ctx')
- qkv_weight_grad: float32 [1024, 3072], P(('ctx', 'fsdp'))
- query_bias_grad: float32 [1024], P(('ctx', 'fsdp'))
- value_bias_grad: float32 [1024], P(('ctx', 'fsdp'))
- out_weight_grad: float32 [1024, 1024], P(('ctx', 'fsdp'))
- out_bias_grad: float32 [1024], P(('ctx', 'fsdp'))
- first_gain_grad: float32 [1024], P(('ctx', 'fsdp'))
- first_shift_grad: float32 [1024], P(('ctx', 'fsdp'))
- up_weight_grad: float32 [1024, 4096], P(('ctx', 'fsdp'))
- up_bias_grad: float32 [4096], P(('ctx', 'fsdp'))
- down_weight_grad: float32 [4096, 1024], P(('ctx', 'fsdp'))
- down_bias_grad: float32 [1024], P(('ctx', 'fsdp'))
- second_gain_grad: float32 [1024], P(('ctx', 'fsdp'))
- second_shift_grad: float32 [1024], P(('ctx', 'fsdp'))
The draws below stay inside these ranges and needn't reach their ends.
Inputs may be any that keep to these rules, and one draw needn't show every extreme that they name: `segments`: along each sequence the numbers start at 0, never fall and rise by at most one from a token to the next; each sequence holds 9 documents of any lengths.
All inputs are finite; a program needn't handle non-finite values.
Results may differ from the reference program's by a relative error of at most 0.015.
Values may be sent and summed in bfloat16 or wider, within the bound.
No kernel may reach another device: no remote copies, remote signals or barrier semaphores. Data moves between devices by JAX's collectives and lax.ppermute only.
A program may use at most 192 MiB of HBM per device.

```python
import jax
import jax.numpy as jnp
from jax import lax

D = 1024
H = 16
HD = 64
FF = 4096
WINDOW = 1024
TOK_DEV = 512
SEQ = 8192
SEQS = 2


def draw_segments(key, part):
    key = jax.random.fold_in(key, 11)
    cut_count = SEQ // (2 * TOK_DEV)

    def one_row(row_key):
        cuts = jax.random.permutation(row_key, SEQ - 1)[:cut_count].astype(jnp.int32) + 1
        marks = jnp.zeros((SEQ,), jnp.int32).at[cuts].set(1)
        return jnp.cumsum(marks).astype(jnp.int32)
    return jax.vmap(one_row)(jax.random.split(key, SEQS)).astype(jnp.int32)


def shard_levels(own_key, shape, cuts, smallest, top_value):
    level, own = 1.0, jax.random.fold_in(own_key, 6)
    for axis_at, shards_of in cuts:
        draws = jnp.exp(jax.random.uniform(jax.random.fold_in(own, axis_at), (shards_of,), jnp.float32, smallest / len(cuts), top_value / len(cuts)))
        level = level * jnp.repeat(draws, shape[axis_at] // shards_of).reshape([-1 if axis == axis_at else 1 for axis in range(len(shape))])
    return level


def bell_draw(stream_key, extent, width, most, shards=(), kind=jnp.bfloat16):
    level = shard_levels(stream_key, extent, shards, -0.22, 0.18) if shards else 1.0
    array = jax.random.normal(stream_key, extent, jnp.float32) * width * level
    return jnp.minimum(jnp.maximum(array, -most), most).astype(kind)


def setup_inputs(seed: int = 0) -> dict:
    key_of = jax.random.split(jax.random.key(seed), 17)
    return {
        "inputs": bell_draw(key_of[0], (SEQS, SEQ, D), 1.0, 6.0, ((0, 2), (1, 16))),
        "segments": draw_segments(jax.random.fold_in(key_of[16], 71), 0),
        "cotangent": bell_draw(key_of[2], (SEQS, SEQ, D), 1.0, 6.0, ((0, 2), (1, 16))),
        "qkv_weight": bell_draw(key_of[3], (D, 3 * D), (D // 2) ** -0.5, 0.25, ((0, 32),)),
        "query_bias": bell_draw(key_of[4], (D,), 0.5, 3.0, ((0, 32),)),
        "value_bias": bell_draw(key_of[5], (D,), 0.5, 3.0, ((0, 32),)),
        "out_weight": bell_draw(key_of[6], (D, D), (D // 16) ** -0.5, 0.75, ((0, 32),)),
        "out_bias": bell_draw(key_of[7], (D,), 0.5, 3.0, ((0, 32),)),
        "first_gain": jnp.clip(1.0 + 0.18 * jax.random.normal(key_of[8], (D,), jnp.float32), 0.099609375, 1.8984375).astype(jnp.bfloat16),
        "first_shift": bell_draw(key_of[9], (D,), 0.5, 3.0, ((0, 32),)),
        "up_weight": bell_draw(key_of[10], (D, FF), D ** -0.5, 0.1875, ((0, 32),)),
        "up_bias": bell_draw(key_of[11], (FF,), 0.5, 3.0, ((0, 32),)),
        "down_weight": bell_draw(key_of[12], (FF, D), (FF // 2) ** -0.5, 0.125, ((0, 32),)),
        "down_bias": bell_draw(key_of[13], (D,), 0.5, 3.0, ((0, 32),)),
        "second_gain": jnp.clip(1.0 + 0.18 * jax.random.normal(key_of[14], (D,), jnp.float32), 0.099609375, 1.8984375).astype(jnp.bfloat16),
        "second_shift": bell_draw(key_of[15], (D,), 0.5, 3.0, ((0, 32),)),
    }


@jax.custom_vjp
def low(v):
    return lax.optimization_barrier(v.astype(jnp.bfloat16)).astype(jnp.float32)

@jax.custom_vjp
def low_back(v):
    return v

def low_keep(v):
    return (low(v), None)

def low_pass(kept, grad):
    return (grad,)

def back_keep(v):
    return (v, None)

def back_low(kept, grad):
    return (low(grad),)
low.defvjp(low_keep, low_pass)
low_back.defvjp(back_keep, back_low)
masked_fill = -1e+30
norm_epsilon = 1e-05

def norm_rows(values, gain, shift):
    average = lax.optimization_barrier(jnp.mean(values, axis=-1, keepdims=True))
    centered = values - average
    spread = lax.optimization_barrier(jnp.mean(centered * centered, axis=-1, keepdims=True))
    return centered * lax.rsqrt(spread + norm_epsilon) * gain + shift

def attend(query_rows, key_rows, value_rows, seq_segments):
    half_width = WINDOW // 2
    block_rows = min(512, SEQ)
    count_blocks = SEQ // block_rows
    span_rows = block_rows + 2 * half_width
    score_scale = HD ** (-0.5)
    query_heads = query_rows.reshape(SEQ, H, HD)
    key_padded = jnp.pad(key_rows.reshape(SEQ, H, HD), ((half_width, half_width), (0, 0), (0, 0)))
    value_padded = jnp.pad(value_rows.reshape(SEQ, H, HD), ((half_width, half_width), (0, 0), (0, 0)))
    seg_padded = jnp.pad(seq_segments, (half_width, half_width), constant_values=-1)

    def one_block(block_index):
        row_start = block_index * block_rows
        query_block = lax.dynamic_slice_in_dim(query_heads, row_start, block_rows, 0)
        key_block = lax.dynamic_slice_in_dim(key_padded, row_start, span_rows, 0)
        value_block = lax.dynamic_slice_in_dim(value_padded, row_start, span_rows, 0)
        seg_query = lax.dynamic_slice_in_dim(seq_segments, row_start, block_rows, 0)
        seg_keys = lax.dynamic_slice_in_dim(seg_padded, row_start, span_rows, 0)
        query_pos = row_start + jnp.arange(block_rows, dtype=jnp.int32)
        key_pos = row_start - half_width + jnp.arange(span_rows, dtype=jnp.int32)
        distance = key_pos[None, :] - query_pos[:, None]
        allowed = (seg_query[:, None] == seg_keys[None, :]) & (jnp.abs(distance) < half_width)
        scores = jnp.einsum('qhd,khd->hqk', query_block, key_block, precision=lax.Precision.HIGHEST) * score_scale
        scores = low_back(jnp.where(allowed[None], scores, masked_fill))
        peak = lax.optimization_barrier(jnp.max(scores, axis=-1, keepdims=True))
        expo = jnp.exp(scores - peak)
        probs = expo / lax.optimization_barrier(jnp.sum(expo, axis=-1, keepdims=True))
        return jnp.einsum('hqk,khd->qhd', low(probs), value_block, precision=lax.Precision.HIGHEST)
    blocks = lax.map(jax.checkpoint(one_block), jnp.arange(count_blocks, dtype=jnp.int32))
    return blocks.reshape(SEQ, D)

def block_layer(seq_rows, seq_segments, weights):
    qkv_weight, query_bias, value_bias, out_weight, out_bias, first_gain, first_shift, up_weight, up_bias, down_weight, down_bias, second_gain, second_shift = weights
    mixed = jnp.dot(seq_rows, qkv_weight, precision=lax.Precision.HIGHEST)
    query_rows = low(low_back(mixed[:, :D] + query_bias))
    key_rows = low(low_back(mixed[:, D:2 * D]))
    value_rows = low(low_back(mixed[:, 2 * D:] + value_bias))
    heads = low(low_back(attend(query_rows, key_rows, value_rows, seq_segments)))
    branch = low_back(jnp.dot(heads, out_weight, precision=lax.Precision.HIGHEST) + out_bias)
    first = norm_rows(seq_rows + branch, first_gain, first_shift)
    lifted = low_back(jnp.dot(low(first), up_weight, precision=lax.Precision.HIGHEST) + up_bias)
    active = low(jax.nn.gelu(lifted, approximate=False))
    second = low_back(jnp.dot(active, down_weight, precision=lax.Precision.HIGHEST) + down_bias)
    return norm_rows(first + second, second_gain, second_shift)

def reference(inputs, segments, cotangent, qkv_weight, query_bias, value_bias, out_weight, out_bias, first_gain, first_shift, up_weight, up_bias, down_weight, down_bias, second_gain, second_shift):
    params = tuple((argument.astype(jnp.float32) for argument in (qkv_weight, query_bias, value_bias, out_weight, out_bias, first_gain, first_shift, up_weight, up_bias, down_weight, down_bias, second_gain, second_shift)))

    def forward(values, weights):

        def per_sequence(carry, paired):
            seq_rows, seq_segments = paired
            return (carry, block_layer(seq_rows, seq_segments, weights))
        unused, stacked = lax.scan(per_sequence, jnp.zeros((), jnp.float32), (values, segments))
        return stacked
    output, pullback = jax.vjp(forward, inputs.astype(jnp.float32), params)
    grad_inputs, grads = pullback(cotangent.astype(jnp.float32))
    return (output.astype(jnp.bfloat16), grad_inputs.astype(jnp.bfloat16), grads[0], grads[1], grads[2], grads[3], grads[4], grads[5], grads[6], grads[7], grads[8], grads[9], grads[10], grads[11], grads[12])
```

```python
import functools

import jax
import jax.numpy as jnp
from jax import lax
from jax.experimental import pallas as pl
from jax.experimental.pallas import tpu as pltpu
from jax.sharding import PartitionSpec as P

H = 16
HD = 64
WINDOW = 1024
HALF = WINDOW // 2
ROWS = 128
PAIR = 2 * HD
FILL = -1e30
EPS = 1e-05
F32 = jnp.float32
BF16 = jnp.bfloat16
VMEM_BYTES = 56 * 1024 * 1024


def nn(a, b):
    return lax.dot_general(a, b, (((1,), (0,)), ((), ())), preferred_element_type=F32)


def nt(a, b):
    return lax.dot_general(a, b, (((1,), (1,)), ((), ())), preferred_element_type=F32)


def tn(a, b):
    return lax.dot_general(a, b, (((0,), (0,)), ((), ())), preferred_element_type=F32)


def cat(parts, axis):
    return jnp.concatenate(parts, axis=axis)


def cost(flops, bytes_accessed, exps=0):
    return pl.CostEstimate(flops=flops, bytes_accessed=bytes_accessed, transcendentals=exps)


def params():
    return pltpu.CompilerParams(vmem_limit_bytes=VMEM_BYTES)


def head_masks(scale):
    lane = lax.broadcasted_iota(jnp.int32, (1, PAIR), 1)
    first = jnp.where(lane < HD, scale, 0.0).astype(F32)
    second = jnp.where(lane < HD, 0.0, scale).astype(F32)
    return first.astype(BF16), second.astype(BF16)


def stacked(values, masks):
    return cat([values * masks[0], values * masks[1]], 0)


def strip(i, tokens):
    return slice(ROWS * i, ROWS * i + tokens + ROWS)


def attend_kernel(q_ref, ko_ref, kp_ref, kn_ref, vo_ref, vp_ref, vn_ref, bo_ref, bh_ref, out_ref, lse_ref, kh, vh):
    tokens = q_ref.shape[0]
    kh[:tokens] = kp_ref[...]
    kh[tokens:] = kn_ref[...]
    ones = head_masks(1.0)
    vh[:tokens] = vp_ref[...]
    vh[tokens:] = vn_ref[...]
    vo = stacked(vo_ref[...], ones)
    scaled = head_masks(HD ** -0.5)
    lane = lax.broadcasted_iota(jnp.int32, (ROWS, PAIR), 1)
    for i in range(tokens // ROWS):
        rows = slice(ROWS * i, ROWS * i + ROWS)
        window = strip(i, tokens)
        q = q_ref[rows]
        own_parts, halo_parts, totals, logs = [], [], [], []
        for mask in scaled:
            qm = q * mask
            so = nt(qm, ko_ref[...]) + bo_ref[rows]
            sh = nt(qm, kh[window]) + bh_ref[i]
            peak = jnp.maximum(jnp.max(so, axis=1, keepdims=True), jnp.max(sh, axis=1, keepdims=True))
            po = jnp.exp(so - peak)
            ph = jnp.exp(sh - peak)
            total = jnp.sum(po, axis=1, keepdims=True) + jnp.sum(ph, axis=1, keepdims=True)
            own_parts.append(po.astype(BF16))
            halo_parts.append(ph.astype(BF16))
            totals.append(1.0 / total)
            logs.append(peak + jnp.log(total))
        out = nn(cat(own_parts, 1), vo) + nn(cat(halo_parts, 1), stacked(vh[window], ones))
        out = out * jnp.where(lane < HD, totals[0], totals[1])
        out_ref[rows] = out.astype(BF16)
        lse_ref[0, rows] = cat(logs, 1)


def attend(mixed, before, after, bias_own, bias_halo):
    tokens, width = mixed.shape[0], mixed.shape[1] // 3
    pairs = width // PAIR

    def column(part):
        return pl.BlockSpec((tokens, PAIR), lambda p: (0, part * pairs + p))

    whole = lambda shape: pl.BlockSpec(shape, lambda p: (0,) * len(shape))
    return pl.pallas_call(
        attend_kernel,
        grid=(pairs,),
        in_specs=[column(0), column(1), column(1), column(1), column(2), column(2), column(2), whole(bias_own.shape), whole(bias_halo.shape)],
        out_specs=[pl.BlockSpec((tokens, PAIR), lambda p: (0, p)), pl.BlockSpec((1, tokens, 2), lambda p: (p, 0, 0))],
        out_shape=[jax.ShapeDtypeStruct((tokens, width), BF16), jax.ShapeDtypeStruct((pairs, tokens, 2), F32)],
        scratch_shapes=[pltpu.VMEM((2 * tokens, PAIR), BF16), pltpu.VMEM((2 * tokens, PAIR), BF16)],
        compiler_params=params(),
        cost_estimate=cost(4 * tokens * 9 * ROWS * width * 4, 16 * tokens * width, H * tokens * 9 * ROWS),
        name="attend",
    )(mixed, mixed, before, after, mixed, before, after, bias_own, bias_halo)


def own_grad_kernel(q_ref, ko_ref, kp_ref, kn_ref, vo_ref, vp_ref, vn_ref, do_ref, lc_ref, dc_ref, lr_ref, dr_ref, bo_ref, bh_ref, dq_ref, dk_ref, dv_ref, kh, vh):
    tokens = q_ref.shape[0]
    kh[:tokens] = kp_ref[...]
    kh[tokens:] = kn_ref[...]
    vh[:tokens] = vp_ref[...]
    vh[tokens:] = vn_ref[...]
    ones = head_masks(1.0)
    scaled = head_masks(HD ** -0.5)
    k_own = ko_ref[...]
    v_own = vo_ref[...]
    k_pair = stacked(k_own, scaled)
    chunk = 2 * ROWS
    for c in range(tokens // chunk):
        cols = slice(chunk * c, chunk * c + chunk)
        q = q_ref[cols]
        do = do_ref[cols]
        probs, grads, qs, dos = [], [], [], []
        for h in range(2):
            qm = q * scaled[h]
            dm = do * ones[h]
            st = nt(k_own, qm) + bo_ref[:, cols]
            pt = jnp.exp(st - lr_ref[0, h : h + 1, cols])
            gt = pt * (nt(v_own, dm) - dr_ref[0, h : h + 1, cols])
            probs.append(pt.astype(BF16))
            grads.append(gt.astype(BF16))
            qs.append(qm)
            dos.append(dm)
        dv = nn(cat(probs, 1), cat(dos, 0))
        dk = nn(cat(grads, 1), cat(qs, 0))
        if c == 0:
            dv_ref[...] = dv
            dk_ref[...] = dk
        else:
            dv_ref[...] += dv
            dk_ref[...] += dk
        dq_own = tn(cat(grads, 0), k_pair)
        for r in range(chunk // ROWS):
            i = c * (chunk // ROWS) + r
            rows = slice(ROWS * i, ROWS * i + ROWS)
            window = strip(i, tokens)
            halo = []
            for h in range(2):
                qm = q[ROWS * r : ROWS * r + ROWS] * scaled[h]
                dm = do[ROWS * r : ROWS * r + ROWS] * ones[h]
                s = nt(qm, kh[window]) + bh_ref[i]
                p = jnp.exp(s - lc_ref[0, rows, h : h + 1])
                halo.append((p * (nt(dm, vh[window]) - dc_ref[0, rows, h : h + 1])).astype(BF16))
            dq = dq_own[ROWS * r : ROWS * r + ROWS] + nn(cat(halo, 1), stacked(kh[window], scaled))
            dq_ref[rows] = dq.astype(BF16)


def own_grads(mixed, before, after, grad_heads, log_cols, mean_cols, log_rows, mean_rows, bias_own, bias_halo):
    tokens, width = grad_heads.shape
    pairs = width // PAIR

    def column(part):
        return pl.BlockSpec((tokens, PAIR), lambda p: (0, part * pairs + p))

    whole = lambda shape: pl.BlockSpec(shape, lambda p: (0,) * len(shape))
    cols = pl.BlockSpec((1, tokens, 2), lambda p: (p, 0, 0))
    rows = pl.BlockSpec((1, 2, tokens), lambda p: (p, 0, 0))
    block = pl.BlockSpec((tokens, PAIR), lambda p: (0, p))
    return pl.pallas_call(
        own_grad_kernel,
        grid=(pairs,),
        in_specs=[column(0), column(1), column(1), column(1), column(2), column(2), column(2), block, cols, cols, rows, rows, whole(bias_own.shape), whole(bias_halo.shape)],
        out_specs=[block, block, block],
        out_shape=[
            jax.ShapeDtypeStruct((tokens, width), BF16),
            jax.ShapeDtypeStruct((tokens, width), F32),
            jax.ShapeDtypeStruct((tokens, width), F32),
        ],
        scratch_shapes=[pltpu.VMEM((2 * tokens, PAIR), BF16), pltpu.VMEM((2 * tokens, PAIR), BF16)],
        compiler_params=params(),
        cost_estimate=cost(10 * tokens * 9 * ROWS * width * 4, 30 * tokens * width, H * tokens * 9 * ROWS),
        name="own_grads",
    )(mixed, mixed, before, after, mixed, before, after, grad_heads, log_cols, mean_cols, log_rows, mean_rows, bias_own, bias_halo)


def halo_grad_kernel(ko_ref, vo_ref, qp_ref, qn_ref, dp_ref, dn_ref, lp_ref, ln_ref, bh_ref, dk_in, dv_in, dk_ref, dv_ref, qh, dh, lh):
    tokens = ko_ref.shape[0]
    qh[:tokens] = qp_ref[...]
    qh[tokens:] = qn_ref[...]
    dh[:tokens] = dp_ref[...]
    dh[tokens:] = dn_ref[...]
    lh[:, :, :tokens] = lp_ref[:, 0]
    lh[:, :, tokens:] = ln_ref[:, 0]
    ones = head_masks(1.0)
    scaled = head_masks(HD ** -0.5)
    for j in range(tokens // ROWS):
        rows = slice(ROWS * j, ROWS * j + ROWS)
        window = strip(j, tokens)
        q = qh[window]
        do = dh[window]
        k = ko_ref[rows]
        v = vo_ref[rows]
        probs, grads, qs, dos = [], [], [], []
        for h in range(2):
            qm = q * scaled[h]
            dm = do * ones[h]
            st = nt(k, qm) + bh_ref[j]
            pt = jnp.exp(st - lh[0, h : h + 1, window])
            gt = pt * (nt(v, dm) - lh[1, h : h + 1, window])
            probs.append(pt.astype(BF16))
            grads.append(gt.astype(BF16))
            qs.append(qm)
            dos.append(dm)
        dk_ref[rows] = (dk_in[rows] + nn(cat(grads, 1), cat(qs, 0))).astype(BF16)
        dv_ref[rows] = (dv_in[rows] + nn(cat(probs, 1), cat(dos, 0))).astype(BF16)


def halo_grads(mixed, before, after, grad_before, grad_after, rows_before, rows_after, bias_halo, dk, dv):
    tokens, width = dk.shape
    pairs = width // PAIR

    def column(part):
        return pl.BlockSpec((tokens, PAIR), lambda p: (0, part * pairs + p))

    whole = lambda shape: pl.BlockSpec(shape, lambda p: (0,) * len(shape))
    rows = pl.BlockSpec((2, 1, 2, tokens), lambda p: (0, p, 0, 0))
    block = pl.BlockSpec((tokens, PAIR), lambda p: (0, p))
    return pl.pallas_call(
        halo_grad_kernel,
        grid=(pairs,),
        in_specs=[column(1), column(2), column(0), column(0), block, block, rows, rows, whole(bias_halo.shape), block, block],
        out_specs=[block, block],
        out_shape=[jax.ShapeDtypeStruct((tokens, width), BF16)] * 2,
        scratch_shapes=[pltpu.VMEM((2 * tokens, PAIR), BF16), pltpu.VMEM((2 * tokens, PAIR), BF16), pltpu.VMEM((2, 2, 2 * tokens), F32)],
        compiler_params=params(),
        cost_estimate=cost(8 * tokens * 5 * ROWS * width * 4, 20 * tokens * width, H * tokens * 5 * ROWS),
        name="halo_grads",
    )(mixed, mixed, before, after, grad_before, grad_after, rows_before, rows_after, bias_halo, dk, dv)


def mask_biases(segments, place, blocks, tokens):
    line = cat([jnp.full((tokens,), -1, jnp.int32), segments, jnp.full((tokens,), -1, jnp.int32)], 0)
    near = lax.dynamic_slice_in_dim(line, place * tokens, 3 * tokens)
    own = near[tokens : 2 * tokens]
    bias_own = jnp.where(own[:, None] == own[None, :], 0.0, FILL).astype(F32)
    halo = cat([near[:tokens], near[2 * tokens :]], 0)
    at = jnp.arange(tokens, dtype=jnp.int32)
    halo_at = cat([at - tokens, at + tokens], 0)
    allowed = (own[:, None] == halo[None, :]) & (jnp.abs(halo_at[None, :] - at[:, None]) < HALF)
    bias = jnp.where(allowed, 0.0, FILL).astype(F32)
    bias_halo = jnp.stack([bias[ROWS * i : ROWS * i + ROWS, strip(i, tokens)] for i in range(tokens // ROWS)])
    return bias_own, bias_halo


def normalized(values):
    average = jnp.mean(values, axis=1, keepdims=True)
    centered = values - average
    spread = jnp.mean(centered * centered, axis=1, keepdims=True)
    inverse = lax.rsqrt(spread + EPS)
    return centered * inverse, inverse


def norm_back(grad, gain, hat, inverse):
    scaled = grad * gain
    return inverse * (
        scaled
        - jnp.mean(scaled, axis=1, keepdims=True)
        - hat * jnp.mean(scaled * hat, axis=1, keepdims=True)
    )


def column_sum(values):
    return jnp.sum(values, axis=0, keepdims=True)


def part_blocks(at_ref, order, second, far):
    for first in range(2):
        rel = {order[0]: first, order[1]: second}
        y = jnp.bitwise_xor(at_ref[0], rel["y"])
        x = jnp.bitwise_xor(at_ref[1], rel["x"])
        for z in range(far):
            yield first, z, (z * 2 + y) * 2 + x


def start_all(copies):
    for copy in copies:
        copy.start()


def wait_all(copies):
    for copy in copies:
        copy.wait()


def flipped_rows(values, flipped, at_ref, far):
    turned = values.T
    if far is None:
        flipped[...] = turned
        return
    rows = turned.shape[0] // (4 * far)
    for z in range(far):
        for y in range(2):
            for x in range(2):
                a = (z * 2 + y) * 2 + x
                to = (jnp.bitwise_xor(at_ref[1], x) * 2 + jnp.bitwise_xor(at_ref[0], y)) * far + z
                flipped[pl.ds(pl.multiple_of(to * rows, rows), rows)] = turned[a * rows : a * rows + rows]


def qkv_copies(refs, full, sems, at_ref, far):
    if far is None:
        return [pltpu.make_async_copy(refs[0], full, sems.at[0])]
    width, columns = full.shape
    rows, half = width // (8 * far), columns // 2
    copies = []
    for core in range(2):
        at_half = jnp.bitwise_xor(at_ref[2], core)
        for color, order in enumerate(("yx", "xy")):
            for second in range(2):
                ref = refs[core * 4 + color * 2 + second]
                for first, z, block in part_blocks(at_ref, order, second, far):
                    row = pl.multiple_of((block * 2 + color) * rows, rows)
                    to = full.at[pl.ds(row, rows), pl.ds(pl.multiple_of(at_half * half, half), half)]
                    copies.append(pltpu.make_async_copy(ref.at[first, z, :, pl.ds(0, half)], to, sems.at[len(copies)]))
    return copies


def project_kernel(far, parts, *refs):
    at_ref, refs = refs[0], refs[1:]
    part_refs, refs = refs[:parts], refs[parts:]
    own_ref, before_ref, after_ref, row_ref, own_out, before_out, after_out, full_out, full, sems, out_sem = refs
    copies = qkv_copies(part_refs, full, sems, at_ref, far)
    start_all(copies)
    wait_all(copies)
    keep = pltpu.make_async_copy(full, full_out, out_sem)
    keep.start()
    chunk = 512
    for source, target in ((own_ref, own_out), (before_ref, before_out), (after_ref, after_out)):

        def body(j, carry, source=source, target=target):
            cols = pl.ds(pl.multiple_of(j * chunk, chunk), chunk)
            target[:, cols] = (nn(source[...], full[:, cols]) + row_ref[:, cols]).astype(BF16)
            return carry

        lax.fori_loop(0, full.shape[1] // chunk, body, 0)
    keep.wait()


SMEM = pl.BlockSpec(memory_space=pltpu.SMEM)
ANY = pl.BlockSpec(memory_space=pl.ANY)
VMEM = pl.BlockSpec(memory_space=pltpu.VMEM)


def copy_count(far, each):
    return 1 if far is None else 8 * far * each


def project(far, at, parts, x, before, after, row):
    tokens, width = x.shape
    columns = row.shape[1]
    mixed = jax.ShapeDtypeStruct((tokens, columns), BF16)
    return pl.pallas_call(
        functools.partial(project_kernel, far, len(parts)),
        in_specs=[SMEM] + [ANY] * len(parts) + [VMEM] * 4,
        out_specs=[VMEM, VMEM, VMEM, ANY],
        out_shape=[mixed, mixed, mixed, jax.ShapeDtypeStruct((width, columns), BF16)],
        scratch_shapes=[
            pltpu.VMEM((width, columns), BF16),
            pltpu.SemaphoreType.DMA((copy_count(far, 4),)),
            pltpu.SemaphoreType.DMA,
        ],
        compiler_params=params(),
        cost_estimate=cost(6 * tokens * width * columns, 4 * width * columns + 8 * tokens * columns),
        name="project",
    )(at, *parts, x, before, after, row)


def out_copies(refs, full, sems, at_ref, far):
    if far is None:
        return [pltpu.make_async_copy(refs[0], full, sems.at[0])]
    width = full.shape[0]
    rows, half = width // (8 * far), width // 2
    copies = []
    for core in range(2):
        col = pl.multiple_of(jnp.bitwise_xor(at_ref[2], core) * half, half)
        for second in range(2):
            ref = refs[core * 2 + second]
            skip = ref.shape[2] - rows
            for first, z, block in part_blocks(at_ref, "xy", second, far):
                for side in range(2):
                    row = pl.multiple_of((block * 2 + side) * rows, rows)
                    copies.append(
                        pltpu.make_async_copy(
                            ref.at[first, z, pl.ds(skip, rows), pl.ds(side * half, half)],
                            full.at[pl.ds(row, rows), pl.ds(col, half)],
                            sems.at[len(copies)],
                        )
                    )
    return copies


def out_kernel(far, parts, *refs):
    at_ref, refs = refs[0], refs[1:]
    part_refs, refs = refs[:parts], refs[parts:]
    heads_ref, x_ref, vec_ref, hat_ref, inv_ref, first_ref, low_ref, full_out, full, sems, out_sem = refs
    copies = out_copies(part_refs, full, sems, at_ref, far)
    keep = pltpu.make_async_copy(full, full_out, out_sem)

    @pl.when(pl.program_id(0) == 0)
    def _():
        start_all(copies)
        wait_all(copies)
        keep.start()

    branch = nn(heads_ref[...], full[...]) + vec_ref[0:1]
    hat, inverse = normalized(x_ref[...].astype(F32) + branch)
    first = hat * vec_ref[1:2] + vec_ref[2:3]
    hat_ref[...] = hat
    inv_ref[...] = inverse
    first_ref[...] = first
    low_ref[...] = first.astype(BF16)

    @pl.when(pl.program_id(0) == pl.num_programs(0) - 1)
    def _():
        keep.wait()


def out_project(far, at, parts, heads, x, vectors):
    tokens, width = heads.shape
    rows = tokens // 4
    block = pl.BlockSpec((rows, width), lambda i: (i, 0))
    return pl.pallas_call(
        functools.partial(out_kernel, far, len(parts)),
        grid=(4,),
        in_specs=[SMEM] + [ANY] * len(parts) + [block, block, pl.BlockSpec(vectors.shape, lambda i: (0, 0))],
        out_specs=[block, pl.BlockSpec((rows, 1), lambda i: (i, 0)), block, block, ANY],
        out_shape=[
            jax.ShapeDtypeStruct((tokens, width), F32),
            jax.ShapeDtypeStruct((tokens, 1), F32),
            jax.ShapeDtypeStruct((tokens, width), F32),
            jax.ShapeDtypeStruct((tokens, width), BF16),
            jax.ShapeDtypeStruct((width, width), BF16),
        ],
        scratch_shapes=[
            pltpu.VMEM((width, width), BF16),
            pltpu.SemaphoreType.DMA((copy_count(far, 4),)),
            pltpu.SemaphoreType.DMA,
        ],
        compiler_params=params(),
        cost_estimate=cost(2 * tokens * width * width, 16 * tokens * width),
        name="out_project",
    )(at, *parts, heads, x, vectors)


def up_copies(refs, full, sems, at_ref, far):
    if far is None:
        return [pltpu.make_async_copy(refs[0], full, sems.at[0])]
    width, hidden = full.shape
    rows, half = width // (4 * far), hidden // 2
    copies = []
    for core in range(2):
        col = pl.multiple_of(jnp.bitwise_xor(at_ref[2], core) * half, half)
        for second in range(2):
            ref = refs[core * 2 + second]
            for first, z, block in part_blocks(at_ref, "yx", second, far):
                to = full.at[pl.ds(pl.multiple_of(block * rows, rows), rows), pl.ds(col, half)]
                copies.append(pltpu.make_async_copy(ref.at[first, z], to, sems.at[len(copies)]))
    return copies


def down_copies(refs, full, sems, at_ref, far):
    if far is None:
        return [pltpu.make_async_copy(refs[0], full, sems.at[0])]
    rows = full.shape[0] // (8 * far)
    copies = []
    for core in range(2):
        side = jnp.bitwise_xor(at_ref[2], core)
        for second in range(2):
            ref = refs[core * 2 + second]
            for first, z, block in part_blocks(at_ref, "xy", second, far):
                to = full.at[pl.ds(pl.multiple_of((block * 2 + side) * rows, rows), rows)]
                copies.append(pltpu.make_async_copy(ref.at[first, z, pl.ds(0, rows)], to, sems.at[len(copies)]))
    return copies


def forward_kernel(far, ups, downs, *refs):
    at_ref, refs = refs[0], refs[1:]
    up_refs, down_refs, refs = refs[:ups], refs[ups : ups + downs], refs[ups + downs :]
    low_ref, first_ref, upb_ref, vec_ref, dy_ref, act_ref, slope_ref, result_ref, grad_ref, glow_ref, sums_ref, up_out, down_out = refs[:13]
    total, up_full, down_full, up_sems, down_sems, out_sems = refs[13:]
    step = pl.program_id(0)
    chunk = act_ref.shape[1]
    cols = pl.ds(pl.multiple_of(step * chunk, chunk), chunk)
    from_up = up_copies(up_refs, up_full, up_sems, at_ref, far)
    from_down = down_copies(down_refs, down_full, down_sems, at_ref, far)
    keep_up = pltpu.make_async_copy(up_full, up_out, out_sems.at[0])
    keep_down = pltpu.make_async_copy(down_full, down_out, out_sems.at[1])

    @pl.when(step == 0)
    def _():
        start_all(from_up)
        start_all(from_down)
        wait_all(from_up)
        keep_up.start()

    lifted = nn(low_ref[...], up_full[:, cols]) + upb_ref[...]
    phi = 0.5 * (1.0 + lax.erf(lifted * (0.5 ** 0.5)))
    density = jnp.exp(lifted * lifted * -0.5) * 0.3989422804014327
    active = (lifted * phi).astype(BF16)
    act_ref[...] = active
    slope_ref[...] = phi + lifted * density

    @pl.when(step == 0)
    def _():
        wait_all(from_down)
        keep_down.start()

    part = nn(active, down_full[cols])

    @pl.when(step == 0)
    def _():
        total[...] = part

    @pl.when(step > 0)
    def _():
        total[...] += part

    @pl.when(step == pl.num_programs(0) - 1)
    def _():
        rows = total.shape[0] // 4
        sums = None
        for i in range(4):
            at = slice(rows * i, rows * i + rows)
            hat, inverse = normalized(first_ref[at] + (total[at] + vec_ref[0:1]))
            result_ref[at] = (hat * vec_ref[1:2] + vec_ref[2:3]).astype(BF16)
            dy = dy_ref[at].astype(F32)
            grad = norm_back(dy, vec_ref[1:2], hat, inverse)
            low = grad.astype(BF16)
            grad_ref[at] = grad
            glow_ref[at] = low
            part = cat([column_sum(dy * hat), column_sum(dy), column_sum(low.astype(F32))], 0)
            sums = part if sums is None else sums + part
        sums_ref[...] = sums
        keep_up.wait()
        keep_down.wait()


def forward(far, at, up_parts, down_parts, low, first, up_bias, vectors, dy, chunk=512):
    tokens, width = low.shape
    hidden = up_bias.shape[1]
    whole = lambda shape: pl.BlockSpec(shape, lambda i: (0, 0))
    return pl.pallas_call(
        functools.partial(forward_kernel, far, len(up_parts), len(down_parts)),
        grid=(hidden // chunk,),
        in_specs=[SMEM]
        + [ANY] * (len(up_parts) + len(down_parts))
        + [
            whole((tokens, width)),
            whole((tokens, width)),
            pl.BlockSpec((1, chunk), lambda i: (0, i)),
            whole(vectors.shape),
            whole((tokens, width)),
        ],
        out_specs=[
            pl.BlockSpec((tokens, chunk), lambda i: (0, i)),
            pl.BlockSpec((tokens, chunk), lambda i: (0, i)),
            whole((tokens, width)),
            whole((tokens, width)),
            whole((tokens, width)),
            whole((3, width)),
            ANY,
            ANY,
        ],
        out_shape=[
            jax.ShapeDtypeStruct((tokens, hidden), BF16),
            jax.ShapeDtypeStruct((tokens, hidden), F32),
            jax.ShapeDtypeStruct((tokens, width), BF16),
            jax.ShapeDtypeStruct((tokens, width), F32),
            jax.ShapeDtypeStruct((tokens, width), BF16),
            jax.ShapeDtypeStruct((3, width), F32),
            jax.ShapeDtypeStruct((width, hidden), BF16),
            jax.ShapeDtypeStruct((hidden, width), BF16),
        ],
        scratch_shapes=[
            pltpu.VMEM((tokens, width), F32),
            pltpu.VMEM((width, hidden), BF16),
            pltpu.VMEM((hidden, width), BF16),
            pltpu.SemaphoreType.DMA((copy_count(far, 2),)),
            pltpu.SemaphoreType.DMA((copy_count(far, 2),)),
            pltpu.SemaphoreType.DMA((2,)),
        ],
        compiler_params=params(),
        cost_estimate=cost(4 * tokens * width * hidden, 8 * width * hidden + 6 * tokens * hidden, 2 * tokens * hidden),
        name="feed_forward",
    )(at, *up_parts, *down_parts, low, first, up_bias, vectors, dy)


def down_grad_kernel(far, at_ref, glow_ref, down_ref, slope_ref, act_ref, lift_ref, keep_ref, send_ref, ub_ref):
    step = pl.program_id(0)
    glow = glow_ref[...]
    lift = (nt(glow, down_ref[...]) * slope_ref[...]).astype(BF16)
    lift_ref[...] = lift
    ub_ref[...] = column_sum(lift.astype(F32))
    dw = tn(act_ref[...], glow).astype(BF16)
    chunk = dw.shape[0]
    if far is None:
        half = keep_ref.shape[0] // chunk

        @pl.when(step < half)
        def _():
            keep_ref[pl.ds(pl.multiple_of(step * chunk, chunk), chunk)] = dw

        @pl.when(step >= half)
        def _():
            send_ref[pl.ds(pl.multiple_of((step - half) * chunk, chunk), chunk)] = dw

        return
    rows = keep_ref.shape[0] // (4 * far)
    for j in range(chunk // rows):
        block, side = step * (chunk // rows // 2) + j // 2, j % 2
        z, y, x = block // 4, block // 2 % 2, block % 2
        to = (jnp.bitwise_xor(at_ref[0], y) * 2 + jnp.bitwise_xor(at_ref[1], x)) * far + z
        rows_to = pl.ds(pl.multiple_of(to * rows, rows), rows)
        value = dw[j * rows : j * rows + rows]

        @pl.when(at_ref[2] == side)
        def _(value=value, rows_to=rows_to):
            keep_ref[rows_to] = value

        @pl.when(at_ref[2] != side)
        def _(value=value, rows_to=rows_to):
            send_ref[rows_to] = value


def down_grads(far, at, glow, down_full, slope, active, chunk=512):
    tokens, width = glow.shape
    hidden = down_full.shape[0]
    block = pl.BlockSpec((tokens, chunk), lambda i: (0, i))
    half = pl.BlockSpec((hidden // 2, width), lambda i: (0, 0))
    return pl.pallas_call(
        functools.partial(down_grad_kernel, far),
        grid=(hidden // chunk,),
        in_specs=[SMEM, pl.BlockSpec((tokens, width), lambda i: (0, 0)), pl.BlockSpec((chunk, width), lambda i: (i, 0)), block, block],
        out_specs=[block, half, half, pl.BlockSpec((1, chunk), lambda i: (0, i))],
        out_shape=[
            jax.ShapeDtypeStruct((tokens, hidden), BF16),
            jax.ShapeDtypeStruct((hidden // 2, width), BF16),
            jax.ShapeDtypeStruct((hidden // 2, width), BF16),
            jax.ShapeDtypeStruct((1, hidden), F32),
        ],
        compiler_params=params(),
        cost_estimate=cost(4 * tokens * width * hidden, 4 * width * hidden + 8 * tokens * hidden),
        name="down_grads",
    )(at, glow, down_full, slope, active)


def split_store(at_ref, half, keep_ref, send_ref, cols, value):
    @pl.when(at_ref[2] == half)
    def _():
        keep_ref[:, cols] = value

    @pl.when(at_ref[2] != half)
    def _():
        send_ref[:, cols] = value


def up_grad_kernel(far, at_ref, low_ref, lift_ref, up_ref, grad_ref, hat_ref, inv_ref, gain_ref, keep_ref, send_ref, one_ref, branch_ref, sums_ref, total, flipped):
    step = pl.program_id(0)

    @pl.when(step == 0)
    def _():
        flipped_rows(low_ref[...], flipped, at_ref, far)

    lift = lift_ref[...]
    dw = nn(flipped[...], lift).astype(BF16)
    chunk = dw.shape[1]
    steps = keep_ref.shape[1] // chunk
    cols = pl.ds(pl.multiple_of(step % steps * chunk, chunk), chunk)
    split_store(at_ref, step // steps, keep_ref, send_ref, cols, dw)
    part = nt(lift, up_ref[...])

    @pl.when(step == 0)
    def _():
        total[...] = grad_ref[...] + part

    @pl.when(step > 0)
    def _():
        total[...] += part

    @pl.when(step == pl.num_programs(0) - 1)
    def _():
        rows = total.shape[0] // 4
        sums = None
        for i in range(4):
            at = slice(rows * i, rows * i + rows)
            grad = total[at]
            hat = hat_ref[at]
            one = norm_back(grad, gain_ref[...], hat, inv_ref[at])
            branch = one.astype(BF16)
            one_ref[at] = one
            branch_ref[at] = branch
            part = cat([column_sum(grad * hat), column_sum(grad), column_sum(branch.astype(F32))], 0)
            sums = part if sums is None else sums + part
        sums_ref[...] = sums


def up_grads(far, at, low, lift, up_full, grad_two, hat, inverse, gain, chunk=512):
    tokens, width = low.shape
    hidden = up_full.shape[1]
    whole = lambda shape: pl.BlockSpec(shape, lambda i: (0, 0))
    half = whole((width, hidden // 2))
    return pl.pallas_call(
        functools.partial(up_grad_kernel, far),
        grid=(hidden // chunk,),
        in_specs=[
            SMEM,
            whole((tokens, width)),
            pl.BlockSpec((tokens, chunk), lambda i: (0, i)),
            pl.BlockSpec((width, chunk), lambda i: (0, i)),
            whole((tokens, width)),
            whole((tokens, width)),
            whole((tokens, 1)),
            whole((1, width)),
        ],
        out_specs=[half, half, whole((tokens, width)), whole((tokens, width)), whole((3, width))],
        out_shape=[
            jax.ShapeDtypeStruct((width, hidden // 2), BF16),
            jax.ShapeDtypeStruct((width, hidden // 2), BF16),
            jax.ShapeDtypeStruct((tokens, width), F32),
            jax.ShapeDtypeStruct((tokens, width), BF16),
            jax.ShapeDtypeStruct((3, width), F32),
        ],
        scratch_shapes=[pltpu.VMEM((tokens, width), F32), pltpu.VMEM((width, tokens), BF16)],
        compiler_params=params(),
        cost_estimate=cost(4 * tokens * width * hidden, 4 * width * hidden + 2 * tokens * hidden),
        name="up_grads",
    )(at, low, lift, up_full, grad_two, hat, inverse, gain)


def out_grad_kernel(far, at_ref, branch_ref, w_ref, heads_ref, gh_ref, mean_ref, keep_ref, send_ref, flipped):
    width = branch_ref.shape[1]
    branch = branch_ref[...]
    heads = heads_ref[...]
    grad = nt(branch, w_ref[...]).astype(BF16)
    gh_ref[...] = grad
    flipped_rows(heads, flipped, at_ref, far)
    half = width // 2
    for j in range(2):
        dw = nn(flipped[...], branch[:, j * half : j * half + half]).astype(BF16)
        split_store(at_ref, j, keep_ref, send_ref, slice(None), dw)
    product = grad.astype(F32) * heads.astype(F32)
    head = lax.broadcasted_iota(jnp.int32, (width, H), 0) // HD
    pick = jnp.where(head == lax.broadcasted_iota(jnp.int32, (width, H), 1), 1.0, 0.0).astype(F32)
    mean_ref[...] = lax.dot_general(product, pick, (((1,), (0,)), ((), ())), precision=lax.Precision.HIGHEST, preferred_element_type=F32)


def out_grads(far, at, branch, out_full, heads):
    tokens, width = branch.shape
    half = jax.ShapeDtypeStruct((width, width // 2), BF16)
    return pl.pallas_call(
        functools.partial(out_grad_kernel, far),
        in_specs=[SMEM, VMEM, VMEM, VMEM],
        out_shape=[jax.ShapeDtypeStruct((tokens, width), BF16), jax.ShapeDtypeStruct((tokens, H), F32), half, half],
        scratch_shapes=[pltpu.VMEM((width, tokens), BF16)],
        compiler_params=params(),
        cost_estimate=cost(4 * tokens * width * width, 4 * width * width + 6 * tokens * width),
        name="out_grads",
    )(at, branch, out_full, heads)


def qkv_grad_kernel(far, at_ref, x_ref, dq_ref, dk_ref, dv_ref, keep_ref, send_ref, sums_ref, flipped):
    flipped_rows(x_ref[...], flipped, at_ref, far)
    chunk = 512
    parts = [(ref, j) for ref in (dq_ref, dk_ref, dv_ref) for j in range(ref.shape[1] // chunk)]
    for n, (ref, j) in enumerate(parts):
        dw = nn(flipped[...], ref[:, j * chunk : j * chunk + chunk]).astype(BF16)
        half = n // (len(parts) // 2)
        to = n % (len(parts) // 2) * chunk
        split_store(at_ref, half, keep_ref, send_ref, slice(to, to + chunk), dw)
    sums_ref[...] = cat([column_sum(dq_ref[...].astype(F32)), column_sum(dv_ref[...].astype(F32))], 0)


def qkv_grads(far, at, x, dq, dk, dv):
    tokens, width = x.shape
    half = jax.ShapeDtypeStruct((width, 3 * width // 2), BF16)
    return pl.pallas_call(
        functools.partial(qkv_grad_kernel, far),
        in_specs=[SMEM] + [VMEM] * 4,
        out_shape=[half, half, jax.ShapeDtypeStruct((2, width), F32)],
        scratch_shapes=[pltpu.VMEM((width, tokens), BF16)],
        compiler_params=params(),
        cost_estimate=cost(6 * tokens * width * width, 12 * width * width + 8 * tokens * width),
        name="qkv_grads",
    )(at, x, dq, dk, dv)


FAR, Y, X, CORE = "far", "y", "x", "fsdp"
CTX = (FAR, Y, X)
ALL = CTX + (CORE,)


def swap(values, axis):
    return lax.ppermute(values, axis, [(0, 1), (1, 0)])


def choose(core, left, right):
    return jnp.where(core == 0, left, right), jnp.where(core == 0, right, left)


def halves(values):
    middle = values.shape[1] // 2
    return values[:, :middle], values[:, middle:]


def added(*terms):
    total = terms[0].astype(F32)
    for term in terms[1:]:
        total = total + term.astype(F32)
    return total.astype(BF16)


def gather_first(block):
    wide = lax.all_gather(block, FAR, axis=0)
    parts = []
    for color, (one, two) in enumerate(((Y, X), (X, Y))):
        mine = wide[:, color]
        pair = jnp.stack([mine, swap(mine, one)])
        parts += [pair, swap(pair, two)]
    return parts


def gather_up(block):
    wide = lax.all_gather(block, FAR, axis=0)
    pair = jnp.stack([wide, swap(wide, Y)])
    return [pair, swap(pair, X)]


def gather_down(block):
    pair = jnp.stack([block, swap(block, X)])
    wide = lax.all_gather(pair, FAR, axis=1)
    return [wide, swap(wide, Y)]


def scatter_up(keep, got):
    there = swap(added(keep[1], got[1]), X)
    there_y = swap(added(keep[0, 1], got[0, 1], there[1]), Y)
    mine = added(keep[0, 0], got[0, 0], there[0], there_y)
    return lax.psum_scatter(mine, FAR, scatter_dimension=0, tiled=False)


def scatter_down(keep, got):
    there = swap(added(keep[1], got[1]), Y)
    mine = added(keep[0], got[0], there)
    wide = lax.psum_scatter(mine.swapaxes(0, 1), FAR, scatter_dimension=0, tiled=False)
    return wide[0].astype(F32) + swap(wide[1], X).astype(F32)


def scatter_last(keep, got):
    a, b = keep[:, :, :, 0], got[:, :, :, 0]
    there = swap(added(a[1], b[1]), X)
    there_y = swap(added(a[0, 1], b[0, 1], there[1]), Y)
    first = added(a[0, 0], b[0, 0], there[0], there_y)
    a, b = keep[:, :, :, 1], got[:, :, :, 1]
    there = swap(added(a[:, 1], b[:, 1]), Y)
    there_x = swap(added(a[1, 0], b[1, 0], there[1]), X)
    second = added(a[0, 0], b[0, 0], there[0], there_x)
    return lax.psum_scatter(jnp.stack([first, second], 1), FAR, scatter_dimension=0, tiled=False)


def own_rows(core, summed):
    mine, send = choose(core, summed[0], summed[1])
    got = swap(send, CORE)
    left, right = choose(core, mine, got)
    return left, right


def shards(inputs, segments, cotangent, qkv_weight, query_bias, value_bias, out_weight, out_bias, first_gain, first_shift, up_weight, up_bias, down_weight, down_bias, second_gain, second_shift):
    tokens, width = inputs.shape[1:]
    hidden = up_weight.shape[1]
    pairs = width // PAIR
    blocks = lax.axis_size(CTX)
    place = lax.axis_index(CTX)
    core = lax.axis_index(CORE)
    at = jnp.stack([lax.axis_index(Y), lax.axis_index(X), core]).astype(jnp.int32)
    rows = qkv_weight.shape[0]
    far = lax.axis_size(FAR) if rows % 16 == 0 else None
    onward = [(i, i + 1) for i in range(blocks - 1)]
    back = [(i + 1, i) for i in range(blocks - 1)]

    def from_before(v):
        return lax.ppermute(v, CTX, onward)

    def from_after(v):
        return lax.ppermute(v, CTX, back)

    x = inputs[0]
    vector = cat([query_bias, value_bias, out_bias, first_gain, first_shift, down_bias, second_gain, second_shift, up_bias], 0)
    if far is None:
        at = jnp.zeros_like(at)
        whole = lambda v: [lax.all_gather(v, ALL, axis=0, tiled=True)]
        qkv_parts, out_parts, up_parts, down_parts = whole(qkv_weight), whole(out_weight), whole(up_weight), whole(down_weight)
        table = whole(vector[None])[0]
    else:
        pieces = [choose(core, *halves(w)) for w in (qkv_weight, out_weight, up_weight)]
        mine = cat([p[0] for p in pieces], 1)
        got = swap(cat([p[1] for p in pieces], 1), CORE)
        both = jnp.stack(choose(core, mine, got))
        cut = 3 * width // 2
        cut_out = cut + width // 2
        lines = vector.shape[0] // 128
        note = jnp.zeros((rows, 128), BF16).at[:lines].set(vector.reshape(lines, 128))
        note = jnp.stack([note, jnp.zeros_like(note)])
        first_parts = gather_first(cat([both[:, :, :cut], note], 2))
        qkv_parts = first_parts + [swap(p, CORE) for p in first_parts]
        up_own = gather_up(both[:, :, cut_out:].reshape(2 * rows, hidden // 2))
        up_parts = up_own + [swap(p, CORE) for p in up_own]
        out_block = cat([both[0, :, cut:cut_out], both[1, :, cut:cut_out]], 1)
        down_own = gather_down(cat([down_weight, out_block], 0))
        down_parts = down_own + [swap(p, CORE) for p in down_own]
        out_parts = down_parts
        notes = jnp.stack([jnp.stack([qkv_parts[4 * c + s][:, :, :lines, cut:] for s in range(2)]) for c in range(2)])
        notes = notes.reshape(2, 2, 2, far, -1)
        for axis, index in ((0, at[2]), (1, at[1]), (2, at[0])):
            notes = jnp.where(index == 0, notes, jnp.flip(notes, axis))
        table = notes.transpose(3, 2, 1, 0, 4).reshape(2 * blocks, -1)

    each = query_bias.shape[0]
    rows_of = [table[:, each * i : each * i + each].reshape(1, width).astype(F32) for i in range(8)]
    query_row, value_row, out_row, gain_one, shift_one, down_row, gain_two, shift_two = rows_of
    up_row = table[:, 8 * each :].reshape(1, hidden).astype(F32)

    x_before = from_before(x)
    x_after = from_after(x)
    bias_own, bias_halo = mask_biases(segments[0], place, blocks, tokens)
    qkv_row = cat([query_row, jnp.zeros_like(query_row), value_row], 1)
    mixed, before, after, qkv_full = project(far, at, qkv_parts, x, x_before, x_after, qkv_row)
    heads, log_cols = attend(mixed, before, after, bias_own, bias_halo)
    hat, inverse, first, low, out_full = out_project(far, at, out_parts, heads, x, cat([out_row, gain_one, shift_one], 0))
    active, slope, result, grad_two, glow, sums_two, up_full, down_full = forward(
        far, at, up_parts, down_parts, low, first, up_row, cat([down_row, gain_two, shift_two], 0), cotangent[0]
    )
    lift, down_keep, down_send, up_bias_part = down_grads(far, at, glow, down_full, slope, active)
    down_got = None if far is None else swap(down_send, CORE)
    up_keep, up_send, grad_one, branch, sums_one = up_grads(far, at, low, lift, up_full, grad_two, hat, inverse, gain_one)
    up_got = None if far is None else swap(up_send, CORE)
    grad_heads, means, out_keep, out_send = out_grads(far, at, branch, out_full, heads)
    out_got = None if far is None else swap(out_send, CORE)
    mean_cols = means.reshape(tokens, pairs, 2).transpose(1, 0, 2)
    row_pair = jnp.stack([log_cols.transpose(0, 2, 1), mean_cols.transpose(0, 2, 1)])
    grad_before = from_before(grad_heads)
    grad_after = from_after(grad_heads)
    rows_before = from_before(row_pair)
    rows_after = from_after(row_pair)
    dq, dk, dv = own_grads(mixed, before, after, grad_heads, log_cols, mean_cols, row_pair[0], row_pair[1], bias_own, bias_halo)
    dk, dv = halo_grads(mixed, before, after, grad_before, grad_after, rows_before, rows_after, bias_halo, dk, dv)
    qkv_keep, qkv_send, sums_qkv = qkv_grads(far, at, x, dq, dk, dv)
    inputs_grad = (grad_one + nt(cat([dq, dk, dv], 1), qkv_full)).astype(BF16)[None]

    small_parts = (sums_qkv[0], sums_qkv[1], sums_one[2], sums_one[0], sums_one[1], sums_two[2], sums_two[0], sums_two[1])
    small = cat([v.reshape(2 * blocks, each) for v in small_parts] + [up_bias_part.reshape(2 * blocks, -1)], 1)
    if far is None:
        total = lambda keep, send, axis: lax.psum_scatter(cat([keep, send], axis), ALL, scatter_dimension=0, tiled=True).astype(F32)
        down_sum = total(down_keep, down_send, 0)
        up_sum = total(up_keep, up_send, 1)
        out_sum = total(out_keep, out_send, 1)
        qkv_sum = total(qkv_keep, qkv_send, 1)
        small_sum = lax.psum_scatter(small, ALL, scatter_dimension=0, tiled=True)[0]
    else:
        by = lambda v: v.reshape(2, 2, far, -1, v.shape[-1])
        down_sum = scatter_down(by(down_keep), by(down_got))
        up_out = scatter_up(cat([by(up_keep), by(out_keep)], 4), cat([by(up_got), by(out_got)], 4))
        small = small.reshape(far, 2, 2, 2, lines, 128).transpose(3, 2, 1, 0, 4, 5)
        for axis, index in ((0, at[2]), (1, at[1]), (2, at[0])):
            small = jnp.where(index == 0, small, jnp.flip(small, axis))
        note = jnp.zeros((2, 2, 2, far, 2, rows, 128), BF16).at[:, :, :, :, 0, :lines].set(small.astype(BF16))
        note_got = swap(note[1], CORE)
        qkv_got = swap(qkv_send, CORE)
        colors = lambda v: v.reshape(2, 2, far, 2, rows, v.shape[-1])
        last = scatter_last(cat([colors(qkv_keep), note[0]], 5), cat([colors(qkv_got), note_got], 5))
        qkv_left, qkv_right = own_rows(core, last[:, :, :cut])
        qkv_sum = cat([qkv_left, qkv_right], 1).astype(F32)
        small_sum = last[0, :lines, cut:].reshape(-1).astype(F32)
        left, right = own_rows(core, up_out.reshape(2, rows, -1))
        cut_up = hidden // 2
        up_sum = cat([left[:, :cut_up], right[:, :cut_up]], 1).astype(F32)
        out_sum = cat([left[:, cut_up:], right[:, cut_up:]], 1).astype(F32)
    s = [small_sum[each * i : each * i + each] for i in range(8)]
    return (
        result[None], inputs_grad, qkv_sum, s[0], s[1], out_sum, s[2], s[3], s[4], up_sum, small_sum[8 * each :], down_sum, s[5], s[6], s[7],
    )


def solution(mesh):
    devices = mesh.devices
    split = jax.sharding.Mesh(devices.reshape(devices.shape[0] // 4, 2, 2, devices.shape[1]), ALL)
    rows, vec = P(ALL, None), P(ALL)
    tokens = P(CORE, CTX, None)
    return jax.shard_map(
        shards,
        mesh=split,
        in_specs=(tokens, P(CORE, None), tokens, rows, vec, vec, rows, vec, vec, vec, rows, vec, rows, vec, vec, vec),
        out_specs=(tokens, tokens, rows, vec, vec, rows, vec, vec, vec, rows, vec, rows, vec, vec, vec),
        check_vma=False,
    )
```

```python
import functools

import jax
import jax.numpy as jnp
from jax import lax
from jax.experimental import pallas as pl
from jax.experimental.pallas import tpu as pltpu
from jax.sharding import PartitionSpec as P

H = 16
HD = 64
WINDOW = 1024
HALF = WINDOW // 2
ROWS = 128
PAIR = 2 * HD
FILL = -1e30
EPS = 1e-05
HIDDEN_BLOCK = 128
F32 = jnp.float32
BF16 = jnp.bfloat16
VMEM_BYTES = 56 * 1024 * 1024
SMEM = pl.BlockSpec(memory_space=pltpu.SMEM)
ANY = pl.BlockSpec(memory_space=pl.ANY)
VMEM = pl.BlockSpec(memory_space=pltpu.VMEM)


def nn(a, b):
    return lax.dot_general(a, b, (((1,), (0,)), ((), ())), preferred_element_type=F32)


def nt(a, b):
    return lax.dot_general(a, b, (((1,), (1,)), ((), ())), preferred_element_type=F32)


def tn(a, b):
    return lax.dot_general(a, b, (((0,), (0,)), ((), ())), preferred_element_type=F32)


def cat(parts, axis):
    return jnp.concatenate(parts, axis=axis)


def cost():
    return pl.CostEstimate(flops=1, bytes_accessed=1, transcendentals=0)


def params():
    return pltpu.CompilerParams(vmem_limit_bytes=VMEM_BYTES)


def head_masks(scale):
    lane = lax.broadcasted_iota(jnp.int32, (1, PAIR), 1)
    first = jnp.where(lane < HD, scale, 0.0).astype(F32)
    second = jnp.where(lane < HD, 0.0, scale).astype(F32)
    return first.astype(BF16), second.astype(BF16)


def stacked(values, masks):
    return cat([values * masks[0], values * masks[1]], 0)


def strip(i, tokens):
    return slice(ROWS * i, ROWS * i + tokens + ROWS)


def put_rows(ref, cols, pair):
    head = lax.broadcasted_iota(jnp.int32, (H, 1), 0) - 2 * pl.program_id(0)
    ref[:, cols] = jnp.where(head == 0, pair[0], jnp.where(head == 1, pair[1], ref[:, cols]))


def far_first(p, pairs):
    return lax.rem(p + pairs // 2, pairs)


def take_row(values, h, pair=None):
    head = lax.broadcasted_iota(jnp.int32, (H, 1), 0) - 2 * (pl.program_id(0) if pair is None else pair)
    return jnp.sum(jnp.where(head == h, values, 0.0), axis=0, keepdims=True)


def attend_kernel(q_ref, ko_ref, kp_ref, kn_ref, vo_ref, vp_ref, vn_ref, bo_ref, bh_ref, out_ref, lse_ref, kh, vh):
    tokens = q_ref.shape[0]
    kh[:tokens] = kp_ref[...]
    kh[tokens:] = kn_ref[...]
    ones = head_masks(1.0)
    vh[:tokens] = vp_ref[...]
    vh[tokens:] = vn_ref[...]
    vo = stacked(vo_ref[...], ones)
    scaled = head_masks(HD ** -0.5)
    lane = lax.broadcasted_iota(jnp.int32, (ROWS, PAIR), 1)
    for i in range(tokens // ROWS):
        rows = slice(ROWS * i, ROWS * i + ROWS)
        window = strip(i, tokens)
        q = q_ref[rows]
        own_parts, halo_parts, totals, logs = [], [], [], []
        for mask in scaled:
            qm = q * mask
            so = nt(qm, ko_ref[...]) + bo_ref[rows]
            sh = nt(qm, kh[window]) + bh_ref[i]
            peak = jnp.maximum(jnp.max(so, axis=1, keepdims=True), jnp.max(sh, axis=1, keepdims=True))
            po = jnp.exp(so - peak)
            ph = jnp.exp(sh - peak)
            total = jnp.sum(po, axis=1, keepdims=True) + jnp.sum(ph, axis=1, keepdims=True)
            own_parts.append(po.astype(BF16))
            halo_parts.append(ph.astype(BF16))
            totals.append(1.0 / total)
            logs.append((peak + jnp.log(total)).T)
        out = nn(cat(own_parts, 1), vo) + nn(cat(halo_parts, 1), stacked(vh[window], ones))
        out = out * jnp.where(lane < HD, totals[0], totals[1])
        out_ref[rows] = out.astype(BF16)
        put_rows(lse_ref, rows, logs)


def attend(mixed, before, after, bias_own, bias_halo):
    tokens, width = mixed.shape[0], mixed.shape[1] // 3
    pairs = width // PAIR

    near = pairs // 2

    def column(part):
        return pl.BlockSpec((tokens, PAIR), lambda p: (0, (p // near * 3 + part) * near + p % near))

    whole = lambda shape: pl.BlockSpec(shape, lambda p: (0,) * len(shape))
    return pl.pallas_call(
        attend_kernel,
        grid=(pairs,),
        in_specs=[column(0), column(1), column(1), column(1), column(2), column(2), column(2), whole(bias_own.shape), whole(bias_halo.shape)],
        out_specs=[pl.BlockSpec((tokens, PAIR), lambda p: (0, p)), whole((H, tokens))],
        out_shape=[jax.ShapeDtypeStruct((tokens, width), BF16), jax.ShapeDtypeStruct((H, tokens), F32)],
        scratch_shapes=[pltpu.VMEM((2 * tokens, PAIR), BF16), pltpu.VMEM((2 * tokens, PAIR), BF16)],
        compiler_params=params(),
        cost_estimate=cost(),
        name="attend",
    )(mixed, mixed, before, after, mixed, before, after, bias_own, bias_halo)


def own_grad_kernel(q_ref, ko_ref, kp_ref, kn_ref, vo_ref, vp_ref, vn_ref, do_ref, log_ref, mean_ref, bo_ref, bh_ref, dq_ref, dkv_ref, sum_ref, kh, vh):
    tokens = q_ref.shape[0]
    kh[:tokens] = kp_ref[...]
    kh[tokens:] = kn_ref[...]
    vh[:tokens] = vp_ref[...]
    vh[tokens:] = vn_ref[...]
    ones = head_masks(1.0)
    scaled = head_masks(HD ** -0.5)
    k_own = ko_ref[...]
    v_own = vo_ref[...]
    k_pair = stacked(k_own, scaled)
    log_rows = [take_row(log_ref[...], h) for h in range(2)]
    mean_rows = [take_row(mean_ref[...], h) for h in range(2)]
    chunk = 2 * ROWS
    for c in range(tokens // chunk):
        cols = slice(chunk * c, chunk * c + chunk)
        q = q_ref[cols]
        do = do_ref[cols]
        probs, grads, qs, dos = [], [], [], []
        for h in range(2):
            qm = q * scaled[h]
            dm = do * ones[h]
            st = nt(k_own, qm) + bo_ref[:, cols]
            pt = jnp.exp(st - log_rows[h][:, cols])
            gt = pt * (nt(v_own, dm) - mean_rows[h][:, cols])
            probs.append(pt.astype(BF16))
            grads.append(gt.astype(BF16))
            qs.append(qm)
            dos.append(dm)
        dv = nn(cat(probs, 1), cat(dos, 0))
        dk = nn(cat(grads, 1), cat(qs, 0))
        if c == 0:
            dkv_ref[0, 0] = dk
            dkv_ref[0, 1] = dv
        else:
            dkv_ref[0, 0] += dk
            dkv_ref[0, 1] += dv
        dq_own = tn(cat(grads, 0), k_pair)
        for r in range(chunk // ROWS):
            i = c * (chunk // ROWS) + r
            rows = slice(ROWS * i, ROWS * i + ROWS)
            window = strip(i, tokens)
            halo = []
            for h in range(2):
                qm = q[ROWS * r : ROWS * r + ROWS] * scaled[h]
                dm = do[ROWS * r : ROWS * r + ROWS] * ones[h]
                s = nt(qm, kh[window]) + bh_ref[i]
                p = jnp.exp(s - log_rows[h][:, rows].T)
                halo.append((p * (nt(dm, vh[window]) - mean_rows[h][:, rows].T)).astype(BF16))
            dq = dq_own[ROWS * r : ROWS * r + ROWS] + nn(cat(halo, 1), stacked(kh[window], scaled))
            dq = dq.astype(BF16)
            dq_ref[0, rows] = dq
            sum_ref[...] = column_sum(dq.astype(F32)) + (sum_ref[...] if i else 0.0)


def own_grads(mixed, before, after, payload, logs, means, bias_own, bias_halo):
    tokens, width = mixed.shape[0], payload.shape[1]
    pairs = width // PAIR

    near = pairs // 2

    def column(part):
        return pl.BlockSpec((tokens, PAIR), lambda p: (0, (p // near * 3 + part) * near + p % near))

    whole = lambda shape: pl.BlockSpec(shape, lambda p: (0,) * len(shape))
    block = pl.BlockSpec((tokens, PAIR), lambda p: (0, p))
    return pl.pallas_call(
        own_grad_kernel,
        grid=(pairs,),
        in_specs=[column(0), column(1), column(1), column(1), column(2), column(2), column(2), block, whole(logs.shape), whole(means.shape), whole(bias_own.shape), whole(bias_halo.shape)],
        out_specs=[
            pl.BlockSpec((1, tokens, PAIR), lambda p: (p // near, 0, p % near)),
            pl.BlockSpec((1, 2, tokens, PAIR), lambda p: (p // near, 0, 0, p % near)),
            pl.BlockSpec((1, PAIR), lambda p: (0, p)),
        ],
        out_shape=[
            jax.ShapeDtypeStruct((2, tokens, width // 2), BF16),
            jax.ShapeDtypeStruct((2, 2, tokens, width // 2), F32),
            jax.ShapeDtypeStruct((1, width), F32),
        ],
        scratch_shapes=[pltpu.VMEM((2 * tokens, PAIR), BF16), pltpu.VMEM((2 * tokens, PAIR), BF16)],
        compiler_params=params(),
        cost_estimate=cost(),
        name="own_grads",
    )(mixed, mixed, before, after, mixed, before, after, payload, logs, means, bias_own, bias_halo)


def halo_grad_kernel(ko_ref, vo_ref, qp_ref, qn_ref, dp_ref, dn_ref, lp0, lp1, lp2, ln0, ln1, ln2, bh_ref, dq_in, dkv_in, keep_ref, send_ref, sum_ref, qh, dh, lh, made):
    tokens = ko_ref.shape[0]
    qh[:tokens] = qp_ref[...]
    qh[tokens:] = qn_ref[...]
    dh[:tokens] = dp_ref[...]
    dh[tokens:] = dn_ref[...]
    for first, refs in ((0, (lp0, lp1, lp2)), (tokens, (ln0, ln1, ln2))):
        table = refs[0][...].astype(F32) + refs[1][...].astype(F32) + refs[2][...].astype(F32)
        for h in range(2):
            row = take_row(table, h, far_first(pl.program_id(0), pl.num_programs(0)))
            lh[0, h : h + 1, first : first + tokens] = row[:, :tokens]
            lh[1, h : h + 1, first : first + tokens] = row[:, tokens:]
    ones = head_masks(1.0)
    scaled = head_masks(HD ** -0.5)
    for j in range(tokens // ROWS):
        rows = slice(ROWS * j, ROWS * j + ROWS)
        window = strip(j, tokens)
        q = qh[window]
        do = dh[window]
        k = ko_ref[rows]
        v = vo_ref[rows]
        probs, grads, qs, dos = [], [], [], []
        for h in range(2):
            qm = q * scaled[h]
            dm = do * ones[h]
            st = nt(k, qm) + bh_ref[j]
            pt = jnp.exp(st - lh[0, h : h + 1, window])
            gt = pt * (nt(v, dm) - lh[1, h : h + 1, window])
            probs.append(pt.astype(BF16))
            grads.append(gt.astype(BF16))
            qs.append(qm)
            dos.append(dm)
        made[1, rows] = (dkv_in[0, 0, rows] + nn(cat(grads, 1), cat(qs, 0))).astype(BF16)
        dv = (dkv_in[0, 1, rows] + nn(cat(probs, 1), cat(dos, 0))).astype(BF16)
        made[2, rows] = dv
        sum_ref[...] = column_sum(dv.astype(F32)) + (sum_ref[...] if j else 0.0)
    made[0] = dq_in[0]
    put_half(pl.program_id(0), pl.num_programs(0), send_ref, keep_ref, made[...])


def halo_grads(mixed, before, after, grad_before, grad_after, bias_halo, dq, dkv):
    tokens, width = dkv.shape[2], 2 * dkv.shape[3]
    pairs = width // PAIR
    near = pairs // 2

    def column(part):
        return pl.BlockSpec((tokens, PAIR), lambda p: (0, (far_first(p, pairs) // near * 3 + part) * near + p % near))

    whole = lambda shape: pl.BlockSpec(shape, lambda p: (0,) * len(shape))
    both = pl.BlockSpec((1, 2, tokens, PAIR), lambda p: (far_first(p, pairs) // near, 0, 0, p % near))
    one = pl.BlockSpec((1, tokens, PAIR), lambda p: (far_first(p, pairs) // near, 0, p % near))
    tables = [pl.BlockSpec((H, width), lambda p, k=k: (tokens // H + k, 0)) for k in range(3)]
    block = pl.BlockSpec((tokens, PAIR), lambda p: (0, far_first(p, pairs)))
    half = jax.ShapeDtypeStruct((3, tokens, width // 2), BF16)
    return pl.pallas_call(
        halo_grad_kernel,
        grid=(pairs,),
        in_specs=[column(1), column(2), column(0), column(0), block, block] + tables + tables + [whole(bias_halo.shape), one, both],
        out_specs=[
            pl.BlockSpec((3, tokens, PAIR), lambda p: (0, 0, jnp.maximum(p - near, 0))),
            pl.BlockSpec((3, tokens, PAIR), lambda p: (0, 0, jnp.minimum(p, near - 1))),
            pl.BlockSpec((1, PAIR), lambda p: (0, far_first(p, pairs))),
        ],
        out_shape=[half, half, jax.ShapeDtypeStruct((1, width), F32)],
        scratch_shapes=[
            pltpu.VMEM((2 * tokens, PAIR), BF16),
            pltpu.VMEM((2 * tokens, PAIR), BF16),
            pltpu.VMEM((2, 2, 2 * tokens), F32),
            pltpu.VMEM((3, tokens, PAIR), BF16),
        ],
        compiler_params=params(),
        cost_estimate=cost(),
        name="halo_grads",
    )(mixed, mixed, before, after, grad_before, grad_after, *[grad_before] * 3, *[grad_after] * 3, bias_halo, dq, dkv)


def mask_biases(segments, place, blocks, tokens):
    line = cat([jnp.full((tokens,), -1, jnp.int32), segments, jnp.full((tokens,), -1, jnp.int32)], 0)
    near = lax.dynamic_slice_in_dim(line, place * tokens, 3 * tokens)
    own = near[tokens : 2 * tokens]
    bias_own = jnp.where(own[:, None] == own[None, :], 0.0, FILL).astype(F32)
    halo = cat([near[:tokens], near[2 * tokens :]], 0)
    at = jnp.arange(tokens, dtype=jnp.int32)
    halo_at = cat([at - tokens, at + tokens], 0)
    allowed = (own[:, None] == halo[None, :]) & (jnp.abs(halo_at[None, :] - at[:, None]) < HALF)
    bias = jnp.where(allowed, 0.0, FILL).astype(F32)
    bias_halo = jnp.stack([bias[ROWS * i : ROWS * i + ROWS, strip(i, tokens)] for i in range(tokens // ROWS)])
    return bias_own, bias_halo


def normalized(values):
    average = jnp.mean(values, axis=1, keepdims=True)
    centered = values - average
    spread = jnp.mean(centered * centered, axis=1, keepdims=True)
    inverse = lax.rsqrt(spread + EPS)
    return centered * inverse, inverse


def norm_back(grad, gain, hat, inverse):
    scaled = grad * gain
    return inverse * (
        scaled
        - jnp.mean(scaled, axis=1, keepdims=True)
        - hat * jnp.mean(scaled * hat, axis=1, keepdims=True)
    )


def column_sum(values):
    return jnp.sum(values, axis=0, keepdims=True)


def part_blocks(at_ref, order, second, far):
    for first in range(2):
        rel = {order[-2]: first, order[-1]: second}
        y = jnp.bitwise_xor(at_ref[0], rel["y"])
        x = jnp.bitwise_xor(at_ref[1], rel["x"])
        for i in range(far):
            z = jnp.bitwise_xor(at_ref[3], (i % 2) * 2 + i // 2) if order[0] == "z" else i
            yield first, i, (z * 2 + y) * 2 + x


def start_all(copies):
    for copy in copies:
        copy.start()


def wait_all(copies):
    for copy in copies:
        copy.wait()


def block_place(at_ref, order, z, y, x, far):
    where = {"z": (z, far), "y": (jnp.bitwise_xor(at_ref[0], y), 2), "x": (jnp.bitwise_xor(at_ref[1], x), 2)}
    to = 0
    for axis in order:
        to = to * where[axis][1] + where[axis][0]
    return to


def prepare_kernel(at_ref, qkv_ref, out_ref, up_ref, *refs):
    vectors, mine_ref, send_ref, note_ref = refs[:-3], *refs[-3:]
    width = out_ref.shape[1]
    place = 0
    for ref, piece in ((qkv_ref, width // 2), (out_ref, width // 2), (up_ref, HIDDEN_BLOCK)):
        for i in range(0, ref.shape[1], 2 * piece):
            mine_ref[:, place : place + piece] = ref[:, pl.ds(pl.multiple_of(i + at_ref[2] * piece, piece), piece)]
            send_ref[:, place : place + piece] = ref[:, pl.ds(pl.multiple_of(i + (1 - at_ref[2]) * piece, piece), piece)]
            place += piece
    line = cat([v[...].astype(F32) for v in vectors], 1).astype(BF16)
    note_ref[...] = jnp.zeros_like(note_ref)
    for i in range(line.shape[1] // 128):
        note_ref[i : i + 1] = line[:, i * 128 : i * 128 + 128]


def prepare(at, qkv, out, up, vectors):
    rows = qkv.shape[0]
    columns = (qkv.shape[1] + out.shape[1] + up.shape[1]) // 2
    half = jax.ShapeDtypeStruct((rows, columns), BF16)
    return pl.pallas_call(
        prepare_kernel,
        in_specs=[SMEM] + [VMEM] * (3 + len(vectors)),
        out_shape=[half, half, jax.ShapeDtypeStruct((rows, 128), BF16)],
        compiler_params=params(),
        cost_estimate=cost(),
        name="prepare",
    )(at, qkv, out, up, *[v[None] for v in vectors])


def arrange_kernel(at_ref, mine_ref, got_ref, note_ref, block_ref, up_ref):
    rows, cut = mine_ref.shape[0], block_ref.shape[2] - 128
    block_ref[0, :, cut:] = note_ref[...]
    block_ref[1, :, cut:] = jnp.zeros_like(note_ref)

    def lay(first, second):
        for i, ref in ((0, first), (1, second)):
            block_ref[i, :, :cut] = ref[:, :cut]
            up_ref[i * rows : i * rows + rows] = ref[:, cut:]

    @pl.when(at_ref[2] == 0)
    def _():
        lay(mine_ref, got_ref)

    @pl.when(at_ref[2] != 0)
    def _():
        lay(got_ref, mine_ref)


def arrange(at, mine, got, note, hidden):
    rows, columns = mine.shape
    return pl.pallas_call(
        arrange_kernel,
        in_specs=[SMEM] + [VMEM] * 3,
        out_shape=[
            jax.ShapeDtypeStruct((2, rows, columns - hidden // 2 + 128), BF16),
            jax.ShapeDtypeStruct((2 * rows, hidden // 2), BF16),
        ],
        compiler_params=params(),
        cost_estimate=cost(),
        name="arrange",
    )(at, mine, got, note)


def first_copies(refs, qkv, out, sems, at_ref, far):
    width, columns = qkv.shape
    half, near = width // 2, columns // 2
    copies = []

    def add(source, target):
        copies.append(pltpu.make_async_copy(source, target, sems.at[len(copies)]))

    def column(core):
        return pl.ds(pl.multiple_of(jnp.bitwise_xor(at_ref[2], core) * half, half), half)

    for core in range(2):
        if far is None:
            add(refs[core], qkv.at[:, pl.ds(core * near, near)])
            for part in range(2):
                row = pl.ds(pl.multiple_of(jnp.bitwise_xor(at_ref[2], part) * half, half), half)
                add(refs[2 + core].at[pl.ds(part * half, half)], out.at[row, column(core)])
            continue
        rows = width // (8 * far)
        for color, order in enumerate(("zyx", "zxy")):
            for second in range(2):
                ref = refs[core * 4 + color * 2 + second]
                for first, z, block in part_blocks(at_ref, order, second, far):
                    row = (block * 2 + color) * rows
                    add(ref.at[first, z, :, pl.ds(0, near)], qkv.at[pl.ds(pl.multiple_of(row, rows), rows), pl.ds(core * near, near)])
                    row = jnp.bitwise_xor(row, at_ref[2] * half)
                    add(ref.at[first, z, :, pl.ds(near, half)], out.at[pl.ds(pl.multiple_of(row, rows), rows), column(core)])
    return copies


def project_kernel(far, parts, *refs):
    at_ref, refs = refs[0], refs[1:]
    part_refs, refs = refs[:parts], refs[parts:]
    own_ref, before_ref, row_ref, own_out, before_out, qkv_out, out_out, qkv, out, sems, out_sems = refs
    copies = first_copies(part_refs, qkv, out, sems, at_ref, far)
    start_all(copies)
    wait_all(copies)
    keep = [pltpu.make_async_copy(qkv, qkv_out, out_sems.at[0]), pltpu.make_async_copy(out, out_out, out_sems.at[1])]
    start_all(keep)
    chunk = 512
    for source, target in ((own_ref, own_out), (before_ref, before_out)):

        def body(j, carry, source=source, target=target):
            cols = pl.ds(pl.multiple_of(j * chunk, chunk), chunk)
            target[:, cols] = (nn(source[...], qkv[:, cols]) + row_ref[:, cols]).astype(BF16)
            return carry

        lax.fori_loop(0, qkv.shape[1] // chunk, body, 0)
    wait_all(keep)


def copy_count(far, each):
    return 2 if far is None else 8 * far * each


def project(far, at, parts, x, before, row):
    tokens, width = x.shape
    columns = row.shape[1]
    mixed = jax.ShapeDtypeStruct((tokens, columns), BF16)
    return pl.pallas_call(
        functools.partial(project_kernel, far, len(parts)),
        in_specs=[SMEM] + [ANY] * len(parts) + [VMEM] * 3,
        out_specs=[VMEM, VMEM, ANY, ANY],
        out_shape=[mixed, mixed, jax.ShapeDtypeStruct((width, columns), BF16), jax.ShapeDtypeStruct((width, width), BF16)],
        scratch_shapes=[
            pltpu.VMEM((width, columns), BF16),
            pltpu.VMEM((width, width), BF16),
            pltpu.SemaphoreType.DMA((6 if far is None else 64 * far,)),
            pltpu.SemaphoreType.DMA((2,)),
        ],
        compiler_params=params(),
        cost_estimate=cost(),
        name="project",
    )(at, *parts, x, before, row)


def project_more_kernel(x_ref, w_ref, row_ref, out_ref):
    out_ref[...] = (nn(x_ref[...], w_ref[...]) + row_ref[...]).astype(BF16)


def project_more(x, full, row, chunk=512):
    tokens, width = x.shape
    columns = full.shape[1]
    return pl.pallas_call(
        project_more_kernel,
        grid=(columns // chunk,),
        in_specs=[
            pl.BlockSpec((tokens, width), lambda i: (0, 0)),
            pl.BlockSpec((width, chunk), lambda i: (0, i)),
            pl.BlockSpec((1, chunk), lambda i: (0, i)),
        ],
        out_specs=pl.BlockSpec((tokens, chunk), lambda i: (0, i)),
        out_shape=jax.ShapeDtypeStruct((tokens, columns), BF16),
        compiler_params=params(),
        cost_estimate=cost(),
        name="project_more",
    )(x, full, row)


def out_kernel(heads_ref, w_ref, x_ref, vec_ref, hat_ref, inv_ref, first_ref, low_ref):
    branch = nn(heads_ref[...], w_ref[...]) + vec_ref[0:1]
    hat, inverse = normalized(x_ref[...].astype(F32) + branch)
    first = hat * vec_ref[1:2] + vec_ref[2:3]
    hat_ref[...] = hat
    inv_ref[...] = inverse
    first_ref[...] = first
    low_ref[...] = first.astype(BF16)


def out_project(heads, out_full, x, vectors):
    tokens, width = heads.shape
    rows = tokens // 2
    block = pl.BlockSpec((rows, width), lambda i: (i, 0))
    return pl.pallas_call(
        out_kernel,
        grid=(2,),
        in_specs=[block, pl.BlockSpec(out_full.shape, lambda i: (0, 0)), block, pl.BlockSpec(vectors.shape, lambda i: (0, 0))],
        out_specs=[block, pl.BlockSpec((rows, 1), lambda i: (i, 0)), block, block],
        out_shape=[
            jax.ShapeDtypeStruct((tokens, width), F32),
            jax.ShapeDtypeStruct((tokens, 1), F32),
            jax.ShapeDtypeStruct((tokens, width), F32),
            jax.ShapeDtypeStruct((tokens, width), BF16),
        ],
        compiler_params=params(),
        cost_estimate=cost(),
        name="out_project",
    )(heads, out_full, x, vectors)


def up_copies(refs, full, sems, at_ref, far):
    width, half = full.shape[0], full.shape[1] // 2
    copies = []
    for core in range(2):
        cols = pl.ds(core * half, half)
        if far is None:
            copies.append(pltpu.make_async_copy(refs[core], full.at[:, cols], sems.at[core]))
            continue
        rows = width // (4 * far)
        for second in range(2):
            ref = refs[core * 2 + second]
            for first, z, block in part_blocks(at_ref, "zyx", second, far):
                to = full.at[pl.ds(pl.multiple_of(block * rows, rows), rows), cols]
                copies.append(pltpu.make_async_copy(ref.at[first, z], to, sems.at[len(copies)]))
    return copies


def down_copies(refs, full, sems, at_ref, far):
    half = full.shape[0] // 2
    copies = []
    for core in range(2):
        if far is None:
            copies.append(pltpu.make_async_copy(refs[core], full.at[pl.ds(core * half, half)], sems.at[core]))
            continue
        rows = half // (4 * far)
        for second in range(2):
            ref = refs[core * 2 + second]
            for first, z, block in part_blocks(at_ref, "xy", second, far):
                to = full.at[pl.ds(pl.multiple_of(core * half + block * rows, rows), rows)]
                copies.append(pltpu.make_async_copy(ref.at[first, z], to, sems.at[len(copies)]))
    return copies


def put_half(step, steps, keep_ref, send_ref, value):
    @pl.when(step < steps // 2)
    def _():
        keep_ref[...] = value

    @pl.when(step >= steps // 2)
    def _():
        send_ref[...] = value


def take_half(step, steps, keep_ref, send_ref):
    return jnp.where(step < steps // 2, keep_ref[...], send_ref[...])


def half_blocks(rows, chunk, steps):
    last = steps // 2 - 1
    return [
        pl.BlockSpec((rows, chunk), lambda i: (0, jnp.minimum(i, last))),
        pl.BlockSpec((rows, chunk), lambda i: (0, jnp.maximum(i - last - 1, 0))),
    ]


def lift_kernel(far, parts, *refs):
    at_ref, refs = refs[0], refs[1:]
    part_refs, refs = refs[:parts], refs[parts:]
    low_ref, row_ref, act_ref, act_send, slope_ref, full_out, full, sems, out_sem = refs
    step = pl.program_id(0)
    chunk = act_ref.shape[1]
    copies = up_copies(part_refs, full, sems, at_ref, far)
    keep = pltpu.make_async_copy(full, full_out, out_sem)

    @pl.when(step == 0)
    def _():
        start_all(copies)
        wait_all(copies)
        keep.start()

    lifted = nn(low_ref[...], full[:, pl.ds(pl.multiple_of(step * chunk, chunk), chunk)]) + row_ref[...]
    phi = 0.5 * (1.0 + lax.erf(lifted * (0.5 ** 0.5)))
    density = jnp.exp(lifted * lifted * -0.5) * 0.3989422804014327
    put_half(step, pl.num_programs(0), act_ref, act_send, (lifted * phi).astype(BF16))
    slope_ref[...] = phi + lifted * density

    @pl.when(step == pl.num_programs(0) - 1)
    def _():
        keep.wait()


def lift(far, at, parts, low, row, chunk=512):
    tokens, width = low.shape
    hidden = row.shape[1]
    block = pl.BlockSpec((tokens, chunk), lambda i: (0, i))
    return pl.pallas_call(
        functools.partial(lift_kernel, far, len(parts)),
        grid=(hidden // chunk,),
        in_specs=[SMEM] + [ANY] * len(parts) + [pl.BlockSpec((tokens, width), lambda i: (0, 0)), pl.BlockSpec((1, chunk), lambda i: (0, i))],
        out_specs=half_blocks(tokens, chunk, hidden // chunk) + [block, ANY],
        out_shape=[
            jax.ShapeDtypeStruct((tokens, hidden // 2), BF16),
            jax.ShapeDtypeStruct((tokens, hidden // 2), BF16),
            jax.ShapeDtypeStruct((tokens, hidden), F32),
            jax.ShapeDtypeStruct((width, hidden), BF16),
        ],
        scratch_shapes=[pltpu.VMEM((width, hidden), BF16), pltpu.SemaphoreType.DMA((copy_count(far, 2),)), pltpu.SemaphoreType.DMA],
        compiler_params=params(),
        cost_estimate=cost(),
        name="lift",
    )(at, *parts, low, row)


def settle_kernel(far, parts, *refs):
    at_ref, refs = refs[0], refs[1:]
    part_refs, refs = refs[:parts], refs[parts:]
    act_ref, act_send, first_ref, vec_ref, dy_ref, result_ref, grad_ref, glow_ref, sums_ref, full_out, total, full, sems, out_sem = refs
    step = pl.program_id(0)
    chunk = act_ref.shape[1]
    copies = down_copies(part_refs, full, sems, at_ref, far)
    keep = pltpu.make_async_copy(full, full_out, out_sem)

    @pl.when(step == 0)
    def _():
        start_all(copies)
        wait_all(copies)
        keep.start()

    active = take_half(step, pl.num_programs(0), act_ref, act_send)
    part = nn(active, full[pl.ds(pl.multiple_of(step * chunk, chunk), chunk)])

    @pl.when(step == 0)
    def _():
        total[...] = part

    @pl.when(step > 0)
    def _():
        total[...] += part

    @pl.when(step == pl.num_programs(0) - 1)
    def _():
        rows = total.shape[0] // 4
        sums = None
        for i in range(4):
            at = slice(rows * i, rows * i + rows)
            hat, inverse = normalized(first_ref[at] + (total[at] + vec_ref[0:1]))
            result_ref[at] = (hat * vec_ref[1:2] + vec_ref[2:3]).astype(BF16)
            dy = dy_ref[at].astype(F32)
            grad = norm_back(dy, vec_ref[1:2], hat, inverse)
            low = grad.astype(BF16)
            grad_ref[at] = grad
            glow_ref[at] = low
            part = cat([column_sum(dy * hat), column_sum(dy), column_sum(low.astype(F32))], 0)
            sums = part if sums is None else sums + part
        sums_ref[...] = sums
        keep.wait()


def settle(far, at, parts, active, act_send, first, vectors, dy, chunk=1024):
    tokens, hidden = active.shape[0], 2 * active.shape[1]
    width = first.shape[1]
    whole = lambda shape: pl.BlockSpec(shape, lambda i: (0, 0))
    return pl.pallas_call(
        functools.partial(settle_kernel, far, len(parts)),
        grid=(hidden // chunk,),
        in_specs=[SMEM]
        + [ANY] * len(parts)
        + half_blocks(tokens, chunk, hidden // chunk)
        + [whole((tokens, width)), whole(vectors.shape), whole((tokens, width))],
        out_specs=[whole((tokens, width)), whole((tokens, width)), whole((tokens, width)), whole((3, width)), ANY],
        out_shape=[
            jax.ShapeDtypeStruct((tokens, width), BF16),
            jax.ShapeDtypeStruct((tokens, width), F32),
            jax.ShapeDtypeStruct((tokens, width), BF16),
            jax.ShapeDtypeStruct((3, width), F32),
            jax.ShapeDtypeStruct((hidden, width), BF16),
        ],
        scratch_shapes=[
            pltpu.VMEM((tokens, width), F32),
            pltpu.VMEM((hidden, width), BF16),
            pltpu.SemaphoreType.DMA((copy_count(far, 2),)),
            pltpu.SemaphoreType.DMA,
        ],
        compiler_params=params(),
        cost_estimate=cost(),
        name="settle",
    )(at, *parts, active, act_send, first, vectors, dy)


def lift_grad_kernel(glow_ref, down_ref, slope_ref, keep_ref, send_ref, sum_ref):
    value = (nt(glow_ref[...], down_ref[...]) * slope_ref[...]).astype(BF16)
    put_half(pl.program_id(0), pl.num_programs(0), keep_ref, send_ref, value)
    sum_ref[...] = column_sum(value.astype(F32))


def lift_grads(glow, down_full, slope, chunk=512):
    tokens, width = glow.shape
    hidden = down_full.shape[0]
    half = jax.ShapeDtypeStruct((tokens, hidden // 2), BF16)
    return pl.pallas_call(
        lift_grad_kernel,
        grid=(hidden // chunk,),
        in_specs=[
            pl.BlockSpec((tokens, width), lambda i: (0, 0)),
            pl.BlockSpec((chunk, width), lambda i: (i, 0)),
            pl.BlockSpec((tokens, chunk), lambda i: (0, i)),
        ],
        out_specs=half_blocks(tokens, chunk, hidden // chunk) + [pl.BlockSpec((1, chunk), lambda i: (0, i))],
        out_shape=[half, half, jax.ShapeDtypeStruct((1, hidden), F32)],
        compiler_params=params(),
        cost_estimate=cost(),
        name="lift_grads",
    )(glow, down_full, slope)


def down_grad_kernel(far, at_ref, act_ref, act_got, glow_ref, glow_got, dw_ref, glows):
    tokens = glow_ref.shape[0]

    @pl.when(pl.program_id(0) == 0)
    def _():
        glows[:tokens] = glow_ref[...]
        glows[tokens:] = glow_got[...]

    dw = tn(cat([act_ref[...], act_got[...]], 0), glows[...]).astype(BF16)
    if far is None:
        dw_ref[...] = dw
        return
    rows = dw.shape[0] // 4
    for j in range(4):
        to = block_place(at_ref, "yx", 0, j // 2, j % 2, far)
        dw_ref[pl.ds(pl.multiple_of(to * rows, rows), rows)] = dw[j * rows : j * rows + rows]


def down_grads(far, at, active, act_got, glow, glow_got):
    tokens, half = active.shape
    width = glow.shape[1]
    chunk = half // 4
    whole = pl.BlockSpec((tokens, width), lambda i: (0, 0))
    block = pl.BlockSpec((tokens, chunk), lambda i: (0, i))
    return pl.pallas_call(
        functools.partial(down_grad_kernel, far),
        grid=(4,),
        in_specs=[SMEM, block, block, whole, whole],
        out_specs=pl.BlockSpec((chunk, width), lambda i: (i, 0)),
        out_shape=jax.ShapeDtypeStruct((half, width), BF16),
        scratch_shapes=[pltpu.VMEM((2 * tokens, width), BF16)],
        compiler_params=params(),
        cost_estimate=cost(),
        name="down_grads",
    )(at, active, act_got, glow, glow_got)


def first_grad_kernel(at_ref, lift_ref, lift_send, up_ref, grad_ref, hat_ref, inv_ref, gain_ref, one_ref, branch_ref, mine_ref, send_ref, sums_ref, total):
    step = pl.program_id(0)
    part = nt(take_half(step, pl.num_programs(0), lift_ref, lift_send), up_ref[...])

    @pl.when(step == 0)
    def _():
        total[...] = grad_ref[...] + part

    @pl.when(step > 0)
    def _():
        total[...] += part

    @pl.when(step == pl.num_programs(0) - 1)
    def _():
        rows = total.shape[0] // 4
        sums = None
        for i in range(4):
            at = slice(rows * i, rows * i + rows)
            grad = total[at]
            hat = hat_ref[at]
            one = norm_back(grad, gain_ref[...], hat, inv_ref[at])
            branch = one.astype(BF16)
            one_ref[at] = one
            branch_ref[at] = branch
            part = cat([column_sum(grad * hat), column_sum(grad), column_sum(branch.astype(F32))], 0)
            sums = part if sums is None else sums + part
        sums_ref[...] = sums
        half = mine_ref.shape[1]
        mine_ref[...] = branch_ref[:, pl.ds(pl.multiple_of(at_ref[2] * half, half), half)]
        send_ref[...] = branch_ref[:, pl.ds(pl.multiple_of((1 - at_ref[2]) * half, half), half)]


def first_grads(at, lift, lift_send, up_full, grad_two, hat, inverse, gain, chunk=1024):
    tokens, width = hat.shape
    hidden = up_full.shape[1]
    whole = lambda shape: pl.BlockSpec(shape, lambda i: (0, 0))
    half = whole((tokens, width // 2))
    return pl.pallas_call(
        first_grad_kernel,
        grid=(hidden // chunk,),
        in_specs=[SMEM]
        + half_blocks(tokens, chunk, hidden // chunk)
        + [
            pl.BlockSpec((width, chunk), lambda i: (0, i)),
            whole((tokens, width)),
            whole((tokens, width)),
            whole((tokens, 1)),
            whole((1, width)),
        ],
        out_specs=[whole((tokens, width)), whole((tokens, width)), half, half, whole((3, width))],
        out_shape=[
            jax.ShapeDtypeStruct((tokens, width), F32),
            jax.ShapeDtypeStruct((tokens, width), BF16),
            jax.ShapeDtypeStruct((tokens, width // 2), BF16),
            jax.ShapeDtypeStruct((tokens, width // 2), BF16),
            jax.ShapeDtypeStruct((3, width), F32),
        ],
        scratch_shapes=[pltpu.VMEM((tokens, width), F32)],
        compiler_params=params(),
        cost_estimate=cost(),
        name="first_grads",
    )(at, lift, lift_send, up_full, grad_two, hat, inverse, gain)


def pay_kernel(branch_ref, w_ref, heads_ref, log_ref, pay_ref, mean_ref):
    tokens, width = branch_ref.shape
    grad = nt(branch_ref[...], w_ref[...]).astype(BF16)
    pay_ref[:tokens] = grad
    product = grad.astype(F32) * heads_ref[...].astype(F32)
    head = lax.broadcasted_iota(jnp.int32, (H, width), 1) // HD
    pick = jnp.where(head == lax.broadcasted_iota(jnp.int32, (H, width), 0), 1.0, 0.0).astype(F32)
    means = lax.dot_general(pick, product, (((1,), (1,)), ((), ())), precision=lax.Precision.HIGHEST, preferred_element_type=F32)
    mean_ref[...] = means
    rest = cat([log_ref[...], means], 1)
    for k in range(3):
        term = rest.astype(BF16)
        rest = rest - term.astype(F32)
        pay_ref[tokens + H * k : tokens + H * k + H] = term


def pay(branch, out_full, heads, logs):
    tokens, width = branch.shape
    return pl.pallas_call(
        pay_kernel,
        out_shape=[jax.ShapeDtypeStruct((tokens + 3 * H, width), BF16), jax.ShapeDtypeStruct((H, tokens), F32)],
        compiler_params=params(),
        cost_estimate=cost(),
        name="pay",
    )(branch, out_full, heads, logs)


def both_flipped(at_ref, mine_ref, got_ref, flipped, far, heads=False):
    tokens = mine_ref.shape[0]
    for core, ref in ((0, mine_ref), (1, got_ref)):
        turned = ref[...].T
        cols = slice(core * tokens, core * tokens + tokens)
        flip = jnp.bitwise_xor(at_ref[2], core) if heads else 0
        half = turned.shape[0] // 2
        if far is None:
            for part in range(2):
                to = jnp.bitwise_xor(flip, part) * half
                flipped[pl.ds(pl.multiple_of(to, half), half), cols] = turned[part * half : part * half + half]
            continue
        rows = turned.shape[0] // (8 * far)
        for z in range(far):
            at_z = jnp.bitwise_xor(z, flip * (far // 2))
            for y in range(2):
                for x in range(2):
                    a = ((z * 2 + y) * 2 + x) * 2 * rows
                    to_y, to_x = jnp.bitwise_xor(at_ref[0], y), jnp.bitwise_xor(at_ref[1], x)
                    first = ((1 - to_x) * 2 + to_y) * far + at_z
                    second = ((3 - to_y) * 2 + to_x) * far + at_z
                    for i, to in enumerate((first, second)):
                        to = pl.ds(pl.multiple_of(to * rows, rows), rows)
                        flipped[to, cols] = turned[a + i * rows : a + i * rows + rows]


def quarter_specs(rows, columns, index):
    return [pl.BlockSpec((rows // 4, columns), index)] * 4


def put_quarters(refs, cols, value):
    rows = value.shape[0] // 4
    for i, ref in enumerate(refs):
        ref[:, cols] = value[i * rows : i * rows + rows]


def late_grad_kernel(far, at_ref, low_ref, low_got, heads_ref, heads_got, lift_ref, lift_got, branch_ref, branch_got, *refs):
    quarters, flipped = refs[:4], refs[4]
    step = pl.program_id(0)
    last = pl.num_programs(0) - 1

    @pl.when(step == 0)
    def _():
        both_flipped(at_ref, low_ref, low_got, flipped, far)

    @pl.when(step < last)
    def _():
        put_quarters(quarters, slice(None), nn(flipped[...], cat([lift_ref[...], lift_got[...]], 0)).astype(BF16))

    @pl.when(step == last)
    def _():
        both_flipped(at_ref, heads_ref, heads_got, flipped, far, heads=True)
        put_quarters(quarters, slice(None), nn(flipped[...], cat([branch_ref[...], branch_got[...]], 0)).astype(BF16))


def late_grads(far, at, low, low_got, heads, heads_got, lift, lift_got, branch, branch_got):
    tokens, width = low.shape
    chunk = branch.shape[1]
    steps = lift.shape[1] // chunk
    whole = lambda shape: pl.BlockSpec(shape, lambda i: (0, 0))
    block = pl.BlockSpec((tokens, chunk), lambda i: (0, jnp.minimum(i, steps - 1)))
    return pl.pallas_call(
        functools.partial(late_grad_kernel, far),
        grid=(steps + 1,),
        in_specs=[SMEM] + [whole((tokens, width))] * 4 + [block, block] + [whole((tokens, chunk))] * 2,
        out_specs=quarter_specs(width, chunk, lambda i: (0, i)),
        out_shape=[jax.ShapeDtypeStruct((width // 4, (steps + 1) * chunk), BF16)] * 4,
        scratch_shapes=[pltpu.VMEM((width, 2 * tokens), BF16)],
        compiler_params=params(),
        cost_estimate=cost(),
        name="late_grads",
    )(at, low, low_got, heads, heads_got, lift, lift_got, branch, branch_got)


def qkv_grad_kernel(far, at_ref, x_ref, x_got, keep_ref, got_ref, *refs):
    note_refs, quarters, flipped = refs[:-5], refs[-5:-1], refs[-1]
    both_flipped(at_ref, x_ref, x_got, flipped, far)
    chunk = keep_ref.shape[2]
    for n in range(3):
        dw = nn(flipped[...], cat([keep_ref[n], got_ref[n]], 0)).astype(BF16)
        put_quarters(quarters, slice(n * chunk, n * chunk + chunk), dw)
    for ref in note_refs:
        put_quarters(quarters, slice(3 * chunk, 3 * chunk + ref.shape[1]), ref[...])


def qkv_grads(far, at, x, x_got, keep, got, notes=()):
    tokens, width = x.shape
    columns = 3 * keep.shape[2] + sum(v.shape[1] for v in notes)
    return pl.pallas_call(
        functools.partial(qkv_grad_kernel, far),
        in_specs=[SMEM] + [VMEM] * (4 + len(notes)),
        out_shape=[jax.ShapeDtypeStruct((width // 4, columns), BF16)] * 4,
        scratch_shapes=[pltpu.VMEM((width, 2 * tokens), BF16)],
        compiler_params=params(),
        cost_estimate=cost(),
        name="qkv_grads",
    )(at, x, x_got, keep, got, *notes)


FAR, Y, X, CORE = "far", "y", "x", "fsdp"
CTX = (FAR, Y, X)
ALL = CTX + (CORE,)


def swap(values, axis):
    return lax.ppermute(values, axis, [(0, 1), (1, 0)])


def swap_far(values, step):
    return lax.ppermute(values, FAR, [(i, i ^ step) for i in range(lax.axis_size(FAR))])


def together(*arrays):
    return lax.optimization_barrier(arrays)


def choose(core, left, right):
    return jnp.where(core == 0, left, right), jnp.where(core == 0, right, left)


def added(*terms):
    total = terms[0].astype(F32)
    for term in terms[1:]:
        total = total + term.astype(F32)
    return total.astype(BF16)


def own_rows(core, summed):
    mine, send = choose(core, summed[0], summed[1])
    return choose(core, mine, swap(send, CORE))


def color_nexts(keep_x, keep_y, there_x, there_y):
    return added(keep_x[1], there_x[1]), added(keep_y[1], there_y[1])


def color_sums(keep_x, keep_y, there_x, there_y, there_xy, there_yx):
    return jnp.stack([added(keep_x[0], there_x[0], there_xy), added(keep_y[0], there_y[0], there_yx)], 1)


def shards(inputs, segments, cotangent, qkv_weight, query_bias, value_bias, out_weight, out_bias, first_gain, first_shift, up_weight, up_bias, down_weight, down_bias, second_gain, second_shift):
    tokens, width = inputs.shape[1:]
    rows, hidden = up_weight.shape
    piece = down_weight.shape[0]
    near = width // 2
    blocks = lax.axis_size(CTX)
    place = lax.axis_index(CTX)
    core = lax.axis_index(CORE)
    at = jnp.stack([lax.axis_index(Y), lax.axis_index(X), core, lax.axis_index(FAR)]).astype(jnp.int32)
    far = 4 if rows % 32 == 0 and lax.axis_size(FAR) == 4 and piece == HIDDEN_BLOCK else None
    onward = [(i, i + 1) for i in range(blocks - 1)]
    back = [(i + 1, i) for i in range(blocks - 1)]

    def from_before(v):
        return lax.ppermute(v, CTX, onward)

    def from_after(v):
        return lax.ppermute(v, CTX, back)

    def own_first(v):
        return cat(choose(core, v[:, :near], v[:, near:]), 1)

    x = inputs[0]
    vectors = (query_bias, value_bias, out_bias, first_gain, first_shift, down_bias, second_gain, second_shift, up_bias)
    each = query_bias.shape[0]
    if far is None:
        split = lambda w, size: w.reshape(rows, -1, 2, size).swapaxes(0, 2).swapaxes(1, 2).reshape(2, rows, -1)
        sides = cat([split(qkv_weight, near), split(out_weight, near), split(up_weight, piece)], 2)
        mine, send = choose(core, sides[0], sides[1])
        both = cat(choose(core, mine, swap(send, CORE)), 0)
        whole = lambda v: lax.all_gather(v, CTX, axis=0, tiled=True)
        pair = lambda v: [v, swap(v, CORE)]
        qkv_parts = pair(whole(both[:, : 3 * near])) + pair(whole(both[:, 3 * near : 4 * near]))
        up_parts, down_parts = pair(whole(both[:, 4 * near :])), pair(whole(down_weight))
        x_before, x_after = from_before(x), from_after(x)
        table = lax.all_gather(cat(vectors, 0)[None], ALL, axis=0, tiled=True)
    else:
        mine, send, note = prepare(at, qkv_weight, out_weight, up_weight, vectors)
        block, up_block = arrange(at, mine, swap(send, CORE), note, hidden)
        cut = 4 * near
        lines = sum(v.shape[0] for v in vectors) // 128
        pair = jnp.stack([block, swap_far(block, 2)])
        down_pair = jnp.stack([down_weight, swap(down_weight, X)])
        pair, x_before, x_two = together(pair, from_before(x), x)
        wide = jnp.stack([pair, swap_far(pair, 1)]).reshape((4,) + block.shape)
        x_after = from_after(x_two)
        wide, up_block, down_pair, x_after = together(wide, up_block, down_pair, x_after)
        a1, b1, up_hi = swap(wide[:, 0], Y), swap(wide[:, 1], X), swap_far(up_block, 2)
        a1, b1, up_hi = together(a1, b1, up_hi)
        pair_a, pair_b, up_pair = jnp.stack([wide[:, 0], a1]), jnp.stack([wide[:, 1], b1]), jnp.stack([up_block, up_hi])
        a2, b2, up_lo = swap(pair_a, X), swap(pair_b, Y), swap_far(up_pair, 1)
        up_lo, down_pair = together(up_lo, down_pair)
        down_wide = lax.all_gather(down_pair, FAR, axis=1)
        a2, b2, up_lo = together(a2, b2, up_lo)
        first_parts = [pair_a, a2, pair_b, b2]
        qkv_parts = first_parts + [swap(p, CORE) for p in first_parts]
        up_wide = jnp.stack([up_pair, up_lo]).reshape((4,) + up_block.shape)
        up_y = swap(up_wide, Y)
        notes = jnp.stack([jnp.stack([qkv_parts[4 * c + s][:, :, :lines, cut:] for s in range(2)]) for c in range(2)])
        notes = notes.reshape(2, 2, 2, 2, 2, -1).swapaxes(3, 4)
        for axis, index in ((0, core), (1, at[1]), (2, at[0]), (3, at[3] // 2), (4, at[3] % 2)):
            notes = jnp.where(index == 0, notes, jnp.flip(notes, axis))
        table = notes.transpose(3, 4, 2, 1, 0, 5).reshape(2 * blocks, -1)

    rows_of = [table[:, each * i : each * i + each].reshape(1, width).astype(F32) for i in range(8)]
    query_row, value_row, out_row, gain_one, shift_one, down_row, gain_two, shift_two = rows_of
    up_row = table[:, 8 * each :].reshape(blocks, 2, piece).astype(F32)
    up_row = cat(choose(core, up_row[:, 0].reshape(1, -1), up_row[:, 1].reshape(1, -1)), 1)
    bias_own, bias_halo = mask_biases(segments[0], place, blocks, tokens)
    query_row, value_row, gap = own_first(query_row), own_first(value_row), jnp.zeros((1, near), F32)
    qkv_row = cat([query_row[:, :near], gap, value_row[:, :near], query_row[:, near:], gap, value_row[:, near:]], 1)

    mixed, before, qkv_full, out_full = project(far, at, qkv_parts, x, x_before, qkv_row)
    if far is not None:
        qkv_full, up_y = together(qkv_full, up_y)
        up_pair = jnp.stack([up_wide, up_y])
        up_x, up_pair_core = swap(up_pair, X), swap(up_pair, CORE)
    after = project_more(x_after, qkv_full, qkv_row)
    if far is not None:
        after, down_wide = together(after, down_wide)
        down_y, down_wide_core = swap(down_wide, Y), swap(down_wide, CORE)
    heads, logs = attend(mixed, before, after, bias_own, bias_halo)
    hat, inverse, first, low = out_project(heads, out_full, x, cat([out_row, gain_one, shift_one], 0))
    if far is not None:
        low, up_x, up_pair_core, down_wide_core, down_y = together(low, up_x, up_pair_core, down_wide_core, down_y)
        up_parts = [up_pair, up_x, up_pair_core, swap(up_x, CORE)]
        down_parts = [down_wide, down_y, down_wide_core, swap(down_y, CORE)]
    x_got, heads_got, low_got = swap(x, CORE), swap(heads, CORE), swap(low, CORE)
    active, act_send, slope, up_full = lift(far, at, up_parts, low, up_row)
    act_got = swap(act_send, CORE)
    active, x_got, heads_got, low_got = together(active, x_got, heads_got, low_got)
    result, grad_two, glow, sums_two, down_full = settle(
        far, at, down_parts, active, act_send, first, cat([down_row, gain_two, shift_two], 0), cotangent[0]
    )
    glow_got = swap(glow, CORE)
    lift_keep, lift_send, up_bias_part = lift_grads(glow, down_full, slope)
    lift_got = swap(lift_send, CORE)
    grad_one, branch, branch_mine, branch_send, sums_one = first_grads(at, lift_keep, lift_send, up_full, grad_two, hat, inverse, gain_one)
    branch_got = swap(branch_send, CORE)
    payload, means = pay(branch, out_full, heads, logs)
    pay_before, pay_after = from_before(payload), from_after(payload)
    down_part = down_grads(far, at, active, act_got, glow, glow_got)
    late = late_grads(far, at, low, low_got, heads, heads_got, lift_keep, lift_got, branch_mine, branch_got)
    dq, dkv, dq_sum = own_grads(mixed, before, after, payload, logs, means, bias_own, bias_halo)
    if far is not None:
        down_part = lax.psum_scatter(down_part.reshape(far, 2, 2, piece, width), FAR, scatter_dimension=0, tiled=False)
        by = lambda parts: [v.reshape(2, far, rows, v.shape[1]) for v in parts]
        late_send_x, late_keep_x, late_send_y, late_keep_y = by(late)
        late_x, late_y, pay_before, pay_after = together(late_send_x, late_send_y, pay_before, pay_after)
        late_x, late_y = swap(late_x, X), swap(late_y, Y)
    keep, send, dv_sum = halo_grads(mixed, before, after, pay_before, pay_after, bias_halo, dq, dkv)
    got = swap(send, CORE)
    if far is not None:
        got, late_x, late_y = together(got, late_x, late_y)
        late_xy, late_yx = color_nexts(late_keep_x, late_keep_y, late_x, late_y)
        late_xy, late_yx, got = together(late_xy, late_yx, got)
        late_xy, late_yx = swap(late_xy, Y), swap(late_yx, X)
    features = (own_first(dq_sum), own_first(dv_sum), sums_one[2], sums_one[0], sums_one[1], sums_two[2], sums_two[0], sums_two[1])
    small = jnp.stack([v.reshape(blocks, 2, each) for v in features], 2)
    small = small.reshape(blocks, 2, -1)
    small = choose(core, small[:, 0], small[:, 1])
    small = [cat([v, up_bias_part[:, hidden // 2 * i : hidden // 2 * (i + 1)].reshape(blocks, piece)], 1) for i, v in enumerate(small)]
    small = small[0] + swap(small[1], CORE)
    if far is None:
        qkv = qkv_grads(far, at, x, x_got, keep, got)
        total = lambda v: lax.psum_scatter(v, CTX, scatter_dimension=0, tiled=True)
        down_sum, small_sum = total(down_part).astype(F32), total(small)[0]
        late_sum, qkv_sum = [total(cat(v, 0)).reshape(2, rows, -1) for v in (late, qkv)]
    else:
        small = small.reshape(far, 2, 2, lines, 128).transpose(2, 1, 0, 3, 4)
        for axis, index in ((0, at[1]), (1, at[0])):
            small = jnp.where(index == 0, small, jnp.flip(small, axis))
        small = jnp.flip(small, 0).reshape(2 * 2 * far, lines, 128).astype(BF16)
        note = jnp.zeros((8 * far, rows, 128), BF16).at[: 4 * far, :lines].set(small).reshape(width, 128)
        qkv_send_x, qkv_keep_x, qkv_send_y, qkv_keep_y = by(qkv_grads(far, at, x, x_got, keep, got, (note,)))
        qkv_send_x, qkv_send_y, late_xy, late_yx = together(qkv_send_x, qkv_send_y, late_xy, late_yx)
        qkv_x, qkv_y = swap(qkv_send_x, X), swap(qkv_send_y, Y)
        late_sum = color_sums(late_keep_x, late_keep_y, late_x, late_y, late_xy, late_yx)
        late_sum, down_part = together(late_sum, down_part)
        late_sum = lax.psum_scatter(late_sum, FAR, scatter_dimension=0, tiled=False)
        down_y = swap(down_part[1], Y)
        qkv_x, qkv_y, grad_one, down_y = together(qkv_x, qkv_y, grad_one, down_y)
        qkv_xy, qkv_yx = color_nexts(qkv_keep_x, qkv_keep_y, qkv_x, qkv_y)
        qkv_xy, qkv_yx = swap(qkv_xy, Y), swap(qkv_yx, X)
        down_part = added(down_part[0], down_y)
        down_x = swap(down_part[1], X)
        qkv_xy, qkv_yx, late_sum, down_x = together(qkv_xy, qkv_yx, late_sum, down_x)
        qkv_sum = lax.psum_scatter(color_sums(qkv_keep_x, qkv_keep_y, qkv_x, qkv_y, qkv_xy, qkv_yx), FAR, scatter_dimension=0, tiled=False)
        down_sum = down_part[0].astype(F32) + down_x.astype(F32)
        small_sum = qkv_sum[0, :lines, 3 * near :].reshape(-1).astype(F32)
    inputs_grad = nt(cat([*keep, *send], 1), qkv_full)
    inputs_grad = (grad_one + inputs_grad).astype(BF16)[None]
    wide = hidden // 2
    left, right = own_rows(core, late_sum)
    up_sum = jnp.stack([v[:, :wide].reshape(rows, blocks, piece) for v in (left, right)], 2).reshape(rows, hidden).astype(F32)
    out_sum = cat([left[:, wide:], right[:, wide:]], 1).astype(F32)
    left, right = own_rows(core, qkv_sum[:, :, : 3 * near])
    qkv_sum = jnp.stack([v.reshape(rows, 3, near) for v in (left, right)], 2).reshape(rows, 3 * width).astype(F32)
    s = [small_sum[each * i : each * i + each] for i in range(8)]
    return (
        result[None], inputs_grad, qkv_sum, s[0], s[1], out_sum, s[2], s[3], s[4], up_sum, small_sum[8 * each :], down_sum, s[5], s[6], s[7],
    )


def solution(mesh):
    devices = mesh.devices
    split = jax.sharding.Mesh(devices.reshape(devices.shape[0] // 4, 2, 2, devices.shape[1]), ALL)
    rows, vec = P(ALL, None), P(ALL)
    tokens = P(CORE, CTX, None)
    return jax.shard_map(
        shards,
        mesh=split,
        in_specs=(tokens, P(CORE, None), tokens, rows, vec, vec, rows, vec, vec, vec, rows, vec, rows, vec, vec, vec),
        out_specs=(tokens, tokens, rows, vec, vec, rows, vec, vec, vec, rows, vec, rows, vec, vec, vec),
        check_vma=False,
    )
```

```python
import functools

import jax
import jax.numpy as jnp
from jax import lax
from jax.experimental import pallas as pl
from jax.experimental.pallas import tpu as pltpu
from jax.sharding import PartitionSpec as P

H = 16
HD = 64
WINDOW = 1024
HALF = WINDOW // 2
ROWS = 256
NARROW = 128
PAIR = 2 * HD
FILL = -1e30
EPS = 1e-05
HIDDEN_BLOCK = 128
F32 = jnp.float32
BF16 = jnp.bfloat16
VMEM_BYTES = 56 * 1024 * 1024
SMEM = pl.BlockSpec(memory_space=pltpu.SMEM)
ANY = pl.BlockSpec(memory_space=pl.ANY)
VMEM = pl.BlockSpec(memory_space=pltpu.VMEM)


def nn(a, b):
    return lax.dot_general(a, b, (((1,), (0,)), ((), ())), preferred_element_type=F32)


def nt(a, b):
    return lax.dot_general(a, b, (((1,), (1,)), ((), ())), preferred_element_type=F32)


def tn(a, b):
    return lax.dot_general(a, b, (((0,), (0,)), ((), ())), preferred_element_type=F32)


def cat(parts, axis):
    return jnp.concatenate(parts, axis=axis)


def cost(us):
    return pl.CostEstimate(flops=int(us * 1.0e9), bytes_accessed=int(us * 3.5e6), transcendentals=0)


def params():
    return pltpu.CompilerParams(vmem_limit_bytes=VMEM_BYTES)


def head_masks(scale):
    lane = lax.broadcasted_iota(jnp.int32, (1, PAIR), 1)
    first = jnp.where(lane < HD, scale, 0.0).astype(F32)
    second = jnp.where(lane < HD, 0.0, scale).astype(F32)
    return first.astype(BF16), second.astype(BF16)


def stacked(values, masks):
    return cat([values * masks[0], values * masks[1]], 0)


def strip(i, tokens, rows=ROWS):
    return slice(rows * i, rows * i + tokens + rows)


def put_rows(ref, cols, pair):
    head = lax.broadcasted_iota(jnp.int32, (H, 1), 0) - 2 * pl.program_id(0)
    ref[:, cols] = jnp.where(head == 0, pair[0], jnp.where(head == 1, pair[1], ref[:, cols]))


def take_row(values, h, pair=None):
    head = lax.broadcasted_iota(jnp.int32, (H, 1), 0) - 2 * (pl.program_id(0) if pair is None else pair)
    return jnp.sum(jnp.where(head == h, values, 0.0), axis=0, keepdims=True)


def attend_kernel(q_ref, ko_ref, kp_ref, kn_ref, vo_ref, vp_ref, vn_ref, bo_ref, bh_ref, out_ref, lse_ref, kh, vh):
    tokens = q_ref.shape[0]
    kh[:tokens] = kp_ref[...]
    kh[tokens:] = kn_ref[...]
    ones = head_masks(1.0)
    vh[:tokens] = vp_ref[...]
    vh[tokens:] = vn_ref[...]
    vo = stacked(vo_ref[...], ones)
    scaled = head_masks(HD ** -0.5)
    lane = lax.broadcasted_iota(jnp.int32, (ROWS, PAIR), 1)
    for i in range(tokens // ROWS):
        rows = slice(ROWS * i, ROWS * i + ROWS)
        window = strip(i, tokens)
        q = q_ref[rows]
        own_parts, halo_parts, totals, logs = [], [], [], []
        for mask in scaled:
            qm = q * mask
            so = nt(qm, ko_ref[...]) + bo_ref[rows]
            sh = nt(qm, kh[window]) + bh_ref[i]
            peak = jnp.maximum(jnp.max(so, axis=1, keepdims=True), jnp.max(sh, axis=1, keepdims=True))
            po = jnp.exp(so - peak)
            ph = jnp.exp(sh - peak)
            total = jnp.sum(po, axis=1, keepdims=True) + jnp.sum(ph, axis=1, keepdims=True)
            own_parts.append(po.astype(BF16))
            halo_parts.append(ph.astype(BF16))
            totals.append(1.0 / total)
            logs.append((peak + jnp.log(total)).T)
        out = nn(cat(own_parts, 1), vo) + nn(cat(halo_parts, 1), stacked(vh[window], ones))
        out = out * jnp.where(lane < HD, totals[0], totals[1])
        out_ref[rows] = out.astype(BF16)
        put_rows(lse_ref, rows, logs)


def attend(mixed, before, after, bias_own, bias_halo):
    tokens, width = mixed.shape[0], mixed.shape[1] // 3
    pairs = width // PAIR

    near = pairs // 2

    def column(part):
        return pl.BlockSpec((tokens, PAIR), lambda p: (0, (p // near * 3 + part) * near + p % near))

    whole = lambda shape: pl.BlockSpec(shape, lambda p: (0,) * len(shape))
    return pl.pallas_call(
        attend_kernel,
        grid=(pairs,),
        in_specs=[column(0), column(1), column(1), column(1), column(2), column(2), column(2), whole(bias_own.shape), whole(bias_halo.shape)],
        out_specs=[pl.BlockSpec((tokens, PAIR), lambda p: (0, p)), whole((H, tokens))],
        out_shape=[jax.ShapeDtypeStruct((tokens, width), BF16), jax.ShapeDtypeStruct((H, tokens), F32)],
        scratch_shapes=[pltpu.VMEM((2 * tokens, PAIR), BF16), pltpu.VMEM((2 * tokens, PAIR), BF16)],
        compiler_params=params(),
        cost_estimate=cost(0.48),
        name="attend",
    )(mixed, mixed, before, after, mixed, before, after, bias_own, bias_halo)


def own_grad_kernel(q_ref, ko_ref, kp_ref, kn_ref, vo_ref, vp_ref, vn_ref, do_ref, log_ref, mean_ref, bo_ref, bh_ref, dq_ref, dkv_ref, sum_ref, kh, vh):
    tokens = q_ref.shape[0]
    kh[:tokens] = kp_ref[...]
    kh[tokens:] = kn_ref[...]
    vh[:tokens] = vp_ref[...]
    vh[tokens:] = vn_ref[...]
    ones = head_masks(1.0)
    scaled = head_masks(HD ** -0.5)
    k_own = ko_ref[...]
    v_own = vo_ref[...]
    k_pair = stacked(k_own, scaled)
    log_rows = [take_row(log_ref[...], h) for h in range(2)]
    mean_rows = [take_row(mean_ref[...], h) for h in range(2)]
    chunk = ROWS
    for c in range(tokens // chunk):
        cols = slice(chunk * c, chunk * c + chunk)
        q = q_ref[cols]
        do = do_ref[cols]
        probs, grads, qs, dos = [], [], [], []
        for h in range(2):
            qm = q * scaled[h]
            dm = do * ones[h]
            st = nt(k_own, qm) + bo_ref[:, cols]
            pt = jnp.exp(st - log_rows[h][:, cols])
            gt = pt * (nt(v_own, dm) - mean_rows[h][:, cols])
            probs.append(pt.astype(BF16))
            grads.append(gt.astype(BF16))
            qs.append(qm)
            dos.append(dm)
        dv = nn(cat(probs, 1), cat(dos, 0))
        dk = nn(cat(grads, 1), cat(qs, 0))
        if c == 0:
            dkv_ref[0, 0] = dk
            dkv_ref[0, 1] = dv
        else:
            dkv_ref[0, 0] += dk
            dkv_ref[0, 1] += dv
        dq_own = tn(cat(grads, 0), k_pair)
        for r in range(chunk // ROWS):
            i = c * (chunk // ROWS) + r
            rows = slice(ROWS * i, ROWS * i + ROWS)
            window = strip(i, tokens)
            halo = []
            for h in range(2):
                qm = q[ROWS * r : ROWS * r + ROWS] * scaled[h]
                dm = do[ROWS * r : ROWS * r + ROWS] * ones[h]
                s = nt(qm, kh[window]) + bh_ref[i]
                p = jnp.exp(s - log_rows[h][:, rows].T)
                halo.append((p * (nt(dm, vh[window]) - mean_rows[h][:, rows].T)).astype(BF16))
            dq = dq_own[ROWS * r : ROWS * r + ROWS] + nn(cat(halo, 1), stacked(kh[window], scaled))
            dq = dq.astype(BF16)
            dq_ref[0, rows] = dq
            sum_ref[...] = column_sum(dq.astype(F32)) + (sum_ref[...] if i else 0.0)


def own_grads(mixed, before, after, payload, logs, means, bias_own, bias_halo):
    tokens, width = mixed.shape[0], payload.shape[1]
    pairs = width // PAIR

    near = pairs // 2

    def column(part):
        return pl.BlockSpec((tokens, PAIR), lambda p: (0, (p // near * 3 + part) * near + p % near))

    whole = lambda shape: pl.BlockSpec(shape, lambda p: (0,) * len(shape))
    block = pl.BlockSpec((tokens, PAIR), lambda p: (0, p))
    return pl.pallas_call(
        own_grad_kernel,
        grid=(pairs,),
        in_specs=[column(0), column(1), column(1), column(1), column(2), column(2), column(2), block, whole(logs.shape), whole(means.shape), whole(bias_own.shape), whole(bias_halo.shape)],
        out_specs=[
            pl.BlockSpec((1, tokens, PAIR), lambda p: (p // near, 0, p % near)),
            pl.BlockSpec((1, 2, tokens, PAIR), lambda p: (p // near, 0, 0, p % near)),
            pl.BlockSpec((1, PAIR), lambda p: (0, p)),
        ],
        out_shape=[
            jax.ShapeDtypeStruct((2, tokens, width // 2), BF16),
            jax.ShapeDtypeStruct((2, 2, tokens, width // 2), F32),
            jax.ShapeDtypeStruct((1, width), F32),
        ],
        scratch_shapes=[pltpu.VMEM((2 * tokens, PAIR), BF16), pltpu.VMEM((2 * tokens, PAIR), BF16)],
        compiler_params=params(),
        cost_estimate=cost(29.5),
        name="own_grads",
    )(mixed, mixed, before, after, mixed, before, after, payload, logs, means, bias_own, bias_halo)


def halo_grad_kernel(half, ko_ref, vo_ref, qp_ref, qn_ref, dp_ref, dn_ref, lp0, lp1, lp2, ln0, ln1, ln2, bh_ref, dkv_in, dk_ref, dv_ref, sum_ref, qh, dh, lh):
    tokens = ko_ref.shape[0]
    qh[:tokens] = qp_ref[...]
    qh[tokens:] = qn_ref[...]
    dh[:tokens] = dp_ref[...]
    dh[tokens:] = dn_ref[...]
    for first, refs in ((0, (lp0, lp1, lp2)), (tokens, (ln0, ln1, ln2))):
        table = refs[0][...].astype(F32) + refs[1][...].astype(F32) + refs[2][...].astype(F32)
        for h in range(2):
            row = take_row(table, h, pl.program_id(0) + half * pl.num_programs(0))
            lh[0, h : h + 1, first : first + tokens] = row[:, :tokens]
            lh[1, h : h + 1, first : first + tokens] = row[:, tokens:]
    ones = head_masks(1.0)
    scaled = head_masks(HD ** -0.5)
    for j in range(tokens // NARROW):
        rows = slice(NARROW * j, NARROW * j + NARROW)
        window = strip(j, tokens, NARROW)
        q = qh[window]
        do = dh[window]
        k = ko_ref[rows]
        v = vo_ref[rows]
        probs, grads, qs, dos = [], [], [], []
        for h in range(2):
            qm = q * scaled[h]
            dm = do * ones[h]
            st = nt(k, qm) + bh_ref[j]
            pt = jnp.exp(st - lh[0, h : h + 1, window])
            gt = pt * (nt(v, dm) - lh[1, h : h + 1, window])
            probs.append(pt.astype(BF16))
            grads.append(gt.astype(BF16))
            qs.append(qm)
            dos.append(dm)
        dk_ref[rows] = (dkv_in[0, 0, rows] + nn(cat(grads, 1), cat(qs, 0))).astype(BF16)
        dv = (dkv_in[0, 1, rows] + nn(cat(probs, 1), cat(dos, 0))).astype(BF16)
        dv_ref[rows] = dv
        sum_ref[...] = column_sum(dv.astype(F32)) + (sum_ref[...] if j else 0.0)


def halo_grads(mixed, before, after, grad_before, grad_after, bias_halo, dkv, half):
    tokens, width = dkv.shape[2], 2 * dkv.shape[3]
    near = width // PAIR // 2

    def column(part):
        return pl.BlockSpec((tokens, PAIR), lambda p: (0, (half * 3 + part) * near + p))

    whole = lambda shape: pl.BlockSpec(shape, lambda p: (0,) * len(shape))
    both = pl.BlockSpec((1, 2, tokens, PAIR), lambda p: (half, 0, 0, p))
    tables = [pl.BlockSpec((H, width), lambda p, k=k: (tokens // H + k, 0)) for k in range(3)]
    block = pl.BlockSpec((tokens, PAIR), lambda p: (0, half * near + p))
    made = pl.BlockSpec((tokens, PAIR), lambda p: (0, p))
    return pl.pallas_call(
        functools.partial(halo_grad_kernel, half),
        grid=(near,),
        in_specs=[column(1), column(2), column(0), column(0), block, block] + tables + tables + [whole(bias_halo.shape), both],
        out_specs=[made, made, pl.BlockSpec((1, PAIR), lambda p: (0, p))],
        out_shape=[jax.ShapeDtypeStruct((tokens, width // 2), BF16)] * 2 + [jax.ShapeDtypeStruct((1, width // 2), F32)],
        scratch_shapes=[
            pltpu.VMEM((2 * tokens, PAIR), BF16),
            pltpu.VMEM((2 * tokens, PAIR), BF16),
            pltpu.VMEM((2, 2, 2 * tokens), F32),
        ],
        compiler_params=params(),
        cost_estimate=cost(0.05),
        name="halo_grads",
    )(mixed, mixed, before, after, grad_before, grad_after, *[grad_before] * 3, *[grad_after] * 3, bias_halo, dkv)


def mask_biases(segments, place, blocks, tokens):
    line = cat([jnp.full((tokens,), -1, jnp.int32), segments, jnp.full((tokens,), -1, jnp.int32)], 0)
    near = lax.dynamic_slice_in_dim(line, place * tokens, 3 * tokens)
    own = near[tokens : 2 * tokens]
    bias_own = jnp.where(own[:, None] == own[None, :], 0.0, FILL).astype(F32)
    halo = cat([near[:tokens], near[2 * tokens :]], 0)
    at = jnp.arange(tokens, dtype=jnp.int32)
    halo_at = cat([at - tokens, at + tokens], 0)
    allowed = (own[:, None] == halo[None, :]) & (jnp.abs(halo_at[None, :] - at[:, None]) < HALF)
    bias = jnp.where(allowed, 0.0, FILL).astype(F32)
    strips = [jnp.stack([bias[r * i : r * i + r, strip(i, tokens, r)] for i in range(tokens // r)]) for r in (ROWS, NARROW)]
    return bias_own, *strips


def normalized(values):
    average = jnp.mean(values, axis=1, keepdims=True)
    centered = values - average
    spread = jnp.mean(centered * centered, axis=1, keepdims=True)
    inverse = lax.rsqrt(spread + EPS)
    return centered * inverse, inverse


def norm_back(grad, gain, hat, inverse):
    scaled = grad * gain
    return inverse * (
        scaled
        - jnp.mean(scaled, axis=1, keepdims=True)
        - hat * jnp.mean(scaled * hat, axis=1, keepdims=True)
    )


def column_sum(values):
    return jnp.sum(values, axis=0, keepdims=True)


def part_blocks(at_ref, order, second, far):
    for first in range(2):
        rel = {order[-2]: first, order[-1]: second}
        y = jnp.bitwise_xor(at_ref[0], rel["y"])
        x = jnp.bitwise_xor(at_ref[1], rel["x"])
        for i in range(far):
            z = jnp.bitwise_xor(at_ref[3], (i % 2) * 2 + i // 2) if order[0] == "z" else i
            yield first, i, (z * 2 + y) * 2 + x


def start_all(copies):
    for copy in copies:
        copy.start()


def wait_all(copies):
    for copy in copies:
        copy.wait()


def block_place(at_ref, order, z, y, x, far):
    where = {"z": (z, far), "y": (jnp.bitwise_xor(at_ref[0], y), 2), "x": (jnp.bitwise_xor(at_ref[1], x), 2)}
    to = 0
    for axis in order:
        to = to * where[axis][1] + where[axis][0]
    return to


def prepare_kernel(at_ref, qkv_ref, out_ref, up_ref, *refs):
    vectors, mine_ref, send_ref, note_ref = refs[:-3], *refs[-3:]
    width = out_ref.shape[1]
    place = 0
    for ref, piece in ((qkv_ref, width // 2), (out_ref, width // 2), (up_ref, HIDDEN_BLOCK)):
        for i in range(0, ref.shape[1], 2 * piece):
            mine_ref[:, place : place + piece] = ref[:, pl.ds(pl.multiple_of(i + at_ref[2] * piece, piece), piece)]
            send_ref[:, place : place + piece] = ref[:, pl.ds(pl.multiple_of(i + (1 - at_ref[2]) * piece, piece), piece)]
            place += piece
    line = cat([v[...].astype(F32) for v in vectors], 1).astype(BF16)
    note_ref[...] = jnp.zeros_like(note_ref)
    for i in range(line.shape[1] // 128):
        note_ref[i : i + 1] = line[:, i * 128 : i * 128 + 128]


def prepare(at, qkv, out, up, vectors):
    rows = qkv.shape[0]
    columns = (qkv.shape[1] + out.shape[1] + up.shape[1]) // 2
    half = jax.ShapeDtypeStruct((rows, columns), BF16)
    return pl.pallas_call(
        prepare_kernel,
        in_specs=[SMEM] + [VMEM] * (3 + len(vectors)),
        out_shape=[half, half, jax.ShapeDtypeStruct((rows, 128), BF16)],
        compiler_params=params(),
        cost_estimate=cost(0.04),
        name="prepare",
    )(at, qkv, out, up, *[v[None] for v in vectors])


def arrange_kernel(at_ref, mine_ref, got_ref, note_ref, block_ref, up_ref):
    rows, cut = mine_ref.shape[0], block_ref.shape[2] - 128
    block_ref[0, :, cut:] = note_ref[...]
    block_ref[1, :, cut:] = jnp.zeros_like(note_ref)

    def lay(first, second):
        for i, ref in ((0, first), (1, second)):
            block_ref[i, :, :cut] = ref[:, :cut]
            up_ref[i * rows : i * rows + rows] = ref[:, cut:]

    @pl.when(at_ref[2] == 0)
    def _():
        lay(mine_ref, got_ref)

    @pl.when(at_ref[2] != 0)
    def _():
        lay(got_ref, mine_ref)


def arrange(at, mine, got, note, hidden):
    rows, columns = mine.shape
    return pl.pallas_call(
        arrange_kernel,
        in_specs=[SMEM] + [VMEM] * 3,
        out_shape=[
            jax.ShapeDtypeStruct((2, rows, columns - hidden // 2 + 128), BF16),
            jax.ShapeDtypeStruct((2 * rows, hidden // 2), BF16),
        ],
        compiler_params=params(),
        cost_estimate=cost(0.04),
        name="arrange",
    )(at, mine, got, note)


def first_copies(refs, qkv, out, sems, at_ref, far):
    width, columns = qkv.shape
    half, near = width // 2, columns // 2
    copies = []

    def add(source, target):
        copies.append(pltpu.make_async_copy(source, target, sems.at[len(copies)]))

    def column(core):
        return pl.ds(pl.multiple_of(jnp.bitwise_xor(at_ref[2], core) * half, half), half)

    for core in range(2):
        if far is None:
            add(refs[core], qkv.at[:, pl.ds(core * near, near)])
            for part in range(2):
                row = pl.ds(pl.multiple_of(jnp.bitwise_xor(at_ref[2], part) * half, half), half)
                add(refs[2 + core].at[pl.ds(part * half, half)], out.at[row, column(core)])
            continue
        rows = width // (8 * far)
        for color, order in enumerate(("zyx", "zxy")):
            for second in range(2):
                ref = refs[core * 4 + color * 2 + second]
                for first, z, block in part_blocks(at_ref, order, second, far):
                    row = (block * 2 + color) * rows
                    add(ref.at[first, z, :, pl.ds(0, near)], qkv.at[pl.ds(pl.multiple_of(row, rows), rows), pl.ds(core * near, near)])
                    row = jnp.bitwise_xor(row, at_ref[2] * half)
                    add(ref.at[first, z, :, pl.ds(near, half)], out.at[pl.ds(pl.multiple_of(row, rows), rows), column(core)])
    return copies


def project_kernel(far, parts, *refs):
    at_ref, refs = refs[0], refs[1:]
    part_refs, refs = refs[:parts], refs[parts:]
    own_ref, row_ref, own_out, qkv_out, out_out, qkv, out, sems, out_sems = refs
    copies = first_copies(part_refs, qkv, out, sems, at_ref, far)
    start_all(copies)
    wait_all(copies)
    keep = [pltpu.make_async_copy(qkv, qkv_out, out_sems.at[0]), pltpu.make_async_copy(out, out_out, out_sems.at[1])]
    start_all(keep)
    chunk = 512

    def body(j, carry):
        cols = pl.ds(pl.multiple_of(j * chunk, chunk), chunk)
        own_out[:, cols] = (nn(own_ref[...], qkv[:, cols]) + row_ref[:, cols]).astype(BF16)
        return carry

    lax.fori_loop(0, qkv.shape[1] // chunk, body, 0)
    wait_all(keep)


def copy_count(far, each):
    return 2 if far is None else 8 * far * each


def project(far, at, parts, x, row):
    tokens, width = x.shape
    columns = row.shape[1]
    mixed = jax.ShapeDtypeStruct((tokens, columns), BF16)
    return pl.pallas_call(
        functools.partial(project_kernel, far, len(parts)),
        in_specs=[SMEM] + [ANY] * len(parts) + [VMEM] * 2,
        out_specs=[VMEM, ANY, ANY],
        out_shape=[mixed, jax.ShapeDtypeStruct((width, columns), BF16), jax.ShapeDtypeStruct((width, width), BF16)],
        scratch_shapes=[
            pltpu.VMEM((width, columns), BF16),
            pltpu.VMEM((width, width), BF16),
            pltpu.SemaphoreType.DMA((6 if far is None else 64 * far,)),
            pltpu.SemaphoreType.DMA((2,)),
        ],
        compiler_params=params(),
        cost_estimate=cost(0.26),
        name="project",
    )(at, *parts, x, row)


def project_more_kernel(before_ref, after_ref, w_ref, row_ref, before_out, after_out):
    for source, target in ((before_ref, before_out), (after_ref, after_out)):
        target[...] = (nn(source[...], w_ref[...]) + row_ref[...]).astype(BF16)


def project_more(before, after, full, row, chunk=512):
    tokens, width = before.shape
    columns = full.shape[1]
    whole = pl.BlockSpec((tokens, width), lambda i: (0, 0))
    block = pl.BlockSpec((tokens, chunk), lambda i: (0, i))
    return pl.pallas_call(
        project_more_kernel,
        grid=(columns // chunk,),
        in_specs=[whole, whole, pl.BlockSpec((width, chunk), lambda i: (0, i)), pl.BlockSpec((1, chunk), lambda i: (0, i))],
        out_specs=[block, block],
        out_shape=[jax.ShapeDtypeStruct((tokens, columns), BF16)] * 2,
        compiler_params=params(),
        cost_estimate=cost(0.214),
        name="project_more",
    )(before, after, full, row)


def out_kernel(heads_ref, w_ref, x_ref, vec_ref, hat_ref, inv_ref, low_ref):
    branch = nn(heads_ref[...], w_ref[...]) + vec_ref[0:1]
    hat, inverse = normalized(x_ref[...].astype(F32) + branch)
    hat_ref[...] = hat
    inv_ref[...] = inverse
    low_ref[...] = (hat * vec_ref[1:2] + vec_ref[2:3]).astype(BF16)


def out_project(heads, out_full, x, vectors):
    tokens, width = heads.shape
    rows = tokens // 2
    block = pl.BlockSpec((rows, width), lambda i: (i, 0))
    return pl.pallas_call(
        out_kernel,
        grid=(2,),
        in_specs=[block, pl.BlockSpec(out_full.shape, lambda i: (0, 0)), block, pl.BlockSpec(vectors.shape, lambda i: (0, 0))],
        out_specs=[block, pl.BlockSpec((rows, 1), lambda i: (i, 0)), block],
        out_shape=[
            jax.ShapeDtypeStruct((tokens, width), F32),
            jax.ShapeDtypeStruct((tokens, 1), F32),
            jax.ShapeDtypeStruct((tokens, width), BF16),
        ],
        compiler_params=params(),
        cost_estimate=cost(0.114),
        name="out_project",
    )(heads, out_full, x, vectors)


def up_copies(refs, full, sems, at_ref, far):
    width, half = full.shape[0], full.shape[1] // 2
    copies = []
    for core in range(2):
        cols = pl.ds(core * half, half)
        if far is None:
            copies.append(pltpu.make_async_copy(refs[core], full.at[:, cols], sems.at[core]))
            continue
        rows = width // (4 * far)
        for second in range(2):
            ref = refs[core * 2 + second]
            for first, z, block in part_blocks(at_ref, "zyx", second, far):
                to = full.at[pl.ds(pl.multiple_of(block * rows, rows), rows), cols]
                copies.append(pltpu.make_async_copy(ref.at[first, z], to, sems.at[len(copies)]))
    return copies


def down_copies(refs, full, sems, at_ref, far):
    half = full.shape[0] // 2
    copies = []
    for core in range(2):
        if far is None:
            copies.append(pltpu.make_async_copy(refs[core], full.at[pl.ds(core * half, half)], sems.at[core]))
            continue
        rows = half // (4 * far)
        for second in range(2):
            ref = refs[core * 2 + second]
            for first, z, block in part_blocks(at_ref, "xy", second, far):
                to = full.at[pl.ds(pl.multiple_of(core * half + block * rows, rows), rows)]
                copies.append(pltpu.make_async_copy(ref.at[first, z], to, sems.at[len(copies)]))
    return copies


def middle_kernel(far, ups, downs, *refs):
    at_ref, refs = refs[0], refs[1:]
    up_refs, down_refs, refs = refs[:ups], refs[ups : ups + downs], refs[ups + downs :]
    low_ref, row_ref, vec_ref, log_ref, inv_ref, hat_in, dy_in, heads_in, out_in = refs[:9]
    act_out, act_send, result_out, glow_out, lift_out, lift_send, one_out, mine_out, send_out, pay_out, mean_ref, row_sums, two_sums, one_sums = refs[9:23]
    up, down, out, hat, dy, heads, act, slope, result, glow, total, branch, sides, payload, up_sems, down_sems, in_sems, out_sems = refs[23:]
    tokens, width = low_ref.shape
    half = up.shape[1] // 2
    chunk = 512
    steps = 2 * half // chunk
    from_up = up_copies(up_refs, up, up_sems, at_ref, far)
    from_down = down_copies(down_refs, down, down_sems, at_ref, far)
    loads = [pltpu.make_async_copy(*pair, in_sems.at[i]) for i, pair in enumerate(((hat_in, hat), (dy_in, dy), (out_in, out), (heads_in, heads)))]
    start_all(from_up)
    start_all(from_down)
    start_all(loads)
    stores = []

    def store(source, target):
        copy = pltpu.make_async_copy(source, target, out_sems.at[len(stores)])
        stores.append(copy)
        copy.start()

    def cols(i):
        return pl.ds(pl.multiple_of(i * chunk, chunk), chunk)

    def raise_one(i):
        lifted = nn(low_ref[...], up[:, cols(i)]) + row_ref[:, cols(i)]
        phi = 0.5 * (1.0 + lax.erf(lifted * (0.5 ** 0.5)))
        density = jnp.exp(lifted * lifted * -0.5) * 0.3989422804014327
        act[:, cols(i)] = (lifted * phi).astype(BF16)
        slope[:, cols(i)] = (phi + lifted * density).astype(BF16)

    def settle_one(i):
        total[...] += nn(act[:, cols(i)], down[cols(i)])

    half_up, half_down = len(from_up) // 2, len(from_down) // 2
    wait_all(from_up[:half_up])
    total[...] = jnp.zeros_like(total)
    raise_one(0)
    wait_all(from_down[:half_down])

    def both(i, carry):
        raise_one(i)
        settle_one(i - 1)
        return carry

    lax.fori_loop(1, steps // 2, both, 0)
    wait_all(from_up[half_up:])
    both(steps // 2, 0)
    wait_all(from_down[half_down:])
    lax.fori_loop(steps // 2 + 1, steps, both, 0)
    settle_one(steps - 1)
    store(act.at[:, pl.ds(0, half)], act_out)
    store(act.at[:, pl.ds(half, half)], act_send)
    wait_all(loads)

    rows = 128
    for n in range(tokens // rows):
        at = slice(rows * n, rows * n + rows)
        first = hat[at] * vec_ref[3:4] + vec_ref[4:5]
        hat_two, inverse = normalized(first + (total[at] + vec_ref[0:1]))
        result[at] = (hat_two * vec_ref[1:2] + vec_ref[2:3]).astype(BF16)
        grad = dy[at].astype(F32)
        part = [column_sum(grad * hat_two), column_sum(grad)]
        grad = norm_back(grad, vec_ref[1:2], hat_two, inverse)
        low = grad.astype(BF16)
        total[at] = grad
        glow[at] = low
        part = cat(part + [column_sum(low.astype(F32))], 0)
        two_sums[...] = part if n == 0 else two_sums[...] + part
    store(result, result_out)
    store(glow, glow_out)

    def lower_one(i):
        value = (nt(glow[...], down[cols(i)]) * slope[:, cols(i)].astype(F32)).astype(BF16)
        slope[:, cols(i)] = value
        row_sums[:, cols(i)] = column_sum(value.astype(F32))

    def first_one(i):
        total[...] += nt(slope[:, cols(i)], up[:, cols(i)])

    lower_one(0)

    def back(i, carry):
        lower_one(i)
        first_one(i - 1)
        return carry

    lax.fori_loop(1, steps, back, 0)
    store(slope.at[:, pl.ds(0, half)], lift_out)
    store(slope.at[:, pl.ds(half, half)], lift_send)
    first_one(steps - 1)

    for n in range(tokens // rows):
        at = slice(rows * n, rows * n + rows)
        grad = total[at]
        one = norm_back(grad, vec_ref[3:4], hat[at], inv_ref[at])
        low = one.astype(BF16)
        total[at] = one
        branch[at] = low
        part = cat([column_sum(grad * hat[at]), column_sum(grad), column_sum(low.astype(F32))], 0)
        one_sums[...] = part if n == 0 else one_sums[...] + part
    store(total, one_out)
    middle = width // 2
    for n in range(2):
        side = pl.multiple_of(jnp.bitwise_xor(at_ref[2], n) * middle, middle)
        sides[n] = branch[:, pl.ds(side, middle)]
    store(sides.at[0], mine_out)
    store(sides.at[1], send_out)

    head = lax.broadcasted_iota(jnp.int32, (H, width), 1) // HD
    pick = jnp.where(head == lax.broadcasted_iota(jnp.int32, (H, width), 0), 1.0, 0.0).astype(F32)
    for n in range(tokens // rows):
        at = slice(rows * n, rows * n + rows)
        grad = nt(branch[at], out[...]).astype(BF16)
        payload[at] = grad
        product = grad.astype(F32) * heads[at].astype(F32)
        mean_ref[:, at] = lax.dot_general(
            pick, product, (((1,), (1,)), ((), ())), precision=lax.Precision.HIGHEST, preferred_element_type=F32
        )
    rest = cat([log_ref[...], mean_ref[...]], 1)
    for n in range(3):
        term = rest.astype(BF16)
        rest = rest - term.astype(F32)
        payload[tokens + H * n : tokens + H * n + H] = term
    store(payload, pay_out)
    wait_all(stores)


def middle(far, at, up_parts, down_parts, low, row, vectors, logs, inverse, hat, dy, heads, out_full):
    tokens, width = low.shape
    hidden = row.shape[1]
    half = hidden // 2
    shape = jax.ShapeDtypeStruct
    pay_shape = (tokens + 3 * H, width)
    return pl.pallas_call(
        functools.partial(middle_kernel, far, len(up_parts), len(down_parts)),
        in_specs=[SMEM] + [ANY] * (len(up_parts) + len(down_parts)) + [VMEM] * 5 + [ANY] * 4,
        out_specs=[ANY] * 10 + [VMEM] * 4,
        out_shape=[
            shape((tokens, half), BF16),
            shape((tokens, half), BF16),
            shape((tokens, width), BF16),
            shape((tokens, width), BF16),
            shape((tokens, half), BF16),
            shape((tokens, half), BF16),
            shape((tokens, width), F32),
            shape((tokens, width // 2), BF16),
            shape((tokens, width // 2), BF16),
            shape(pay_shape, BF16),
            shape((H, tokens), F32),
            shape((1, hidden), F32),
            shape((3, width), F32),
            shape((3, width), F32),
        ],
        scratch_shapes=[
            pltpu.VMEM((width, hidden), BF16),
            pltpu.VMEM((hidden, width), BF16),
            pltpu.VMEM((width, width), BF16),
            pltpu.VMEM((tokens, width), F32),
            pltpu.VMEM((tokens, width), BF16),
            pltpu.VMEM((tokens, width), BF16),
            pltpu.VMEM((tokens, hidden), BF16),
            pltpu.VMEM((tokens, hidden), BF16),
            pltpu.VMEM((tokens, width), BF16),
            pltpu.VMEM((tokens, width), BF16),
            pltpu.VMEM((tokens, width), F32),
            pltpu.VMEM((tokens, width), BF16),
            pltpu.VMEM((2, tokens, width // 2), BF16),
            pltpu.VMEM(pay_shape, BF16),
            pltpu.SemaphoreType.DMA((copy_count(far, 2),)),
            pltpu.SemaphoreType.DMA((copy_count(far, 2),)),
            pltpu.SemaphoreType.DMA((4,)),
            pltpu.SemaphoreType.DMA((10,)),
        ],
        compiler_params=params(),
        cost_estimate=cost(45),
        name="middle",
    )(at, *up_parts, *down_parts, low, row, vectors, logs, inverse, hat, dy, heads, out_full)


def down_grad_kernel(far, at_ref, act_ref, act_got, glow_ref, glow_got, dw_ref, glows):
    tokens = glow_ref.shape[0]

    @pl.when(pl.program_id(0) == 0)
    def _():
        glows[:tokens] = glow_ref[...]
        glows[tokens:] = glow_got[...]

    dw = tn(cat([act_ref[...], act_got[...]], 0), glows[...]).astype(BF16)
    if far is None:
        dw_ref[...] = dw
        return
    rows = dw.shape[0] // 4
    for j in range(4):
        to = block_place(at_ref, "yx", 0, j // 2, j % 2, far)
        dw_ref[pl.ds(pl.multiple_of(to * rows, rows), rows)] = dw[j * rows : j * rows + rows]


def down_grads(far, at, active, act_got, glow, glow_got):
    tokens, half = active.shape
    width = glow.shape[1]
    chunk = half // 4
    whole = pl.BlockSpec((tokens, width), lambda i: (0, 0))
    block = pl.BlockSpec((tokens, chunk), lambda i: (0, i))
    return pl.pallas_call(
        functools.partial(down_grad_kernel, far),
        grid=(4,),
        in_specs=[SMEM, block, block, whole, whole],
        out_specs=pl.BlockSpec((chunk, width), lambda i: (i, 0)),
        out_shape=jax.ShapeDtypeStruct((half, width), BF16),
        scratch_shapes=[pltpu.VMEM((2 * tokens, width), BF16)],
        compiler_params=params(),
        cost_estimate=cost(8.5),
        name="down_grads",
    )(at, active, act_got, glow, glow_got)


def both_flipped(at_ref, mine_ref, got_ref, flipped, far, heads=False):
    tokens = mine_ref.shape[0]
    for core, ref in ((0, mine_ref), (1, got_ref)):
        turned = ref[...].T
        cols = slice(core * tokens, core * tokens + tokens)
        flip = jnp.bitwise_xor(at_ref[2], core) if heads else 0
        half = turned.shape[0] // 2
        if far is None:
            for part in range(2):
                to = jnp.bitwise_xor(flip, part) * half
                flipped[pl.ds(pl.multiple_of(to, half), half), cols] = turned[part * half : part * half + half]
            continue
        rows = turned.shape[0] // (8 * far)
        for z in range(far):
            at_z = jnp.bitwise_xor(z, flip * (far // 2))
            for y in range(2):
                for x in range(2):
                    a = ((z * 2 + y) * 2 + x) * 2 * rows
                    to_y, to_x = jnp.bitwise_xor(at_ref[0], y), jnp.bitwise_xor(at_ref[1], x)
                    first = ((1 - to_x) * 2 + to_y) * far + at_z
                    second = ((3 - to_y) * 2 + to_x) * far + at_z
                    for i, to in enumerate((first, second)):
                        to = pl.ds(pl.multiple_of(to * rows, rows), rows)
                        flipped[to, cols] = turned[a + i * rows : a + i * rows + rows]


def quarter_specs(rows, columns, index):
    return [pl.BlockSpec((rows // 4, columns), index)] * 4


def put_quarters(refs, cols, value):
    rows = value.shape[0] // 4
    for i, ref in enumerate(refs):
        ref[:, cols] = value[i * rows : i * rows + rows]


def late_grad_kernel(far, at_ref, low_ref, low_got, heads_ref, heads_got, lift_ref, lift_got, branch_ref, branch_got, *refs):
    quarters, flipped = refs[:4], refs[4]
    step = pl.program_id(0)
    last = pl.num_programs(0) - 1

    @pl.when(step == 0)
    def _():
        both_flipped(at_ref, low_ref, low_got, flipped, far)

    @pl.when(step < last)
    def _():
        put_quarters(quarters, slice(None), nn(flipped[...], cat([lift_ref[...], lift_got[...]], 0)).astype(BF16))

    @pl.when(step == last)
    def _():
        both_flipped(at_ref, heads_ref, heads_got, flipped, far, heads=True)
        put_quarters(quarters, slice(None), nn(flipped[...], cat([branch_ref[...], branch_got[...]], 0)).astype(BF16))


def late_grads(far, at, low, low_got, heads, heads_got, lift, lift_got, branch, branch_got):
    tokens, width = low.shape
    chunk = branch.shape[1]
    steps = lift.shape[1] // chunk
    whole = lambda shape: pl.BlockSpec(shape, lambda i: (0, 0))
    block = pl.BlockSpec((tokens, chunk), lambda i: (0, jnp.minimum(i, steps - 1)))
    return pl.pallas_call(
        functools.partial(late_grad_kernel, far),
        grid=(steps + 1,),
        in_specs=[SMEM] + [whole((tokens, width))] * 4 + [block, block] + [whole((tokens, chunk))] * 2,
        out_specs=quarter_specs(width, chunk, lambda i: (0, i)),
        out_shape=[jax.ShapeDtypeStruct((width // 4, (steps + 1) * chunk), BF16)] * 4,
        scratch_shapes=[pltpu.VMEM((width, 2 * tokens), BF16)],
        compiler_params=params(),
        cost_estimate=cost(12),
        name="late_grads",
    )(at, low, low_got, heads, heads_got, lift, lift_got, branch, branch_got)


def qkv_grad_kernel(far, at_ref, x_ref, x_got, *refs):
    keeps, gots, refs = refs[:3], refs[3:6], refs[6:]
    note_refs, quarters, flipped = refs[:-5], refs[-5:-1], refs[-1]
    both_flipped(at_ref, x_ref, x_got, flipped, far)
    chunk = keeps[0].shape[1]
    for n in range(3):
        dw = nn(flipped[...], cat([keeps[n][...], gots[n][...]], 0)).astype(BF16)
        put_quarters(quarters, slice(n * chunk, n * chunk + chunk), dw)
    for ref in note_refs:
        put_quarters(quarters, slice(3 * chunk, 3 * chunk + ref.shape[1]), ref[...])


def qkv_grads(far, at, x, x_got, keep, got, notes=()):
    tokens, width = x.shape
    columns = 3 * keep[0].shape[1] + sum(v.shape[1] for v in notes)
    return pl.pallas_call(
        functools.partial(qkv_grad_kernel, far),
        in_specs=[SMEM] + [VMEM] * (8 + len(notes)),
        out_shape=[jax.ShapeDtypeStruct((width // 4, columns), BF16)] * 4,
        scratch_shapes=[pltpu.VMEM((width, 2 * tokens), BF16)],
        compiler_params=params(),
        cost_estimate=cost(8.3),
        name="qkv_grads",
    )(at, x, x_got, *keep, *got, *notes)


FAR, Y, X, CORE = "far", "y", "x", "fsdp"
CTX = (FAR, Y, X)
ALL = CTX + (CORE,)


def swap(values, axis):
    return lax.ppermute(values, axis, [(0, 1), (1, 0)])


def swap_both(values):
    return lax.ppermute(values, (Y, X), [(i, 3 - i) for i in range(4)])


def swap_far(values, step):
    return lax.ppermute(values, FAR, [(i, i ^ step) for i in range(lax.axis_size(FAR))])


def together(*arrays):
    return lax.optimization_barrier(arrays)


def choose(core, left, right):
    return jnp.where(core == 0, left, right), jnp.where(core == 0, right, left)


def added(*terms):
    total = terms[0].astype(F32)
    for term in terms[1:]:
        total = total + term.astype(F32)
    return total.astype(BF16)


def own_rows(core, summed):
    mine, send = choose(core, summed[0], summed[1])
    return choose(core, mine, swap(send, CORE))


def color_nexts(keep_x, keep_y, there_x, there_y):
    return added(keep_x[1], there_x[1]), added(keep_y[1], there_y[1])


def color_sums(keep_x, keep_y, there_x, there_y, there_xy, there_yx):
    return jnp.stack([added(keep_x[0], there_x[0], there_xy), added(keep_y[0], there_y[0], there_yx)], 1)


def shards(inputs, segments, cotangent, qkv_weight, query_bias, value_bias, out_weight, out_bias, first_gain, first_shift, up_weight, up_bias, down_weight, down_bias, second_gain, second_shift):
    tokens, width = inputs.shape[1:]
    rows, hidden = up_weight.shape
    piece = down_weight.shape[0]
    near = width // 2
    blocks = lax.axis_size(CTX)
    place = lax.axis_index(CTX)
    core = lax.axis_index(CORE)
    at = jnp.stack([lax.axis_index(Y), lax.axis_index(X), core, lax.axis_index(FAR)]).astype(jnp.int32)
    far = 4 if rows % 32 == 0 and lax.axis_size(FAR) == 4 and piece == HIDDEN_BLOCK else None
    onward = [(i, i + 1) for i in range(blocks - 1)]
    back = [(i + 1, i) for i in range(blocks - 1)]

    def from_before(v):
        return lax.ppermute(v, CTX, onward)

    def from_after(v):
        return lax.ppermute(v, CTX, back)

    def own_first(v):
        return cat(choose(core, v[:, :near], v[:, near:]), 1)

    x = inputs[0]
    vectors = (query_bias, value_bias, out_bias, first_gain, first_shift, down_bias, second_gain, second_shift, up_bias)
    each = query_bias.shape[0]
    if far is None:
        split = lambda w, size: w.reshape(rows, -1, 2, size).swapaxes(0, 2).swapaxes(1, 2).reshape(2, rows, -1)
        sides = cat([split(qkv_weight, near), split(out_weight, near), split(up_weight, piece)], 2)
        mine, send = choose(core, sides[0], sides[1])
        both = cat(choose(core, mine, swap(send, CORE)), 0)
        whole = lambda v: lax.all_gather(v, CTX, axis=0, tiled=True)
        pair = lambda v: [v, swap(v, CORE)]
        qkv_parts = pair(whole(both[:, : 3 * near])) + pair(whole(both[:, 3 * near : 4 * near]))
        up_parts, down_parts = pair(whole(both[:, 4 * near :])), pair(whole(down_weight))
        x_before, x_after = from_before(x), from_after(x)
        table = lax.all_gather(cat(vectors, 0)[None], ALL, axis=0, tiled=True)
    else:
        mine, send, note = prepare(at, qkv_weight, out_weight, up_weight, vectors)
        block, up_block = arrange(at, mine, swap(send, CORE), note, hidden)
        cut = 4 * near
        lines = sum(v.shape[0] for v in vectors) // 128
        pair = jnp.stack([block, swap_far(block, 2)])
        down_pair = jnp.stack([down_weight, swap(down_weight, X)])
        pair, x_before, x_two = together(pair, from_before(x), x)
        wide = jnp.stack([pair, swap_far(pair, 1)]).reshape((4,) + block.shape)
        x_after = from_after(x_two)
        wide, up_block, down_pair, x_after = together(wide, up_block, down_pair, x_after)
        a1, b1, up_hi = swap(wide[:, 0], Y), swap(wide[:, 1], X), swap_far(up_block, 2)
        a1, b1, up_hi = together(a1, b1, up_hi)
        pair_a, pair_b, up_pair = jnp.stack([wide[:, 0], a1]), jnp.stack([wide[:, 1], b1]), jnp.stack([up_block, up_hi])
        a2, b2, up_lo = swap(pair_a, X), swap(pair_b, Y), swap_far(up_pair, 1)
        up_lo, down_pair = together(up_lo, down_pair)
        down_wide = lax.all_gather(down_pair, FAR, axis=1)
        a2, b2, up_lo = together(a2, b2, up_lo)
        first_parts = [pair_a, a2, pair_b, b2]
        qkv_parts = first_parts + [swap(p, CORE) for p in first_parts]
        up_wide = jnp.stack([up_pair, up_lo]).reshape((4,) + up_block.shape)
        up_y = swap(up_wide, Y)
        notes = jnp.stack([jnp.stack([qkv_parts[4 * c + s][:, :, :lines, cut:] for s in range(2)]) for c in range(2)])
        notes = notes.reshape(2, 2, 2, 2, 2, -1).swapaxes(3, 4)
        for axis, index in ((0, core), (1, at[1]), (2, at[0]), (3, at[3] // 2), (4, at[3] % 2)):
            notes = jnp.where(index == 0, notes, jnp.flip(notes, axis))
        table = notes.transpose(3, 4, 2, 1, 0, 5).reshape(2 * blocks, -1)

    rows_of = [table[:, each * i : each * i + each].reshape(1, width).astype(F32) for i in range(8)]
    query_row, value_row, out_row, gain_one, shift_one, down_row, gain_two, shift_two = rows_of
    up_row = table[:, 8 * each :].reshape(blocks, 2, piece).astype(F32)
    up_row = cat(choose(core, up_row[:, 0].reshape(1, -1), up_row[:, 1].reshape(1, -1)), 1)
    bias_own, bias_halo, bias_narrow = mask_biases(segments[0], place, blocks, tokens)
    query_row, value_row, gap = own_first(query_row), own_first(value_row), jnp.zeros((1, near), F32)
    qkv_row = cat([query_row[:, :near], gap, value_row[:, :near], query_row[:, near:], gap, value_row[:, near:]], 1)

    mixed, qkv_full, out_full = project(far, at, qkv_parts, x, qkv_row)
    if far is not None:
        qkv_full, up_y = together(qkv_full, up_y)
        up_pair = jnp.stack([up_wide, up_y])
        up_x, up_pair_core = swap(up_pair, X), swap(up_pair, CORE)
    before, after = project_more(x_before, x_after, qkv_full, qkv_row)
    if far is not None:
        before, down_wide = together(before, down_wide)
        down_y, down_wide_core = swap(down_wide, Y), swap(down_wide, CORE)
    heads, logs = attend(mixed, before, after, bias_own, bias_halo)
    hat, inverse, low = out_project(heads, out_full, x, cat([out_row, gain_one, shift_one], 0))
    low, x_got, heads_got = together(low, swap(x, CORE), swap(heads, CORE))
    if far is not None:
        low, up_x, up_pair_core, down_wide_core, down_y = together(low, up_x, up_pair_core, down_wide_core, down_y)
        up_parts = [up_pair, up_x, up_pair_core, swap(up_x, CORE)]
        down_parts = [down_wide, down_y, down_wide_core, swap(down_y, CORE)]
    low_got = swap(low, CORE)
    (
        active, act_send, result, glow, lift_keep, lift_send, grad_one, branch_mine, branch_send, payload, means, up_bias_part, sums_two, sums_one,
    ) = middle(
        far, at, up_parts, down_parts, low, up_row, cat([down_row, gain_two, shift_two, gain_one, shift_one], 0),
        logs, inverse, hat, cotangent[0], heads, out_full,
    )
    payload, low_got = together(payload, low_got)
    pay_before, pay_after = from_before(payload), from_after(payload)
    act_got, glow_got, lift_got, branch_got = swap(act_send, CORE), swap(glow, CORE), swap(lift_send, CORE), swap(branch_send, CORE)
    down_part = down_grads(far, at, active, act_got, glow, glow_got)
    late = late_grads(far, at, low, low_got, heads, heads_got, lift_keep, lift_got, branch_mine, branch_got)
    dq, dkv, dq_sum = own_grads(mixed, before, after, payload, logs, means, bias_own, bias_halo)
    dq_keep, dq_send = dq[0], dq[1]
    if far is not None:
        down_part = lax.psum_scatter(down_part.reshape(far, 2, 2, piece, width), FAR, scatter_dimension=0, tiled=False)
        by = lambda parts: [v.reshape(2, far, rows, v.shape[1]) for v in parts]
        late_send_x, late_keep_x, late_send_y, late_keep_y = by(late)
        late_x, late_y, pay_before, pay_after, dkv = together(late_send_x, late_send_y, pay_before, pay_after, dkv)
        late_x, late_y = swap(late_x, X), swap(late_y, Y)
    *send, sum_send = halo_grads(mixed, before, after, pay_before, pay_after, bias_narrow, dkv, 1)
    send = [dq_send] + send
    *keep, sum_keep = halo_grads(mixed, before, after, pay_before, pay_after, bias_narrow, dkv, 0)
    if far is not None:
        late_x, late_y, sum_keep = together(late_x, late_y, sum_keep)
    keep, dv_sum = [dq_keep] + keep, cat([sum_keep, sum_send], 1)
    got = [swap(v, CORE) for v in send]
    if far is not None:
        late_xy, late_yx = color_nexts(late_keep_x, late_keep_y, late_x, late_y)
        late_xy, late_yx, *got = together(late_xy, late_yx, *got)
        late_xy, late_yx = swap(late_xy, Y), swap(late_yx, X)
    features = (own_first(dq_sum), own_first(dv_sum), sums_one[2], sums_one[0], sums_one[1], sums_two[2], sums_two[0], sums_two[1])
    small = jnp.stack([v.reshape(blocks, 2, each) for v in features], 2).reshape(blocks, 2, -1)
    sides = choose(core, up_bias_part[:, : hidden // 2], up_bias_part[:, hidden // 2 :])
    small = cat([small, jnp.stack([v.reshape(blocks, piece) for v in sides], 1)], 2)
    if far is None:
        qkv = qkv_grads(far, at, x, x_got, keep, got)
        total = lambda v: lax.psum_scatter(v, CTX, scatter_dimension=0, tiled=True)
        down_sum = total(down_part).astype(F32)
        small_sum = lax.psum_scatter(small.reshape(2 * blocks, -1), ALL, scatter_dimension=0, tiled=True)[0]
        late_sum, qkv_sum = [total(cat(v, 0)).reshape(2, rows, -1) for v in (late, qkv)]
    else:
        small = small.astype(BF16).reshape(far, 2, 2, 2, lines, 128).transpose(3, 2, 1, 0, 4, 5)
        for axis, index in ((1, at[1]), (2, at[0])):
            small = jnp.where(index == 0, small, jnp.flip(small, axis))
        small = jnp.stack([jnp.flip(small[0], 0), jnp.flip(small[1].swapaxes(0, 1), 0)])
        small = small.reshape(8 * far, lines, 128)
        note = jnp.zeros((8 * far, rows, 128), BF16).at[:, :lines].set(small).reshape(width, 128)
        qkv_send_x, qkv_keep_x, qkv_send_y, qkv_keep_y = by(qkv_grads(far, at, x, x_got, keep, got, (note,)))
        qkv_send_x, qkv_send_y, late_xy, late_yx = together(qkv_send_x, qkv_send_y, late_xy, late_yx)
        qkv_x, qkv_y = swap(qkv_send_x, X), swap(qkv_send_y, Y)
        late_sum = color_sums(late_keep_x, late_keep_y, late_x, late_y, late_xy, late_yx)
        late_sum = lax.psum_scatter(late_sum, FAR, scatter_dimension=0, tiled=False)
        qkv_x, qkv_y, down_part = together(qkv_x, qkv_y, down_part)
        qkv_xy, qkv_yx = color_nexts(qkv_keep_x, qkv_keep_y, qkv_x, qkv_y)
        qkv_xy, qkv_yx, down_part, *both = together(qkv_xy, qkv_yx, down_part, *keep, *send)
        keep, send = both[:3], both[3:]
        qkv_xy, qkv_yx = swap(qkv_xy, Y), swap(qkv_yx, X)
        down_y, down_x, down_xy = swap(down_part[1, 0], Y), swap(down_part[0, 1], X), swap_both(down_part[1, 1])
        qkv_xy, qkv_yx, late_sum = together(qkv_xy, qkv_yx, late_sum)
        qkv_sum = lax.psum_scatter(color_sums(qkv_keep_x, qkv_keep_y, qkv_x, qkv_y, qkv_xy, qkv_yx), FAR, scatter_dimension=0, tiled=False)
        qkv_sum, down_y, down_x, down_xy, late_sum = together(qkv_sum, down_y, down_x, down_xy, late_sum)
        down_sum = down_part[0, 0].astype(F32) + down_y.astype(F32) + down_x.astype(F32) + down_xy.astype(F32)
    inputs_grad = nt(cat([*keep, *send], 1), qkv_full)
    inputs_grad = (grad_one + inputs_grad).astype(BF16)[None]
    wide = hidden // 2
    left, right = own_rows(core, late_sum)
    up_sum = jnp.stack([v[:, :wide].reshape(rows, blocks, piece) for v in (left, right)], 2).reshape(rows, hidden).astype(F32)
    out_sum = cat([left[:, wide:], right[:, wide:]], 1).astype(F32)
    mine, send = choose(core, qkv_sum[0], qkv_sum[1])
    got = swap(send, CORE)
    left, right = choose(core, mine[:, : 3 * near], got[:, : 3 * near])
    if far is not None:
        small_sum = (mine[:lines, 3 * near :].astype(F32) + got[:lines, 3 * near :].astype(F32)).reshape(-1)
    qkv_sum = jnp.stack([v.reshape(rows, 3, near) for v in (left, right)], 2).reshape(rows, 3 * width).astype(F32)
    s = [small_sum[each * i : each * i + each] for i in range(8)]
    return (
        result[None], inputs_grad, qkv_sum, s[0], s[1], out_sum, s[2], s[3], s[4], up_sum, small_sum[8 * each :], down_sum, s[5], s[6], s[7],
    )


def solution(mesh):
    devices = mesh.devices
    split = jax.sharding.Mesh(devices.reshape(devices.shape[0] // 4, 2, 2, devices.shape[1]), ALL)
    rows, vec = P(ALL, None), P(ALL)
    tokens = P(CORE, CTX, None)
    return jax.shard_map(
        shards,
        mesh=split,
        in_specs=(tokens, P(CORE, None), tokens, rows, vec, vec, rows, vec, vec, vec, rows, vec, rows, vec, vec, vec),
        out_specs=(tokens, tokens, rows, vec, vec, rows, vec, vec, vec, rows, vec, rows, vec, vec, vec),
        check_vma=False,
    )
```

```python
import functools

import jax
import jax.numpy as jnp
from jax import lax
from jax.experimental import pallas as pl
from jax.experimental.pallas import tpu as pltpu
from jax.sharding import PartitionSpec as P

H = 16
HD = 64
WINDOW = 1024
HALF = WINDOW // 2
ROWS = 256
NARROW = 128
PAIR = 2 * HD
FILL = -1e30
EPS = 1e-05
HIDDEN_BLOCK = 128
F32 = jnp.float32
BF16 = jnp.bfloat16
VMEM_BYTES = 56 * 1024 * 1024
SMEM = pl.BlockSpec(memory_space=pltpu.SMEM)
ANY = pl.BlockSpec(memory_space=pl.ANY)
VMEM = pl.BlockSpec(memory_space=pltpu.VMEM)


def nn(a, b):
    return lax.dot_general(a, b, (((1,), (0,)), ((), ())), preferred_element_type=F32)


def nt(a, b):
    return lax.dot_general(a, b, (((1,), (1,)), ((), ())), preferred_element_type=F32)


def tn(a, b):
    return lax.dot_general(a, b, (((0,), (0,)), ((), ())), preferred_element_type=F32)


def cat(parts, axis):
    return jnp.concatenate(parts, axis=axis)


def cost(us):
    return pl.CostEstimate(flops=int(us * 1.0e9), bytes_accessed=int(us * 3.5e6), transcendentals=0)


def params():
    return pltpu.CompilerParams(vmem_limit_bytes=VMEM_BYTES)


def head_masks(scale):
    lane = lax.broadcasted_iota(jnp.int32, (1, PAIR), 1)
    first = jnp.where(lane < HD, scale, 0.0).astype(F32)
    second = jnp.where(lane < HD, 0.0, scale).astype(F32)
    return first.astype(BF16), second.astype(BF16)


def stacked(values, masks):
    return cat([values * masks[0], values * masks[1]], 0)


def strip(i, tokens, rows=ROWS):
    return slice(rows * i, rows * i + tokens + rows)


def put_rows(ref, cols, pair):
    head = lax.broadcasted_iota(jnp.int32, (H, 1), 0) - 2 * pl.program_id(0)
    ref[:, cols] = jnp.where(head == 0, pair[0], jnp.where(head == 1, pair[1], ref[:, cols]))


def take_row(values, h, pair=None):
    head = lax.broadcasted_iota(jnp.int32, (H, 1), 0) - 2 * (pl.program_id(0) if pair is None else pair)
    return jnp.sum(jnp.where(head == h, values, 0.0), axis=0, keepdims=True)


def attend_kernel(q_ref, ko_ref, kp_ref, kn_ref, vo_ref, vp_ref, vn_ref, bo_ref, bh_ref, out_ref, lse_ref, kh, vh):
    tokens = q_ref.shape[0]
    kh[:tokens] = kp_ref[...]
    kh[tokens:] = kn_ref[...]
    ones = head_masks(1.0)
    vh[:tokens] = vp_ref[...]
    vh[tokens:] = vn_ref[...]
    vo = stacked(vo_ref[...], ones)
    scaled = head_masks(HD ** -0.5)
    lane = lax.broadcasted_iota(jnp.int32, (ROWS, PAIR), 1)
    for i in range(tokens // ROWS):
        rows = slice(ROWS * i, ROWS * i + ROWS)
        window = strip(i, tokens)
        q = q_ref[rows]
        own_parts, halo_parts, totals, logs = [], [], [], []
        for mask in scaled:
            qm = q * mask
            so = nt(qm, ko_ref[...]) + bo_ref[rows]
            sh = nt(qm, kh[window]) + bh_ref[i]
            peak = jnp.maximum(jnp.max(so, axis=1, keepdims=True), jnp.max(sh, axis=1, keepdims=True))
            po = jnp.exp(so - peak)
            ph = jnp.exp(sh - peak)
            total = jnp.sum(po, axis=1, keepdims=True) + jnp.sum(ph, axis=1, keepdims=True)
            own_parts.append(po.astype(BF16))
            halo_parts.append(ph.astype(BF16))
            totals.append(1.0 / total)
            logs.append((peak + jnp.log(total)).T)
        out = nn(cat(own_parts, 1), vo) + nn(cat(halo_parts, 1), stacked(vh[window], ones))
        out = out * jnp.where(lane < HD, totals[0], totals[1])
        out_ref[rows] = out.astype(BF16)
        put_rows(lse_ref, rows, logs)


def attend(mixed, before, after, bias_own, bias_halo):
    tokens, width = mixed.shape[0], mixed.shape[1] // 3
    pairs = width // PAIR

    near = pairs // 2

    def column(part):
        return pl.BlockSpec((tokens, PAIR), lambda p: (0, (p // near * 3 + part) * near + p % near))

    whole = lambda shape: pl.BlockSpec(shape, lambda p: (0,) * len(shape))
    return pl.pallas_call(
        attend_kernel,
        grid=(pairs,),
        in_specs=[column(0), column(1), column(1), column(1), column(2), column(2), column(2), whole(bias_own.shape), whole(bias_halo.shape)],
        out_specs=[pl.BlockSpec((tokens, PAIR), lambda p: (0, p)), whole((H, tokens))],
        out_shape=[jax.ShapeDtypeStruct((tokens, width), BF16), jax.ShapeDtypeStruct((H, tokens), F32)],
        scratch_shapes=[pltpu.VMEM((2 * tokens, PAIR), BF16), pltpu.VMEM((2 * tokens, PAIR), BF16)],
        compiler_params=params(),
        cost_estimate=cost(0.48),
        name="attend",
    )(mixed, mixed, before, after, mixed, before, after, bias_own, bias_halo)


def own_grad_kernel(q_ref, ko_ref, kp_ref, kn_ref, vo_ref, vp_ref, vn_ref, do_ref, log_ref, mean_ref, bo_ref, bh_ref, dq_keep, dq_send, dkv_ref, sum_ref, kh, vh, dq_ref):
    tokens = q_ref.shape[0]
    kh[:tokens] = kp_ref[...]
    kh[tokens:] = kn_ref[...]
    vh[:tokens] = vp_ref[...]
    vh[tokens:] = vn_ref[...]
    ones = head_masks(1.0)
    scaled = head_masks(HD ** -0.5)
    k_own = ko_ref[...]
    v_own = vo_ref[...]
    k_pair = stacked(k_own, scaled)
    log_rows = [take_row(log_ref[...], h) for h in range(2)]
    mean_rows = [take_row(mean_ref[...], h) for h in range(2)]
    chunk = ROWS
    for c in range(tokens // chunk):
        cols = slice(chunk * c, chunk * c + chunk)
        q = q_ref[cols]
        do = do_ref[cols]
        probs, grads, qs, dos = [], [], [], []
        for h in range(2):
            qm = q * scaled[h]
            dm = do * ones[h]
            st = nt(k_own, qm) + bo_ref[:, cols]
            pt = jnp.exp(st - log_rows[h][:, cols])
            gt = pt * (nt(v_own, dm) - mean_rows[h][:, cols])
            probs.append(pt.astype(BF16))
            grads.append(gt.astype(BF16))
            qs.append(qm)
            dos.append(dm)
        dv = nn(cat(probs, 1), cat(dos, 0))
        dk = nn(cat(grads, 1), cat(qs, 0))
        if c == 0:
            dkv_ref[0, 0] = dk
            dkv_ref[0, 1] = dv
        else:
            dkv_ref[0, 0] += dk
            dkv_ref[0, 1] += dv
        dq_own = tn(cat(grads, 0), k_pair)
        for r in range(chunk // ROWS):
            i = c * (chunk // ROWS) + r
            rows = slice(ROWS * i, ROWS * i + ROWS)
            window = strip(i, tokens)
            halo = []
            for h in range(2):
                qm = q[ROWS * r : ROWS * r + ROWS] * scaled[h]
                dm = do[ROWS * r : ROWS * r + ROWS] * ones[h]
                s = nt(qm, kh[window]) + bh_ref[i]
                p = jnp.exp(s - log_rows[h][:, rows].T)
                halo.append((p * (nt(dm, vh[window]) - mean_rows[h][:, rows].T)).astype(BF16))
            dq = dq_own[ROWS * r : ROWS * r + ROWS] + nn(cat(halo, 1), stacked(kh[window], scaled))
            dq = dq.astype(BF16)
            dq_ref[rows] = dq
            sum_ref[...] = column_sum(dq.astype(F32)) + (sum_ref[...] if i else 0.0)

    @pl.when(pl.program_id(0) < pl.num_programs(0) // 2)
    def _():
        dq_keep[...] = dq_ref[...]

    @pl.when(pl.program_id(0) >= pl.num_programs(0) // 2)
    def _():
        dq_send[...] = dq_ref[...]


def own_grads(mixed, before, after, payload, logs, means, bias_own, bias_halo):
    tokens, width = mixed.shape[0], payload.shape[1]
    pairs = width // PAIR

    near = pairs // 2

    def column(part):
        return pl.BlockSpec((tokens, PAIR), lambda p: (0, (p // near * 3 + part) * near + p % near))

    whole = lambda shape: pl.BlockSpec(shape, lambda p: (0,) * len(shape))
    block = pl.BlockSpec((tokens, PAIR), lambda p: (0, p))
    return pl.pallas_call(
        own_grad_kernel,
        grid=(pairs,),
        in_specs=[column(0), column(1), column(1), column(1), column(2), column(2), column(2), block, whole(logs.shape), whole(means.shape), whole(bias_own.shape), whole(bias_halo.shape)],
        out_specs=[
            pl.BlockSpec((tokens, PAIR), lambda p: (0, jnp.minimum(p, near - 1))),
            pl.BlockSpec((tokens, PAIR), lambda p: (0, jnp.maximum(p - near, 0))),
            pl.BlockSpec((1, 2, tokens, PAIR), lambda p: (p // near, 0, 0, p % near)),
            pl.BlockSpec((1, PAIR), lambda p: (0, p)),
        ],
        out_shape=[
            jax.ShapeDtypeStruct((tokens, width // 2), BF16),
            jax.ShapeDtypeStruct((tokens, width // 2), BF16),
            jax.ShapeDtypeStruct((2, 2, tokens, width // 2), F32),
            jax.ShapeDtypeStruct((1, width), F32),
        ],
        scratch_shapes=[pltpu.VMEM((2 * tokens, PAIR), BF16), pltpu.VMEM((2 * tokens, PAIR), BF16), pltpu.VMEM((tokens, PAIR), BF16)],
        compiler_params=params(),
        cost_estimate=cost(27.5),
        name="own_grads",
    )(mixed, mixed, before, after, mixed, before, after, payload, logs, means, bias_own, bias_halo)


def halo_grad_kernel(half, ko_ref, vo_ref, qp_ref, qn_ref, dp_ref, dn_ref, lp0, lp1, lp2, ln0, ln1, ln2, bh_ref, dkv_in, dk_ref, dv_ref, sum_ref, qh, dh, lh):
    tokens = ko_ref.shape[0]
    qh[:tokens] = qp_ref[...]
    qh[tokens:] = qn_ref[...]
    dh[:tokens] = dp_ref[...]
    dh[tokens:] = dn_ref[...]
    for first, refs in ((0, (lp0, lp1, lp2)), (tokens, (ln0, ln1, ln2))):
        table = refs[0][...].astype(F32) + refs[1][...].astype(F32) + refs[2][...].astype(F32)
        for h in range(2):
            row = take_row(table, h, pl.program_id(0) + half * pl.num_programs(0))
            lh[0, h : h + 1, first : first + tokens] = row[:, :tokens]
            lh[1, h : h + 1, first : first + tokens] = row[:, tokens:]
    ones = head_masks(1.0)
    scaled = head_masks(HD ** -0.5)
    for j in range(tokens // NARROW):
        rows = slice(NARROW * j, NARROW * j + NARROW)
        window = strip(j, tokens, NARROW)
        q = qh[window]
        do = dh[window]
        k = ko_ref[rows]
        v = vo_ref[rows]
        probs, grads, qs, dos = [], [], [], []
        for h in range(2):
            qm = q * scaled[h]
            dm = do * ones[h]
            st = nt(k, qm) + bh_ref[j]
            pt = jnp.exp(st - lh[0, h : h + 1, window])
            gt = pt * (nt(v, dm) - lh[1, h : h + 1, window])
            probs.append(pt.astype(BF16))
            grads.append(gt.astype(BF16))
            qs.append(qm)
            dos.append(dm)
        dk_ref[rows] = (dkv_in[0, 0, rows] + nn(cat(grads, 1), cat(qs, 0))).astype(BF16)
        dv = (dkv_in[0, 1, rows] + nn(cat(probs, 1), cat(dos, 0))).astype(BF16)
        dv_ref[rows] = dv
        sum_ref[...] = column_sum(dv.astype(F32)) + (sum_ref[...] if j else 0.0)


def halo_grads(mixed, before, after, grad_before, grad_after, bias_halo, dkv, half):
    tokens, width = dkv.shape[2], 2 * dkv.shape[3]
    near = width // PAIR // 2

    def column(part):
        return pl.BlockSpec((tokens, PAIR), lambda p: (0, (half * 3 + part) * near + p))

    whole = lambda shape: pl.BlockSpec(shape, lambda p: (0,) * len(shape))
    both = pl.BlockSpec((1, 2, tokens, PAIR), lambda p: (half, 0, 0, p))
    tables = [pl.BlockSpec((H, width), lambda p, k=k: (tokens // H + k, 0)) for k in range(3)]
    block = pl.BlockSpec((tokens, PAIR), lambda p: (0, half * near + p))
    made = pl.BlockSpec((tokens, PAIR), lambda p: (0, p))
    return pl.pallas_call(
        functools.partial(halo_grad_kernel, half),
        grid=(near,),
        in_specs=[column(1), column(2), column(0), column(0), block, block] + tables + tables + [whole(bias_halo.shape), both],
        out_specs=[made, made, pl.BlockSpec((1, PAIR), lambda p: (0, p))],
        out_shape=[jax.ShapeDtypeStruct((tokens, width // 2), BF16)] * 2 + [jax.ShapeDtypeStruct((1, width // 2), F32)],
        scratch_shapes=[
            pltpu.VMEM((2 * tokens, PAIR), BF16),
            pltpu.VMEM((2 * tokens, PAIR), BF16),
            pltpu.VMEM((2, 2, 2 * tokens), F32),
        ],
        compiler_params=params(),
        cost_estimate=cost(0.05),
        name="halo_grads",
    )(mixed, mixed, before, after, grad_before, grad_after, *[grad_before] * 3, *[grad_after] * 3, bias_halo, dkv)


def mask_biases(segments, place, blocks, tokens):
    line = cat([jnp.full((tokens,), -1, jnp.int32), segments, jnp.full((tokens,), -1, jnp.int32)], 0)
    near = lax.dynamic_slice_in_dim(line, place * tokens, 3 * tokens)
    own = near[tokens : 2 * tokens]
    bias_own = jnp.where(own[:, None] == own[None, :], 0.0, FILL).astype(F32)
    halo = cat([near[:tokens], near[2 * tokens :]], 0)
    at = jnp.arange(tokens, dtype=jnp.int32)
    halo_at = cat([at - tokens, at + tokens], 0)
    allowed = (own[:, None] == halo[None, :]) & (jnp.abs(halo_at[None, :] - at[:, None]) < HALF)
    bias = jnp.where(allowed, 0.0, FILL).astype(F32)
    strips = [jnp.stack([bias[r * i : r * i + r, strip(i, tokens, r)] for i in range(tokens // r)]) for r in (ROWS, NARROW)]
    return bias_own, *strips


def normalized(values):
    average = jnp.mean(values, axis=1, keepdims=True)
    centered = values - average
    spread = jnp.mean(centered * centered, axis=1, keepdims=True)
    inverse = lax.rsqrt(spread + EPS)
    return centered * inverse, inverse


def norm_back(grad, gain, hat, inverse):
    scaled = grad * gain
    return inverse * (
        scaled
        - jnp.mean(scaled, axis=1, keepdims=True)
        - hat * jnp.mean(scaled * hat, axis=1, keepdims=True)
    )


def column_sum(values):
    return jnp.sum(values, axis=0, keepdims=True)


def part_blocks(at_ref, order, second, far):
    for first in range(2):
        rel = {order[-2]: first, order[-1]: second}
        y = jnp.bitwise_xor(at_ref[0], rel["y"])
        x = jnp.bitwise_xor(at_ref[1], rel["x"])
        for i in range(far):
            z = jnp.bitwise_xor(at_ref[3], (i % 2) * 2 + i // 2) if order[0] == "z" else i
            yield first, i, (z * 2 + y) * 2 + x


def start_all(copies):
    for copy in copies:
        copy.start()


def wait_all(copies):
    for copy in copies:
        copy.wait()


def block_place(at_ref, order, z, y, x, far):
    where = {"z": (z, far), "y": (jnp.bitwise_xor(at_ref[0], y), 2), "x": (jnp.bitwise_xor(at_ref[1], x), 2)}
    to = 0
    for axis in order:
        to = to * where[axis][1] + where[axis][0]
    return to


def prepare_kernel(at_ref, qkv_ref, out_ref, up_ref, *refs):
    vectors, mine_ref, send_ref, note_ref = refs[:-3], *refs[-3:]
    width = out_ref.shape[1]
    place = 0
    for ref, piece in ((qkv_ref, width // 2), (out_ref, width // 2), (up_ref, HIDDEN_BLOCK)):
        for i in range(0, ref.shape[1], 2 * piece):
            mine_ref[:, place : place + piece] = ref[:, pl.ds(pl.multiple_of(i + at_ref[2] * piece, piece), piece)]
            send_ref[:, place : place + piece] = ref[:, pl.ds(pl.multiple_of(i + (1 - at_ref[2]) * piece, piece), piece)]
            place += piece
    line = cat([v[...].astype(F32) for v in vectors], 1).astype(BF16)
    note_ref[...] = jnp.zeros_like(note_ref)
    for i in range(line.shape[1] // 128):
        note_ref[i : i + 1] = line[:, i * 128 : i * 128 + 128]


def prepare(at, qkv, out, up, vectors):
    rows = qkv.shape[0]
    columns = (qkv.shape[1] + out.shape[1] + up.shape[1]) // 2
    half = jax.ShapeDtypeStruct((rows, columns), BF16)
    return pl.pallas_call(
        prepare_kernel,
        in_specs=[SMEM] + [VMEM] * (3 + len(vectors)),
        out_shape=[half, half, jax.ShapeDtypeStruct((rows, 128), BF16)],
        compiler_params=params(),
        cost_estimate=cost(0.04),
        name="prepare",
    )(at, qkv, out, up, *[v[None] for v in vectors])


def arrange_kernel(at_ref, mine_ref, got_ref, note_ref, block_ref, up_ref):
    rows, cut = mine_ref.shape[0], block_ref.shape[2] - 128
    block_ref[0, :, cut:] = note_ref[...]
    block_ref[1, :, cut:] = jnp.zeros_like(note_ref)

    def lay(first, second):
        for i, ref in ((0, first), (1, second)):
            block_ref[i, :, :cut] = ref[:, :cut]
            up_ref[i * rows : i * rows + rows] = ref[:, cut:]

    @pl.when(at_ref[2] == 0)
    def _():
        lay(mine_ref, got_ref)

    @pl.when(at_ref[2] != 0)
    def _():
        lay(got_ref, mine_ref)


def arrange(at, mine, got, note, hidden):
    rows, columns = mine.shape
    return pl.pallas_call(
        arrange_kernel,
        in_specs=[SMEM] + [VMEM] * 3,
        out_shape=[
            jax.ShapeDtypeStruct((2, rows, columns - hidden // 2 + 128), BF16),
            jax.ShapeDtypeStruct((2 * rows, hidden // 2), BF16),
        ],
        compiler_params=params(),
        cost_estimate=cost(0.04),
        name="arrange",
    )(at, mine, got, note)


def first_copies(refs, qkv, out, sems, at_ref, far):
    width, columns = qkv.shape
    half, near = width // 2, columns // 2
    copies = []

    def add(source, target):
        copies.append(pltpu.make_async_copy(source, target, sems.at[len(copies)]))

    def column(core):
        return pl.ds(pl.multiple_of(jnp.bitwise_xor(at_ref[2], core) * half, half), half)

    for core in range(2):
        if far is None:
            add(refs[core], qkv.at[:, pl.ds(core * near, near)])
            for part in range(2):
                row = pl.ds(pl.multiple_of(jnp.bitwise_xor(at_ref[2], part) * half, half), half)
                add(refs[2 + core].at[pl.ds(part * half, half)], out.at[row, column(core)])
            continue
        rows = width // (8 * far)
        for color, order in enumerate(("zyx", "zxy")):
            for second in range(2):
                ref = refs[core * 4 + color * 2 + second]
                for first, z, block in part_blocks(at_ref, order, second, far):
                    row = (block * 2 + color) * rows
                    add(ref.at[first, z, :, pl.ds(0, near)], qkv.at[pl.ds(pl.multiple_of(row, rows), rows), pl.ds(core * near, near)])
                    row = jnp.bitwise_xor(row, at_ref[2] * half)
                    add(ref.at[first, z, :, pl.ds(near, half)], out.at[pl.ds(pl.multiple_of(row, rows), rows), column(core)])
    return copies


def project_kernel(far, parts, *refs):
    at_ref, refs = refs[0], refs[1:]
    part_refs, refs = refs[:parts], refs[parts:]
    own_ref, row_ref, own_out, qkv_out, out_out, qkv, out, sems, out_sems = refs
    copies = first_copies(part_refs, qkv, out, sems, at_ref, far)
    start_all(copies)
    wait_all(copies)
    keep = [pltpu.make_async_copy(qkv, qkv_out, out_sems.at[0]), pltpu.make_async_copy(out, out_out, out_sems.at[1])]
    start_all(keep)
    chunk = 512

    def body(j, carry):
        cols = pl.ds(pl.multiple_of(j * chunk, chunk), chunk)
        own_out[:, cols] = (nn(own_ref[...], qkv[:, cols]) + row_ref[:, cols]).astype(BF16)
        return carry

    lax.fori_loop(0, qkv.shape[1] // chunk, body, 0)
    wait_all(keep)


def copy_count(far, each):
    return 2 if far is None else 8 * far * each


def project(far, at, parts, x, row):
    tokens, width = x.shape
    columns = row.shape[1]
    mixed = jax.ShapeDtypeStruct((tokens, columns), BF16)
    return pl.pallas_call(
        functools.partial(project_kernel, far, len(parts)),
        in_specs=[SMEM] + [ANY] * len(parts) + [VMEM] * 2,
        out_specs=[VMEM, ANY, ANY],
        out_shape=[mixed, jax.ShapeDtypeStruct((width, columns), BF16), jax.ShapeDtypeStruct((width, width), BF16)],
        scratch_shapes=[
            pltpu.VMEM((width, columns), BF16),
            pltpu.VMEM((width, width), BF16),
            pltpu.SemaphoreType.DMA((6 if far is None else 64 * far,)),
            pltpu.SemaphoreType.DMA((2,)),
        ],
        compiler_params=params(),
        cost_estimate=cost(0.26),
        name="project",
    )(at, *parts, x, row)


def project_more_kernel(before_ref, after_ref, w_ref, row_ref, before_out, after_out):
    for source, target in ((before_ref, before_out), (after_ref, after_out)):
        target[...] = (nn(source[...], w_ref[...]) + row_ref[...]).astype(BF16)


def project_more(before, after, full, row, chunk=512):
    tokens, width = before.shape
    columns = full.shape[1]
    whole = pl.BlockSpec((tokens, width), lambda i: (0, 0))
    block = pl.BlockSpec((tokens, chunk), lambda i: (0, i))
    return pl.pallas_call(
        project_more_kernel,
        grid=(columns // chunk,),
        in_specs=[whole, whole, pl.BlockSpec((width, chunk), lambda i: (0, i)), pl.BlockSpec((1, chunk), lambda i: (0, i))],
        out_specs=[block, block],
        out_shape=[jax.ShapeDtypeStruct((tokens, columns), BF16)] * 2,
        compiler_params=params(),
        cost_estimate=cost(0.214),
        name="project_more",
    )(before, after, full, row)


def out_kernel(heads_ref, w_ref, x_ref, vec_ref, hat_ref, inv_ref, low_ref):
    branch = nn(heads_ref[...], w_ref[...]) + vec_ref[0:1]
    hat, inverse = normalized(x_ref[...].astype(F32) + branch)
    hat_ref[...] = hat
    inv_ref[...] = inverse
    low_ref[...] = (hat * vec_ref[1:2] + vec_ref[2:3]).astype(BF16)


def out_project(heads, out_full, x, vectors):
    tokens, width = heads.shape
    rows = tokens // 2
    block = pl.BlockSpec((rows, width), lambda i: (i, 0))
    return pl.pallas_call(
        out_kernel,
        grid=(2,),
        in_specs=[block, pl.BlockSpec(out_full.shape, lambda i: (0, 0)), block, pl.BlockSpec(vectors.shape, lambda i: (0, 0))],
        out_specs=[block, pl.BlockSpec((rows, 1), lambda i: (i, 0)), block],
        out_shape=[
            jax.ShapeDtypeStruct((tokens, width), F32),
            jax.ShapeDtypeStruct((tokens, 1), F32),
            jax.ShapeDtypeStruct((tokens, width), BF16),
        ],
        compiler_params=params(),
        cost_estimate=cost(0.114),
        name="out_project",
    )(heads, out_full, x, vectors)


def up_copies(refs, full, sems, at_ref, far):
    width, half = full.shape[0], full.shape[1] // 2
    copies = []
    for core in range(2):
        cols = pl.ds(core * half, half)
        if far is None:
            copies.append(pltpu.make_async_copy(refs[core], full.at[:, cols], sems.at[core]))
            continue
        rows = width // (4 * far)
        for second in range(2):
            ref = refs[core * 2 + second]
            for first, z, block in part_blocks(at_ref, "zyx", second, far):
                to = full.at[pl.ds(pl.multiple_of(block * rows, rows), rows), cols]
                copies.append(pltpu.make_async_copy(ref.at[first, z], to, sems.at[len(copies)]))
    return copies


def down_copies(refs, full, sems, at_ref, far):
    half = full.shape[0] // 2
    copies = []
    for core in range(2):
        if far is None:
            copies.append(pltpu.make_async_copy(refs[core], full.at[pl.ds(core * half, half)], sems.at[core]))
            continue
        rows = half // (4 * far)
        for second in range(2):
            ref = refs[core * 2 + second]
            for first, z, block in part_blocks(at_ref, "xy", second, far):
                to = full.at[pl.ds(pl.multiple_of(core * half + block * rows, rows), rows)]
                copies.append(pltpu.make_async_copy(ref.at[first, z], to, sems.at[len(copies)]))
    return copies


def middle_kernel(far, ups, downs, *refs):
    at_ref, refs = refs[0], refs[1:]
    up_refs, down_refs, refs = refs[:ups], refs[ups : ups + downs], refs[ups + downs :]
    low_ref, row_ref, vec_ref, log_ref, inv_ref, hat_in, dy_in, heads_in, out_in = refs[:9]
    act_out, act_send, result_out, glow_out, lift_out, lift_send, one_out, mine_out, send_out, pay_out, mean_ref, row_sums, two_sums, one_sums = refs[9:23]
    up, down, out, hat, dy, heads, act, slope, result, glow, total, branch, sides, payload, up_sems, down_sems, in_sems, out_sems = refs[23:]
    tokens, width = low_ref.shape
    half = up.shape[1] // 2
    chunk = half
    from_up = up_copies(up_refs, up, up_sems, at_ref, far)
    from_down = down_copies(down_refs, down, down_sems, at_ref, far)
    loads = [pltpu.make_async_copy(*pair, in_sems.at[i]) for i, pair in enumerate(((hat_in, hat), (dy_in, dy), (out_in, out), (heads_in, heads)))]
    start_all(from_up)
    start_all(from_down)
    start_all(loads)
    stores = []

    def store(source, target):
        copy = pltpu.make_async_copy(source, target, out_sems.at[len(stores)])
        stores.append(copy)
        copy.start()

    def cols(i):
        return slice(i * chunk, i * chunk + chunk)

    def raise_one(i):
        lifted = nn(low_ref[...], up[:, cols(i)]) + row_ref[:, cols(i)]
        phi = 0.5 * (1.0 + lax.erf(lifted * (0.5 ** 0.5)))
        density = jnp.exp(lifted * lifted * -0.5) * 0.3989422804014327
        act[:, cols(i)] = (lifted * phi).astype(BF16)
        slope[:, cols(i)] = (phi + lifted * density).astype(BF16)

    def settle_one(i):
        total[...] += nn(act[:, cols(i)], down[cols(i)])

    half_up, half_down = len(from_up) // 2, len(from_down) // 2
    wait_all(from_up[:half_up])
    raise_one(0)
    wait_all(from_up[half_up:])
    wait_all(from_down[:half_down])
    raise_one(1)
    total[...] = nn(act[:, cols(0)], down[cols(0)])
    wait_all(from_down[half_down:])
    settle_one(1)
    store(act.at[:, pl.ds(0, half)], act_out)
    store(act.at[:, pl.ds(half, half)], act_send)
    wait_all(loads)

    rows = 128
    for n in range(tokens // rows):
        at = slice(rows * n, rows * n + rows)
        first = hat[at] * vec_ref[3:4] + vec_ref[4:5]
        hat_two, inverse = normalized(first + (total[at] + vec_ref[0:1]))
        result[at] = (hat_two * vec_ref[1:2] + vec_ref[2:3]).astype(BF16)
        grad = dy[at].astype(F32)
        part = [column_sum(grad * hat_two), column_sum(grad)]
        grad = norm_back(grad, vec_ref[1:2], hat_two, inverse)
        low = grad.astype(BF16)
        total[at] = grad
        glow[at] = low
        part = cat(part + [column_sum(low.astype(F32))], 0)
        two_sums[...] = part if n == 0 else two_sums[...] + part
    store(result, result_out)
    store(glow, glow_out)

    def lower_one(i):
        value = (nt(glow[...], down[cols(i)]) * slope[:, cols(i)].astype(F32)).astype(BF16)
        slope[:, cols(i)] = value
        row_sums[:, cols(i)] = column_sum(value.astype(F32))

    def first_one(i):
        total[...] += nt(slope[:, cols(i)], up[:, cols(i)])

    lower_one(0)
    store(slope.at[:, pl.ds(0, half)], lift_out)
    lower_one(1)
    store(slope.at[:, pl.ds(half, half)], lift_send)
    first_one(0)
    first_one(1)

    for n in range(tokens // rows):
        at = slice(rows * n, rows * n + rows)
        grad = total[at]
        one = norm_back(grad, vec_ref[3:4], hat[at], inv_ref[at])
        low = one.astype(BF16)
        total[at] = one
        branch[at] = low
        part = cat([column_sum(grad * hat[at]), column_sum(grad), column_sum(low.astype(F32))], 0)
        one_sums[...] = part if n == 0 else one_sums[...] + part
    store(total, one_out)
    middle = width // 2
    for n in range(2):
        side = pl.multiple_of(jnp.bitwise_xor(at_ref[2], n) * middle, middle)
        sides[n] = branch[:, pl.ds(side, middle)]
    store(sides.at[0], mine_out)
    store(sides.at[1], send_out)

    head = lax.broadcasted_iota(jnp.int32, (H, width), 1) // HD
    pick = jnp.where(head == lax.broadcasted_iota(jnp.int32, (H, width), 0), 1.0, 0.0).astype(F32)
    for n in range(4):
        part = slice(width // 4 * n, width // 4 * (n + 1))
        grad = nt(branch[...], out[part]).astype(BF16)
        payload[:tokens, part] = grad
        product = grad.astype(F32) * heads[:, part].astype(F32)
        means = lax.dot_general(
            pick[:, part], product, (((1,), (1,)), ((), ())), precision=lax.Precision.HIGHEST, preferred_element_type=F32
        )
        mean_ref[...] = means if n == 0 else mean_ref[...] + means
    rest = cat([log_ref[...], mean_ref[...]], 1)
    for n in range(3):
        term = rest.astype(BF16)
        rest = rest - term.astype(F32)
        payload[tokens + H * n : tokens + H * n + H] = term
    store(payload, pay_out)
    wait_all(stores)


def middle(far, at, up_parts, down_parts, low, row, vectors, logs, inverse, hat, dy, heads, out_full):
    tokens, width = low.shape
    hidden = row.shape[1]
    half = hidden // 2
    shape = jax.ShapeDtypeStruct
    pay_shape = (tokens + 3 * H, width)
    return pl.pallas_call(
        functools.partial(middle_kernel, far, len(up_parts), len(down_parts)),
        in_specs=[SMEM] + [ANY] * (len(up_parts) + len(down_parts)) + [VMEM] * 5 + [ANY] * 4,
        out_specs=[ANY] * 10 + [VMEM] * 4,
        out_shape=[
            shape((tokens, half), BF16),
            shape((tokens, half), BF16),
            shape((tokens, width), BF16),
            shape((tokens, width), BF16),
            shape((tokens, half), BF16),
            shape((tokens, half), BF16),
            shape((tokens, width), F32),
            shape((tokens, width // 2), BF16),
            shape((tokens, width // 2), BF16),
            shape(pay_shape, BF16),
            shape((H, tokens), F32),
            shape((1, hidden), F32),
            shape((3, width), F32),
            shape((3, width), F32),
        ],
        scratch_shapes=[
            pltpu.VMEM((width, hidden), BF16),
            pltpu.VMEM((hidden, width), BF16),
            pltpu.VMEM((width, width), BF16),
            pltpu.VMEM((tokens, width), F32),
            pltpu.VMEM((tokens, width), BF16),
            pltpu.VMEM((tokens, width), BF16),
            pltpu.VMEM((tokens, hidden), BF16),
            pltpu.VMEM((tokens, hidden), BF16),
            pltpu.VMEM((tokens, width), BF16),
            pltpu.VMEM((tokens, width), BF16),
            pltpu.VMEM((tokens, width), F32),
            pltpu.VMEM((tokens, width), BF16),
            pltpu.VMEM((2, tokens, width // 2), BF16),
            pltpu.VMEM(pay_shape, BF16),
            pltpu.SemaphoreType.DMA((copy_count(far, 2),)),
            pltpu.SemaphoreType.DMA((copy_count(far, 2),)),
            pltpu.SemaphoreType.DMA((4,)),
            pltpu.SemaphoreType.DMA((10,)),
        ],
        compiler_params=params(),
        cost_estimate=cost(45),
        name="middle",
    )(at, *up_parts, *down_parts, low, row, vectors, logs, inverse, hat, dy, heads, out_full)


def down_grad_kernel(far, at_ref, act_ref, act_got, glow_ref, glow_got, dw_ref, glows):
    tokens = glow_ref.shape[0]

    @pl.when(pl.program_id(0) == 0)
    def _():
        glows[:tokens] = glow_ref[...]
        glows[tokens:] = glow_got[...]

    dw = tn(cat([act_ref[...], act_got[...]], 0), glows[...]).astype(BF16)
    if far is None:
        dw_ref[...] = dw
        return
    rows = dw.shape[0] // 4
    for j in range(4):
        to = block_place(at_ref, "yx", 0, j // 2, j % 2, far)
        dw_ref[pl.ds(pl.multiple_of(to * rows, rows), rows)] = dw[j * rows : j * rows + rows]


def down_grads(far, at, active, act_got, glow, glow_got):
    tokens, half = active.shape
    width = glow.shape[1]
    chunk = half // 4
    whole = pl.BlockSpec((tokens, width), lambda i: (0, 0))
    block = pl.BlockSpec((tokens, chunk), lambda i: (0, i))
    return pl.pallas_call(
        functools.partial(down_grad_kernel, far),
        grid=(4,),
        in_specs=[SMEM, block, block, whole, whole],
        out_specs=pl.BlockSpec((chunk, width), lambda i: (i, 0)),
        out_shape=jax.ShapeDtypeStruct((half, width), BF16),
        scratch_shapes=[pltpu.VMEM((2 * tokens, width), BF16)],
        compiler_params=params(),
        cost_estimate=cost(8.5),
        name="down_grads",
    )(at, active, act_got, glow, glow_got)


def both_flipped(at_ref, mine_ref, got_ref, flipped, far, heads=False, distant=False):
    tokens = mine_ref.shape[0]
    for core, ref in ((0, mine_ref), (1, got_ref)):
        turned = ref[...].T
        cols = slice(core * tokens, core * tokens + tokens)
        flip = jnp.bitwise_xor(at_ref[2], core) if heads else 0
        half = turned.shape[0] // 2
        if far is None:
            for part in range(2):
                to = jnp.bitwise_xor(flip, part) * half
                flipped[pl.ds(pl.multiple_of(to, half), half), cols] = turned[part * half : part * half + half]
            continue
        rows = turned.shape[0] // (8 * far)
        for z in range(far):
            at_z = jnp.bitwise_xor(z, flip * (far // 2))
            if distant:
                away = jnp.bitwise_xor(at_z, at_ref[3])
                at_z = away % 2 * 2 + away // 2
            for y in range(2):
                for x in range(2):
                    a = ((z * 2 + y) * 2 + x) * 2 * rows
                    to_y, to_x = jnp.bitwise_xor(at_ref[0], y), jnp.bitwise_xor(at_ref[1], x)
                    first = ((1 - to_x) * 2 + to_y) * far + at_z
                    second = ((3 - to_y) * 2 + to_x) * far + at_z
                    for i, to in enumerate((first, second)):
                        to = pl.ds(pl.multiple_of(to * rows, rows), rows)
                        flipped[to, cols] = turned[a + i * rows : a + i * rows + rows]


def quarter_specs(rows, columns, index):
    return [pl.BlockSpec((rows // 4, columns), index)] * 4


def put_quarters(refs, cols, value):
    rows = value.shape[0] // 4
    for i, ref in enumerate(refs):
        ref[:, cols] = value[i * rows : i * rows + rows]


def late_grad_kernel(far, at_ref, low_ref, low_got, heads_ref, heads_got, lift_ref, lift_got, branch_ref, branch_got, *refs):
    quarters, flipped = refs[:4], refs[4]
    step = pl.program_id(0)
    last = pl.num_programs(0) - 1

    @pl.when(step == 0)
    def _():
        both_flipped(at_ref, low_ref, low_got, flipped, far, distant=True)

    @pl.when(step < last)
    def _():
        put_quarters(quarters, slice(None), nn(flipped[...], cat([lift_ref[...], lift_got[...]], 0)).astype(BF16))

    @pl.when(step == last)
    def _():
        both_flipped(at_ref, heads_ref, heads_got, flipped, far, heads=True, distant=True)
        put_quarters(quarters, slice(None), nn(flipped[...], cat([branch_ref[...], branch_got[...]], 0)).astype(BF16))


def late_grads(far, at, low, low_got, heads, heads_got, lift, lift_got, branch, branch_got):
    tokens, width = low.shape
    chunk = branch.shape[1]
    steps = lift.shape[1] // chunk
    whole = lambda shape: pl.BlockSpec(shape, lambda i: (0, 0))
    block = pl.BlockSpec((tokens, chunk), lambda i: (0, jnp.minimum(i, steps - 1)))
    return pl.pallas_call(
        functools.partial(late_grad_kernel, far),
        grid=(steps + 1,),
        in_specs=[SMEM] + [whole((tokens, width))] * 4 + [block, block] + [whole((tokens, chunk))] * 2,
        out_specs=quarter_specs(width, chunk, lambda i: (0, i)),
        out_shape=[jax.ShapeDtypeStruct((width // 4, (steps + 1) * chunk), BF16)] * 4,
        scratch_shapes=[pltpu.VMEM((width, 2 * tokens), BF16)],
        compiler_params=params(),
        cost_estimate=cost(9),
        name="late_grads",
    )(at, low, low_got, heads, heads_got, lift, lift_got, branch, branch_got)


def qkv_grad_kernel(far, at_ref, x_ref, x_got, *refs):
    keeps, gots, refs = refs[:3], refs[3:6], refs[6:]
    note_refs, quarters, flipped = refs[:-5], refs[-5:-1], refs[-1]
    both_flipped(at_ref, x_ref, x_got, flipped, far)
    chunk = keeps[0].shape[1]
    for n in range(3):
        dw = nn(flipped[...], cat([keeps[n][...], gots[n][...]], 0)).astype(BF16)
        put_quarters(quarters, slice(n * chunk, n * chunk + chunk), dw)
    for ref in note_refs:
        put_quarters(quarters, slice(3 * chunk, 3 * chunk + ref.shape[1]), ref[...])


def qkv_grads(far, at, x, x_got, keep, got, notes=()):
    tokens, width = x.shape
    columns = 3 * keep[0].shape[1] + sum(v.shape[1] for v in notes)
    return pl.pallas_call(
        functools.partial(qkv_grad_kernel, far),
        in_specs=[SMEM] + [VMEM] * (8 + len(notes)),
        out_shape=[jax.ShapeDtypeStruct((width // 4, columns), BF16)] * 4,
        scratch_shapes=[pltpu.VMEM((width, 2 * tokens), BF16)],
        compiler_params=params(),
        cost_estimate=cost(8.3),
        name="qkv_grads",
    )(at, x, x_got, *keep, *got, *notes)


FAR, Y, X, CORE = "far", "y", "x", "fsdp"
CTX = (FAR, Y, X)
ALL = CTX + (CORE,)


def swap(values, axis):
    return lax.ppermute(values, axis, [(0, 1), (1, 0)])


def swap_both(values):
    return lax.ppermute(values, (Y, X), [(i, 3 - i) for i in range(4)])


def swap_far(values, step):
    return lax.ppermute(values, FAR, [(i, i ^ step) for i in range(lax.axis_size(FAR))])


def together(*arrays):
    return lax.optimization_barrier(arrays)


def choose(core, left, right):
    return jnp.where(core == 0, left, right), jnp.where(core == 0, right, left)


def added(*terms):
    total = terms[0].astype(F32)
    for term in terms[1:]:
        total = total + term.astype(F32)
    return total.astype(BF16)


def own_rows(core, summed):
    mine, send = choose(core, summed[0], summed[1])
    return choose(core, mine, swap(send, CORE))


def color_nexts(keep_x, keep_y, there_x, there_y):
    return added(keep_x[1], there_x[1]), added(keep_y[1], there_y[1])


def color_sums(keep_x, keep_y, there_x, there_y, there_xy, there_yx):
    return jnp.stack([added(keep_x[0], there_x[0], there_xy), added(keep_y[0], there_y[0], there_yx)], 1)


def shards(inputs, segments, cotangent, qkv_weight, query_bias, value_bias, out_weight, out_bias, first_gain, first_shift, up_weight, up_bias, down_weight, down_bias, second_gain, second_shift):
    tokens, width = inputs.shape[1:]
    rows, hidden = up_weight.shape
    piece = down_weight.shape[0]
    near = width // 2
    blocks = lax.axis_size(CTX)
    place = lax.axis_index(CTX)
    core = lax.axis_index(CORE)
    at = jnp.stack([lax.axis_index(Y), lax.axis_index(X), core, lax.axis_index(FAR)]).astype(jnp.int32)
    far = 4 if rows % 32 == 0 and lax.axis_size(FAR) == 4 and piece == HIDDEN_BLOCK else None
    onward = [(i, i + 1) for i in range(blocks - 1)]
    back = [(i + 1, i) for i in range(blocks - 1)]

    def from_before(v):
        return lax.ppermute(v, CTX, onward)

    def from_after(v):
        return lax.ppermute(v, CTX, back)

    def own_first(v):
        return cat(choose(core, v[:, :near], v[:, near:]), 1)

    x = inputs[0]
    vectors = (query_bias, value_bias, out_bias, first_gain, first_shift, down_bias, second_gain, second_shift, up_bias)
    each = query_bias.shape[0]
    if far is None:
        split = lambda w, size: w.reshape(rows, -1, 2, size).swapaxes(0, 2).swapaxes(1, 2).reshape(2, rows, -1)
        sides = cat([split(qkv_weight, near), split(out_weight, near), split(up_weight, piece)], 2)
        mine, send = choose(core, sides[0], sides[1])
        both = cat(choose(core, mine, swap(send, CORE)), 0)
        whole = lambda v: lax.all_gather(v, CTX, axis=0, tiled=True)
        pair = lambda v: [v, swap(v, CORE)]
        qkv_parts = pair(whole(both[:, : 3 * near])) + pair(whole(both[:, 3 * near : 4 * near]))
        up_parts, down_parts = pair(whole(both[:, 4 * near :])), pair(whole(down_weight))
        x_before, x_after = from_before(x), from_after(x)
        table = lax.all_gather(cat(vectors, 0)[None], ALL, axis=0, tiled=True)
    else:
        mine, send, note = prepare(at, qkv_weight, out_weight, up_weight, vectors)
        block, up_block = arrange(at, mine, swap(send, CORE), note, hidden)
        cut = 4 * near
        lines = sum(v.shape[0] for v in vectors) // 128
        pair = jnp.stack([block, swap_far(block, 2)])
        down_pair = jnp.stack([down_weight, swap(down_weight, X)])
        pair, x_before, x_two = together(pair, from_before(x), x)
        wide = jnp.stack([pair, swap_far(pair, 1)]).reshape((4,) + block.shape)
        x_after = from_after(x_two)
        wide, up_block, down_pair, x_after = together(wide, up_block, down_pair, x_after)
        a1, b1, up_hi = swap(wide[:, 0], Y), swap(wide[:, 1], X), swap_far(up_block, 2)
        a1, b1, up_hi = together(a1, b1, up_hi)
        pair_a, pair_b, up_pair = jnp.stack([wide[:, 0], a1]), jnp.stack([wide[:, 1], b1]), jnp.stack([up_block, up_hi])
        a2, b2, up_lo = swap(pair_a, X), swap(pair_b, Y), swap_far(up_pair, 1)
        up_lo, down_pair = together(up_lo, down_pair)
        down_wide = lax.all_gather(down_pair, FAR, axis=1)
        a2, b2, up_lo = together(a2, b2, up_lo)
        first_parts = [pair_a, a2, pair_b, b2]
        qkv_parts = first_parts + [swap(p, CORE) for p in first_parts]
        up_wide = jnp.stack([up_pair, up_lo]).reshape((4,) + up_block.shape)
        up_y = swap(up_wide, Y)
        notes = jnp.stack([jnp.stack([qkv_parts[4 * c + s][:, :, :lines, cut:] for s in range(2)]) for c in range(2)])
        notes = notes.reshape(2, 2, 2, 2, 2, -1).swapaxes(3, 4)
        for axis, index in ((0, core), (1, at[1]), (2, at[0]), (3, at[3] // 2), (4, at[3] % 2)):
            notes = jnp.where(index == 0, notes, jnp.flip(notes, axis))
        table = notes.transpose(3, 4, 2, 1, 0, 5).reshape(2 * blocks, -1)

    rows_of = [table[:, each * i : each * i + each].reshape(1, width).astype(F32) for i in range(8)]
    query_row, value_row, out_row, gain_one, shift_one, down_row, gain_two, shift_two = rows_of
    up_row = table[:, 8 * each :].reshape(blocks, 2, piece).astype(F32)
    up_row = cat(choose(core, up_row[:, 0].reshape(1, -1), up_row[:, 1].reshape(1, -1)), 1)
    bias_own, bias_halo, bias_narrow = mask_biases(segments[0], place, blocks, tokens)
    query_row, value_row, gap = own_first(query_row), own_first(value_row), jnp.zeros((1, near), F32)
    qkv_row = cat([query_row[:, :near], gap, value_row[:, :near], query_row[:, near:], gap, value_row[:, near:]], 1)

    mixed, qkv_full, out_full = project(far, at, qkv_parts, x, qkv_row)
    if far is not None:
        qkv_full, up_y = together(qkv_full, up_y)
        up_pair = jnp.stack([up_wide, up_y])
        up_x, up_pair_core = swap(up_pair, X), swap(up_pair, CORE)
    before, after = project_more(x_before, x_after, qkv_full, qkv_row)
    if far is not None:
        before, down_wide = together(before, down_wide)
        down_y, down_wide_core = swap(down_wide, Y), swap(down_wide, CORE)
    heads, logs = attend(mixed, before, after, bias_own, bias_halo)
    hat, inverse, low = out_project(heads, out_full, x, cat([out_row, gain_one, shift_one], 0))
    low, x_got, heads_got = together(low, swap(x, CORE), swap(heads, CORE))
    if far is not None:
        low, up_x, up_pair_core, down_wide_core, down_y = together(low, up_x, up_pair_core, down_wide_core, down_y)
        up_parts = [up_pair, up_x, up_pair_core, swap(up_x, CORE)]
        down_parts = [down_wide, down_y, down_wide_core, swap(down_y, CORE)]
    low_got = swap(low, CORE)
    (
        active, act_send, result, glow, lift_keep, lift_send, grad_one, branch_mine, branch_send, payload, means, up_bias_part, sums_two, sums_one,
    ) = middle(
        far, at, up_parts, down_parts, low, up_row, cat([down_row, gain_two, shift_two, gain_one, shift_one], 0),
        logs, inverse, hat, cotangent[0], heads, out_full,
    )
    payload, low_got = together(payload, low_got)
    pay_before, pay_after = from_before(payload), from_after(payload)
    act_got, glow_got, lift_got, branch_got = swap(act_send, CORE), swap(glow, CORE), swap(lift_send, CORE), swap(branch_send, CORE)
    down_part = down_grads(far, at, active, act_got, glow, glow_got)
    late = late_grads(far, at, low, low_got, heads, heads_got, lift_keep, lift_got, branch_mine, branch_got)
    dq_keep, dq_send, dkv, dq_sum = own_grads(mixed, before, after, payload, logs, means, bias_own, bias_halo)
    if far is not None:
        down_part = lax.psum_scatter(down_part.reshape(far, 2, 2, piece, width), FAR, scatter_dimension=0, tiled=False)
        by = lambda parts: [v.reshape(2, far, rows, v.shape[1]) for v in parts]
        late_send_x, late_keep_x, late_send_y, late_keep_y = by(late)
        late_x, late_y, pay_before, pay_after, dkv = together(late_send_x, late_send_y, pay_before, pay_after, dkv)
        late_x, late_y = swap(late_x, X), swap(late_y, Y)
    *send, sum_send = halo_grads(mixed, before, after, pay_before, pay_after, bias_narrow, dkv, 1)
    send = [dq_send] + send
    *keep, sum_keep = halo_grads(mixed, before, after, pay_before, pay_after, bias_narrow, dkv, 0)
    if far is not None:
        late_x, late_y, sum_keep = together(late_x, late_y, sum_keep)
    keep, dv_sum = [dq_keep] + keep, cat([sum_keep, sum_send], 1)
    got = [swap(v, CORE) for v in send]
    if far is not None:
        late_xy, late_yx = color_nexts(late_keep_x, late_keep_y, late_x, late_y)
        late_xy, late_yx, *got = together(late_xy, late_yx, *got)
        late_xy, late_yx = swap(late_xy, Y), swap(late_yx, X)
    features = (own_first(dq_sum), own_first(dv_sum), sums_one[2], sums_one[0], sums_one[1], sums_two[2], sums_two[0], sums_two[1])
    small = jnp.stack([v.reshape(blocks, 2, each) for v in features], 2).reshape(blocks, 2, -1)
    sides = choose(core, up_bias_part[:, : hidden // 2], up_bias_part[:, hidden // 2 :])
    small = cat([small, jnp.stack([v.reshape(blocks, piece) for v in sides], 1)], 2)
    if far is None:
        qkv = qkv_grads(far, at, x, x_got, keep, got)
        total = lambda v: lax.psum_scatter(v, CTX, scatter_dimension=0, tiled=True)
        down_sum = total(down_part).astype(F32)
        small_sum = lax.psum_scatter(small.reshape(2 * blocks, -1), ALL, scatter_dimension=0, tiled=True)[0]
        late_sum, qkv_sum = [total(cat(v, 0)).reshape(2, rows, -1) for v in (late, qkv)]
    else:
        small = small.astype(BF16).reshape(far, 2, 2, 2, lines, 128).transpose(3, 2, 1, 0, 4, 5)
        for axis, index in ((1, at[1]), (2, at[0])):
            small = jnp.where(index == 0, small, jnp.flip(small, axis))
        small = jnp.stack([jnp.flip(small[0], 0), jnp.flip(small[1].swapaxes(0, 1), 0)])
        small = small.reshape(8 * far, lines, 128)
        note = jnp.zeros((8 * far, rows, 128), BF16).at[:, :lines].set(small).reshape(width, 128)
        qkv_send_x, qkv_keep_x, qkv_send_y, qkv_keep_y = by(qkv_grads(far, at, x, x_got, keep, got, (note,)))
        qkv_send_x, qkv_send_y, late_xy, late_yx = together(qkv_send_x, qkv_send_y, late_xy, late_yx)
        qkv_x, qkv_y = swap(qkv_send_x, X), swap(qkv_send_y, Y)
        late_sum = color_sums(late_keep_x, late_keep_y, late_x, late_y, late_xy, late_yx)
        late_lo = swap_far(late_sum[2:], 1)
        qkv_x, qkv_y, down_part = together(qkv_x, qkv_y, down_part)
        qkv_xy, qkv_yx = color_nexts(qkv_keep_x, qkv_keep_y, qkv_x, qkv_y)
        qkv_xy, qkv_yx, down_part, *both = together(qkv_xy, qkv_yx, down_part, *keep, *send)
        keep, send = both[:3], both[3:]
        qkv_xy, qkv_yx = swap(qkv_xy, Y), swap(qkv_yx, X)
        down_y, down_x, down_xy = swap(down_part[1, 0], Y), swap(down_part[0, 1], X), swap_both(down_part[1, 1])
        qkv_xy, qkv_yx, late_lo = together(qkv_xy, qkv_yx, late_lo)
        qkv_sum = color_sums(qkv_keep_x, qkv_keep_y, qkv_x, qkv_y, qkv_xy, qkv_yx)
        qkv_sum, late_sum = together(qkv_sum, added(late_sum[:2], late_lo))
        qkv_sum = lax.psum_scatter(qkv_sum, FAR, scatter_dimension=0, tiled=False)
        late_sum = added(late_sum[0], swap_far(late_sum[1], 2))
        late_sum, down_y, down_x, down_xy = together(late_sum, down_y, down_x, down_xy)
        down_sum = down_part[0, 0].astype(F32) + down_y.astype(F32) + down_x.astype(F32) + down_xy.astype(F32)
    inputs_grad = nt(cat([*keep, *send], 1), qkv_full)
    inputs_grad = (grad_one + inputs_grad).astype(BF16)[None]
    wide = hidden // 2
    left, right = own_rows(core, late_sum)
    up_sum = jnp.stack([v[:, :wide].reshape(rows, blocks, piece) for v in (left, right)], 2).reshape(rows, hidden).astype(F32)
    out_sum = cat([left[:, wide:], right[:, wide:]], 1).astype(F32)
    mine, send = choose(core, qkv_sum[0], qkv_sum[1])
    got = swap(send, CORE)
    left, right = choose(core, mine[:, : 3 * near], got[:, : 3 * near])
    if far is not None:
        small_sum = (mine[:lines, 3 * near :].astype(F32) + got[:lines, 3 * near :].astype(F32)).reshape(-1)
    qkv_sum = jnp.stack([v.reshape(rows, 3, near) for v in (left, right)], 2).reshape(rows, 3 * width).astype(F32)
    s = [small_sum[each * i : each * i + each] for i in range(8)]
    return (
        result[None], inputs_grad, qkv_sum, s[0], s[1], out_sum, s[2], s[3], s[4], up_sum, small_sum[8 * each :], down_sum, s[5], s[6], s[7],
    )


def solution(mesh):
    devices = mesh.devices
    split = jax.sharding.Mesh(devices.reshape(devices.shape[0] // 4, 2, 2, devices.shape[1]), ALL)
    rows, vec = P(ALL, None), P(ALL)
    tokens = P(CORE, CTX, None)
    return jax.shard_map(
        shards,
        mesh=split,
        in_specs=(tokens, P(CORE, None), tokens, rows, vec, vec, rows, vec, vec, vec, rows, vec, rows, vec, vec, vec),
        out_specs=(tokens, tokens, rows, vec, vec, rows, vec, vec, vec, rows, vec, rows, vec, vec, vec),
        check_vma=False,
    )
```

```python
import functools

import jax
import jax.numpy as jnp
from jax import lax
from jax.experimental import pallas as pl
from jax.experimental.pallas import tpu as pltpu
from jax.sharding import PartitionSpec as P

H = 16
HD = 64
WINDOW = 1024
HALF = WINDOW // 2
ROWS = 256
NARROW = 128
PAIR = 2 * HD
FILL = -1e30
EPS = 1e-05
HIDDEN_BLOCK = 128
F32 = jnp.float32
BF16 = jnp.bfloat16
VMEM_BYTES = 56 * 1024 * 1024
SMEM = pl.BlockSpec(memory_space=pltpu.SMEM)
ANY = pl.BlockSpec(memory_space=pl.ANY)
VMEM = pl.BlockSpec(memory_space=pltpu.VMEM)


def nn(a, b):
    return lax.dot_general(a, b, (((1,), (0,)), ((), ())), preferred_element_type=F32)


def nt(a, b):
    return lax.dot_general(a, b, (((1,), (1,)), ((), ())), preferred_element_type=F32)


def tn(a, b):
    return lax.dot_general(a, b, (((0,), (0,)), ((), ())), preferred_element_type=F32)


def cat(parts, axis):
    return jnp.concatenate(parts, axis=axis)


def cost(us):
    return pl.CostEstimate(flops=int(us * 1.0e9), bytes_accessed=int(us * 3.5e6), transcendentals=0)


def params():
    return pltpu.CompilerParams(vmem_limit_bytes=VMEM_BYTES)


def head_masks(scale):
    lane = lax.broadcasted_iota(jnp.int32, (1, PAIR), 1)
    first = jnp.where(lane < HD, scale, 0.0).astype(F32)
    second = jnp.where(lane < HD, 0.0, scale).astype(F32)
    return first.astype(BF16), second.astype(BF16)


def stacked(values, masks):
    return cat([values * masks[0], values * masks[1]], 0)


def strip(i, tokens, rows=ROWS):
    return slice(rows * i, rows * i + tokens + rows)


def put_rows(ref, cols, pair):
    head = lax.broadcasted_iota(jnp.int32, (H, 1), 0) - 2 * pl.program_id(0)
    ref[:, cols] = jnp.where(head == 0, pair[0], jnp.where(head == 1, pair[1], ref[:, cols]))


def take_row(values, h, pair=None):
    head = lax.broadcasted_iota(jnp.int32, (H, 1), 0) - 2 * (pl.program_id(0) if pair is None else pair)
    return jnp.sum(jnp.where(head == h, values, 0.0), axis=0, keepdims=True)


def attend_kernel(q_ref, ko_ref, kp_ref, kn_ref, vo_ref, vp_ref, vn_ref, bo_ref, bh_ref, out_ref, lse_ref, kh, vh):
    tokens = q_ref.shape[0]
    kh[:tokens] = kp_ref[...]
    kh[tokens:] = kn_ref[...]
    ones = head_masks(1.0)
    vh[:tokens] = vp_ref[...]
    vh[tokens:] = vn_ref[...]
    vo = stacked(vo_ref[...], ones)
    scaled = head_masks(HD ** -0.5)
    lane = lax.broadcasted_iota(jnp.int32, (ROWS, PAIR), 1)
    for i in range(tokens // ROWS):
        rows = slice(ROWS * i, ROWS * i + ROWS)
        window = strip(i, tokens)
        q = q_ref[rows]
        own_parts, halo_parts, totals, logs = [], [], [], []
        for mask in scaled:
            qm = q * mask
            so = nt(qm, ko_ref[...]) + bo_ref[rows]
            sh = nt(qm, kh[window]) + bh_ref[i]
            peak = jnp.maximum(jnp.max(so, axis=1, keepdims=True), jnp.max(sh, axis=1, keepdims=True))
            po = jnp.exp(so - peak)
            ph = jnp.exp(sh - peak)
            total = jnp.sum(po, axis=1, keepdims=True) + jnp.sum(ph, axis=1, keepdims=True)
            own_parts.append(po.astype(BF16))
            halo_parts.append(ph.astype(BF16))
            totals.append(1.0 / total)
            logs.append((peak + jnp.log(total)).T)
        out = nn(cat(own_parts, 1), vo) + nn(cat(halo_parts, 1), stacked(vh[window], ones))
        out = out * jnp.where(lane < HD, totals[0], totals[1])
        out_ref[rows] = out.astype(BF16)
        put_rows(lse_ref, rows, logs)


def attend(mixed, before, after, bias_own, bias_halo):
    tokens, width = mixed.shape[0], mixed.shape[1] // 3
    pairs = width // PAIR

    near = pairs // 2

    def column(part):
        return pl.BlockSpec((tokens, PAIR), lambda p: (0, (p // near * 3 + part) * near + p % near))

    whole = lambda shape: pl.BlockSpec(shape, lambda p: (0,) * len(shape))
    return pl.pallas_call(
        attend_kernel,
        grid=(pairs,),
        in_specs=[column(0), column(1), column(1), column(1), column(2), column(2), column(2), whole(bias_own.shape), whole(bias_halo.shape)],
        out_specs=[pl.BlockSpec((tokens, PAIR), lambda p: (0, p)), whole((H, tokens))],
        out_shape=[jax.ShapeDtypeStruct((tokens, width), BF16), jax.ShapeDtypeStruct((H, tokens), F32)],
        scratch_shapes=[pltpu.VMEM((2 * tokens, PAIR), BF16), pltpu.VMEM((2 * tokens, PAIR), BF16)],
        compiler_params=params(),
        cost_estimate=cost(0.48),
        name="attend",
    )(mixed, mixed, before, after, mixed, before, after, bias_own, bias_halo)


def own_grad_kernel(q_ref, ko_ref, kp_ref, kn_ref, vo_ref, vp_ref, vn_ref, do_ref, log_ref, mean_ref, bo_ref, bh_ref, dq_keep, dq_send, dkv_ref, sum_ref, kh, vh, dq_ref):
    tokens = q_ref.shape[0]
    kh[:tokens] = kp_ref[...]
    kh[tokens:] = kn_ref[...]
    vh[:tokens] = vp_ref[...]
    vh[tokens:] = vn_ref[...]
    ones = head_masks(1.0)
    scaled = head_masks(HD ** -0.5)
    k_own = ko_ref[...]
    v_own = vo_ref[...]
    k_pair = stacked(k_own, scaled)
    log_rows = [take_row(log_ref[...], h) for h in range(2)]
    mean_rows = [take_row(mean_ref[...], h) for h in range(2)]
    chunk = ROWS
    for c in range(tokens // chunk):
        cols = slice(chunk * c, chunk * c + chunk)
        q = q_ref[cols]
        do = do_ref[cols]
        probs, grads, qs, dos = [], [], [], []
        for h in range(2):
            qm = q * scaled[h]
            dm = do * ones[h]
            st = nt(k_own, qm) + bo_ref[:, cols]
            pt = jnp.exp(st - log_rows[h][:, cols])
            gt = pt * (nt(v_own, dm) - mean_rows[h][:, cols])
            probs.append(pt.astype(BF16))
            grads.append(gt.astype(BF16))
            qs.append(qm)
            dos.append(dm)
        dv = nn(cat(probs, 1), cat(dos, 0))
        dk = nn(cat(grads, 1), cat(qs, 0))
        if c == 0:
            dkv_ref[0, 0] = dk
            dkv_ref[0, 1] = dv
        else:
            dkv_ref[0, 0] += dk
            dkv_ref[0, 1] += dv
        dq_own = tn(cat(grads, 0), k_pair)
        for r in range(chunk // ROWS):
            i = c * (chunk // ROWS) + r
            rows = slice(ROWS * i, ROWS * i + ROWS)
            window = strip(i, tokens)
            halo = []
            for h in range(2):
                qm = q[ROWS * r : ROWS * r + ROWS] * scaled[h]
                dm = do[ROWS * r : ROWS * r + ROWS] * ones[h]
                s = nt(qm, kh[window]) + bh_ref[i]
                p = jnp.exp(s - log_rows[h][:, rows].T)
                halo.append((p * (nt(dm, vh[window]) - mean_rows[h][:, rows].T)).astype(BF16))
            dq = dq_own[ROWS * r : ROWS * r + ROWS] + nn(cat(halo, 1), stacked(kh[window], scaled))
            dq = dq.astype(BF16)
            dq_ref[rows] = dq
            sum_ref[...] = column_sum(dq.astype(F32)) + (sum_ref[...] if i else 0.0)

    @pl.when(pl.program_id(0) < pl.num_programs(0) // 2)
    def _():
        dq_keep[...] = dq_ref[...]

    @pl.when(pl.program_id(0) >= pl.num_programs(0) // 2)
    def _():
        dq_send[...] = dq_ref[...]


def own_grads(mixed, before, after, payload, logs, means, bias_own, bias_halo):
    tokens, width = mixed.shape[0], payload.shape[1]
    pairs = width // PAIR

    near = pairs // 2

    def column(part):
        return pl.BlockSpec((tokens, PAIR), lambda p: (0, (p // near * 3 + part) * near + p % near))

    whole = lambda shape: pl.BlockSpec(shape, lambda p: (0,) * len(shape))
    block = pl.BlockSpec((tokens, PAIR), lambda p: (0, p))
    return pl.pallas_call(
        own_grad_kernel,
        grid=(pairs,),
        in_specs=[column(0), column(1), column(1), column(1), column(2), column(2), column(2), block, whole(logs.shape), whole(means.shape), whole(bias_own.shape), whole(bias_halo.shape)],
        out_specs=[
            pl.BlockSpec((tokens, PAIR), lambda p: (0, jnp.minimum(p, near - 1))),
            pl.BlockSpec((tokens, PAIR), lambda p: (0, jnp.maximum(p - near, 0))),
            pl.BlockSpec((1, 2, tokens, PAIR), lambda p: (p // near, 0, 0, p % near)),
            pl.BlockSpec((1, PAIR), lambda p: (0, p)),
        ],
        out_shape=[
            jax.ShapeDtypeStruct((tokens, width // 2), BF16),
            jax.ShapeDtypeStruct((tokens, width // 2), BF16),
            jax.ShapeDtypeStruct((2, 2, tokens, width // 2), F32),
            jax.ShapeDtypeStruct((1, width), F32),
        ],
        scratch_shapes=[pltpu.VMEM((2 * tokens, PAIR), BF16), pltpu.VMEM((2 * tokens, PAIR), BF16), pltpu.VMEM((tokens, PAIR), BF16)],
        compiler_params=params(),
        cost_estimate=cost(27.5),
        name="own_grads",
    )(mixed, mixed, before, after, mixed, before, after, payload, logs, means, bias_own, bias_halo)


def halo_grad_kernel(half, ko_ref, vo_ref, qp_ref, qn_ref, dp_ref, dn_ref, lp0, lp1, lp2, ln0, ln1, ln2, bh_ref, dkv_in, dk_ref, dv_ref, sum_ref, qh, dh, lh):
    tokens = ko_ref.shape[0]
    qh[:tokens] = qp_ref[...]
    qh[tokens:] = qn_ref[...]
    dh[:tokens] = dp_ref[...]
    dh[tokens:] = dn_ref[...]
    for first, refs in ((0, (lp0, lp1, lp2)), (tokens, (ln0, ln1, ln2))):
        table = refs[0][...].astype(F32) + refs[1][...].astype(F32) + refs[2][...].astype(F32)
        for h in range(2):
            row = take_row(table, h, pl.program_id(0) + half * pl.num_programs(0))
            lh[0, h : h + 1, first : first + tokens] = row[:, :tokens]
            lh[1, h : h + 1, first : first + tokens] = row[:, tokens:]
    ones = head_masks(1.0)
    scaled = head_masks(HD ** -0.5)
    for j in range(tokens // NARROW):
        rows = slice(NARROW * j, NARROW * j + NARROW)
        window = strip(j, tokens, NARROW)
        q = qh[window]
        do = dh[window]
        k = ko_ref[rows]
        v = vo_ref[rows]
        probs, grads, qs, dos = [], [], [], []
        for h in range(2):
            qm = q * scaled[h]
            dm = do * ones[h]
            st = nt(k, qm) + bh_ref[j]
            pt = jnp.exp(st - lh[0, h : h + 1, window])
            gt = pt * (nt(v, dm) - lh[1, h : h + 1, window])
            probs.append(pt.astype(BF16))
            grads.append(gt.astype(BF16))
            qs.append(qm)
            dos.append(dm)
        dk_ref[rows] = (dkv_in[0, 0, rows] + nn(cat(grads, 1), cat(qs, 0))).astype(BF16)
        dv = (dkv_in[0, 1, rows] + nn(cat(probs, 1), cat(dos, 0))).astype(BF16)
        dv_ref[rows] = dv
        sum_ref[...] = column_sum(dv.astype(F32)) + (sum_ref[...] if j else 0.0)


def halo_grads(mixed, before, after, grad_before, grad_after, bias_halo, dkv, half):
    tokens, width = dkv.shape[2], 2 * dkv.shape[3]
    near = width // PAIR // 2

    def column(part):
        return pl.BlockSpec((tokens, PAIR), lambda p: (0, (half * 3 + part) * near + p))

    whole = lambda shape: pl.BlockSpec(shape, lambda p: (0,) * len(shape))
    both = pl.BlockSpec((1, 2, tokens, PAIR), lambda p: (half, 0, 0, p))
    tables = [pl.BlockSpec((H, width), lambda p, k=k: (tokens // H + k, 0)) for k in range(3)]
    block = pl.BlockSpec((tokens, PAIR), lambda p: (0, half * near + p))
    made = pl.BlockSpec((tokens, PAIR), lambda p: (0, p))
    return pl.pallas_call(
        functools.partial(halo_grad_kernel, half),
        grid=(near,),
        in_specs=[column(1), column(2), column(0), column(0), block, block] + tables + tables + [whole(bias_halo.shape), both],
        out_specs=[made, made, pl.BlockSpec((1, PAIR), lambda p: (0, p))],
        out_shape=[jax.ShapeDtypeStruct((tokens, width // 2), BF16)] * 2 + [jax.ShapeDtypeStruct((1, width // 2), F32)],
        scratch_shapes=[
            pltpu.VMEM((2 * tokens, PAIR), BF16),
            pltpu.VMEM((2 * tokens, PAIR), BF16),
            pltpu.VMEM((2, 2, 2 * tokens), F32),
        ],
        compiler_params=params(),
        cost_estimate=cost(0.05),
        name="halo_grads",
    )(mixed, mixed, before, after, grad_before, grad_after, *[grad_before] * 3, *[grad_after] * 3, bias_halo, dkv)


def mask_biases(segments, place, blocks, tokens):
    line = cat([jnp.full((tokens,), -1, jnp.int32), segments, jnp.full((tokens,), -1, jnp.int32)], 0)
    near = lax.dynamic_slice_in_dim(line, place * tokens, 3 * tokens)
    own = near[tokens : 2 * tokens]
    bias_own = jnp.where(own[:, None] == own[None, :], 0.0, FILL).astype(F32)
    halo = cat([near[:tokens], near[2 * tokens :]], 0)
    at = jnp.arange(tokens, dtype=jnp.int32)
    halo_at = cat([at - tokens, at + tokens], 0)
    allowed = (own[:, None] == halo[None, :]) & (jnp.abs(halo_at[None, :] - at[:, None]) < HALF)
    bias = jnp.where(allowed, 0.0, FILL).astype(F32)
    strips = [jnp.stack([bias[r * i : r * i + r, strip(i, tokens, r)] for i in range(tokens // r)]) for r in (ROWS, NARROW)]
    return bias_own, *strips


def normalized(values):
    average = jnp.mean(values, axis=1, keepdims=True)
    centered = values - average
    spread = jnp.mean(centered * centered, axis=1, keepdims=True)
    inverse = lax.rsqrt(spread + EPS)
    return centered * inverse, inverse


def norm_back(grad, gain, hat, inverse):
    scaled = grad * gain
    return inverse * (
        scaled
        - jnp.mean(scaled, axis=1, keepdims=True)
        - hat * jnp.mean(scaled * hat, axis=1, keepdims=True)
    )


def column_sum(values):
    return jnp.sum(values, axis=0, keepdims=True)


def part_blocks(at_ref, order, second, far):
    for first in range(2):
        rel = {order[-2]: first, order[-1]: second}
        y = jnp.bitwise_xor(at_ref[0], rel["y"])
        x = jnp.bitwise_xor(at_ref[1], rel["x"])
        for i in range(far):
            z = jnp.bitwise_xor(at_ref[3], (i % 2) * 2 + i // 2) if order[0] == "z" else i
            yield first, i, (z * 2 + y) * 2 + x


def start_all(copies):
    for copy in copies:
        copy.start()


def wait_all(copies):
    for copy in copies:
        copy.wait()


def block_place(at_ref, order, z, y, x, far):
    where = {"z": (z, far), "y": (jnp.bitwise_xor(at_ref[0], y), 2), "x": (jnp.bitwise_xor(at_ref[1], x), 2)}
    to = 0
    for axis in order:
        to = to * where[axis][1] + where[axis][0]
    return to


def prepare_kernel(at_ref, qkv_ref, out_ref, up_ref, *refs):
    vectors, mine_ref, send_ref, note_ref = refs[:-3], *refs[-3:]
    width = out_ref.shape[1]
    place = 0
    for ref, piece in ((qkv_ref, width // 2), (out_ref, width // 2), (up_ref, HIDDEN_BLOCK)):
        for i in range(0, ref.shape[1], 2 * piece):
            mine_ref[:, place : place + piece] = ref[:, pl.ds(pl.multiple_of(i + at_ref[2] * piece, piece), piece)]
            send_ref[:, place : place + piece] = ref[:, pl.ds(pl.multiple_of(i + (1 - at_ref[2]) * piece, piece), piece)]
            place += piece
    line = cat([v[...].astype(F32) for v in vectors], 1).astype(BF16)
    note_ref[...] = jnp.zeros_like(note_ref)
    for i in range(line.shape[1] // 128):
        note_ref[i : i + 1] = line[:, i * 128 : i * 128 + 128]


def prepare(at, qkv, out, up, vectors):
    rows = qkv.shape[0]
    columns = (qkv.shape[1] + out.shape[1] + up.shape[1]) // 2
    half = jax.ShapeDtypeStruct((rows, columns), BF16)
    return pl.pallas_call(
        prepare_kernel,
        in_specs=[SMEM] + [VMEM] * (3 + len(vectors)),
        out_shape=[half, half, jax.ShapeDtypeStruct((rows, 128), BF16)],
        compiler_params=params(),
        cost_estimate=cost(0.04),
        name="prepare",
    )(at, qkv, out, up, *[v[None] for v in vectors])


def arrange_kernel(at_ref, mine_ref, got_ref, note_ref, block_ref, up_ref):
    rows, cut = mine_ref.shape[0], block_ref.shape[2] - 128
    block_ref[0, :, cut:] = note_ref[...]
    block_ref[1, :, cut:] = jnp.zeros_like(note_ref)

    def lay(first, second):
        for i, ref in ((0, first), (1, second)):
            block_ref[i, :, :cut] = ref[:, :cut]
            up_ref[i * rows : i * rows + rows] = ref[:, cut:]

    @pl.when(at_ref[2] == 0)
    def _():
        lay(mine_ref, got_ref)

    @pl.when(at_ref[2] != 0)
    def _():
        lay(got_ref, mine_ref)


def arrange(at, mine, got, note, hidden):
    rows, columns = mine.shape
    return pl.pallas_call(
        arrange_kernel,
        in_specs=[SMEM] + [VMEM] * 3,
        out_shape=[
            jax.ShapeDtypeStruct((2, rows, columns - hidden // 2 + 128), BF16),
            jax.ShapeDtypeStruct((2 * rows, hidden // 2), BF16),
        ],
        compiler_params=params(),
        cost_estimate=cost(0.04),
        name="arrange",
    )(at, mine, got, note)


def first_copies(refs, qkv, out, sems, at_ref, far):
    width, columns = qkv.shape
    half, near = width // 2, columns // 2
    copies = []

    def add(source, target):
        copies.append(pltpu.make_async_copy(source, target, sems.at[len(copies)]))

    def column(core):
        return pl.ds(pl.multiple_of(jnp.bitwise_xor(at_ref[2], core) * half, half), half)

    for core in range(2):
        if far is None:
            add(refs[core], qkv.at[:, pl.ds(core * near, near)])
            for part in range(2):
                row = pl.ds(pl.multiple_of(jnp.bitwise_xor(at_ref[2], part) * half, half), half)
                add(refs[2 + core].at[pl.ds(part * half, half)], out.at[row, column(core)])
            continue
        rows = width // (8 * far)
        for color, order in enumerate(("zyx", "zxy")):
            for second in range(2):
                ref = refs[core * 4 + color * 2 + second]
                for first, z, block in part_blocks(at_ref, order, second, far):
                    row = (block * 2 + color) * rows
                    add(ref.at[first, z, :, pl.ds(0, near)], qkv.at[pl.ds(pl.multiple_of(row, rows), rows), pl.ds(core * near, near)])
                    row = jnp.bitwise_xor(row, at_ref[2] * half)
                    add(ref.at[first, z, :, pl.ds(near, half)], out.at[pl.ds(pl.multiple_of(row, rows), rows), column(core)])
    return copies


def project_kernel(far, parts, *refs):
    at_ref, refs = refs[0], refs[1:]
    part_refs, refs = refs[:parts], refs[parts:]
    own_ref, row_ref, own_out, qkv_out, out_out, qkv, out, sems, out_sems = refs
    copies = first_copies(part_refs, qkv, out, sems, at_ref, far)
    start_all(copies)
    wait_all(copies)
    keep = [pltpu.make_async_copy(qkv, qkv_out, out_sems.at[0]), pltpu.make_async_copy(out, out_out, out_sems.at[1])]
    start_all(keep)
    chunk = 512

    def body(j, carry):
        cols = pl.ds(pl.multiple_of(j * chunk, chunk), chunk)
        own_out[:, cols] = (nn(own_ref[...], qkv[:, cols]) + row_ref[:, cols]).astype(BF16)
        return carry

    lax.fori_loop(0, qkv.shape[1] // chunk, body, 0)
    wait_all(keep)


def copy_count(far, each):
    return 2 if far is None else 8 * far * each


def project(far, at, parts, x, row):
    tokens, width = x.shape
    columns = row.shape[1]
    mixed = jax.ShapeDtypeStruct((tokens, columns), BF16)
    return pl.pallas_call(
        functools.partial(project_kernel, far, len(parts)),
        in_specs=[SMEM] + [ANY] * len(parts) + [VMEM] * 2,
        out_specs=[VMEM, ANY, ANY],
        out_shape=[mixed, jax.ShapeDtypeStruct((width, columns), BF16), jax.ShapeDtypeStruct((width, width), BF16)],
        scratch_shapes=[
            pltpu.VMEM((width, columns), BF16),
            pltpu.VMEM((width, width), BF16),
            pltpu.SemaphoreType.DMA((6 if far is None else 64 * far,)),
            pltpu.SemaphoreType.DMA((2,)),
        ],
        compiler_params=params(),
        cost_estimate=cost(0.26),
        name="project",
    )(at, *parts, x, row)


def project_more_kernel(before_ref, after_ref, w_ref, row_ref, before_out, after_out):
    for source, target in ((before_ref, before_out), (after_ref, after_out)):
        target[...] = (nn(source[...], w_ref[...]) + row_ref[...]).astype(BF16)


def project_more(before, after, full, row, chunk=512):
    tokens, width = before.shape
    columns = full.shape[1]
    whole = pl.BlockSpec((tokens, width), lambda i: (0, 0))
    block = pl.BlockSpec((tokens, chunk), lambda i: (0, i))
    return pl.pallas_call(
        project_more_kernel,
        grid=(columns // chunk,),
        in_specs=[whole, whole, pl.BlockSpec((width, chunk), lambda i: (0, i)), pl.BlockSpec((1, chunk), lambda i: (0, i))],
        out_specs=[block, block],
        out_shape=[jax.ShapeDtypeStruct((tokens, columns), BF16)] * 2,
        compiler_params=params(),
        cost_estimate=cost(0.214),
        name="project_more",
    )(before, after, full, row)


def out_kernel(heads_ref, w_ref, x_ref, vec_ref, hat_ref, inv_ref, low_ref):
    branch = nn(heads_ref[...], w_ref[...]) + vec_ref[0:1]
    hat, inverse = normalized(x_ref[...].astype(F32) + branch)
    hat_ref[...] = hat
    inv_ref[...] = inverse
    low_ref[...] = (hat * vec_ref[1:2] + vec_ref[2:3]).astype(BF16)


def out_project(heads, out_full, x, vectors):
    tokens, width = heads.shape
    rows = tokens // 2
    block = pl.BlockSpec((rows, width), lambda i: (i, 0))
    return pl.pallas_call(
        out_kernel,
        grid=(2,),
        in_specs=[block, pl.BlockSpec(out_full.shape, lambda i: (0, 0)), block, pl.BlockSpec(vectors.shape, lambda i: (0, 0))],
        out_specs=[block, pl.BlockSpec((rows, 1), lambda i: (i, 0)), block],
        out_shape=[
            jax.ShapeDtypeStruct((tokens, width), F32),
            jax.ShapeDtypeStruct((tokens, 1), F32),
            jax.ShapeDtypeStruct((tokens, width), BF16),
        ],
        compiler_params=params(),
        cost_estimate=cost(0.114),
        name="out_project",
    )(heads, out_full, x, vectors)


def up_copies(refs, full, sems, at_ref, far):
    width, half = full.shape[0], full.shape[1] // 2
    copies = []
    for core in range(2):
        cols = pl.ds(core * half, half)
        if far is None:
            copies.append(pltpu.make_async_copy(refs[core], full.at[:, cols], sems.at[core]))
            continue
        rows = width // (4 * far)
        for second in range(2):
            ref = refs[core * 2 + second]
            for first, z, block in part_blocks(at_ref, "zyx", second, far):
                to = full.at[pl.ds(pl.multiple_of(block * rows, rows), rows), cols]
                copies.append(pltpu.make_async_copy(ref.at[first, z], to, sems.at[len(copies)]))
    return copies


def down_copies(refs, full, sems, at_ref, far):
    half = full.shape[0] // 2
    copies = []
    for core in range(2):
        if far is None:
            copies.append(pltpu.make_async_copy(refs[core], full.at[pl.ds(core * half, half)], sems.at[core]))
            continue
        rows = half // (4 * far)
        for second in range(2):
            ref = refs[core * 2 + second]
            for first, z, block in part_blocks(at_ref, "xy", second, far):
                to = full.at[pl.ds(pl.multiple_of(core * half + block * rows, rows), rows)]
                copies.append(pltpu.make_async_copy(ref.at[first, z], to, sems.at[len(copies)]))
    return copies


def middle_kernel(far, ups, downs, *refs):
    at_ref, refs = refs[0], refs[1:]
    up_refs, down_refs, refs = refs[:ups], refs[ups : ups + downs], refs[ups + downs :]
    low_ref, row_ref, vec_ref, log_ref, inv_ref, hat_in, dy_in, heads_in, out_in = refs[:9]
    act_out, act_send, result_out, glow_out, lift_out, lift_send, one_out, mine_out, send_out, pay_out, mean_ref, row_sums, two_sums, one_sums = refs[9:23]
    up, down, out, hat, dy, heads, act, slope, result, glow, total, branch, sides, payload, up_sems, down_sems, in_sems, out_sems = refs[23:]
    tokens, width = low_ref.shape
    half = up.shape[1] // 2
    chunk = half
    from_up = up_copies(up_refs, up, up_sems, at_ref, far)
    from_down = down_copies(down_refs, down, down_sems, at_ref, far)
    loads = [pltpu.make_async_copy(*pair, in_sems.at[i]) for i, pair in enumerate(((hat_in, hat), (dy_in, dy), (out_in, out), (heads_in, heads)))]
    start_all(from_up)
    start_all(from_down)
    start_all(loads)
    stores = []

    def store(source, target):
        copy = pltpu.make_async_copy(source, target, out_sems.at[len(stores)])
        stores.append(copy)
        copy.start()

    def cols(i):
        return slice(i * chunk, i * chunk + chunk)

    def raise_one(i):
        lifted = nn(low_ref[...], up[:, cols(i)]) + row_ref[:, cols(i)]
        phi = 0.5 * (1.0 + lax.erf(lifted * (0.5 ** 0.5)))
        density = jnp.exp(lifted * lifted * -0.5) * 0.3989422804014327
        act[:, cols(i)] = (lifted * phi).astype(BF16)
        slope[:, cols(i)] = (phi + lifted * density).astype(BF16)

    def settle_one(i):
        total[...] += nn(act[:, cols(i)], down[cols(i)])

    half_up, half_down = len(from_up) // 2, len(from_down) // 2
    wait_all(from_up[:half_up])
    raise_one(0)
    wait_all(from_up[half_up:])
    wait_all(from_down[:half_down])
    raise_one(1)
    total[...] = nn(act[:, cols(0)], down[cols(0)])
    wait_all(from_down[half_down:])
    settle_one(1)
    store(act.at[:, pl.ds(0, half)], act_out)
    store(act.at[:, pl.ds(half, half)], act_send)
    wait_all(loads)

    rows = 128
    for n in range(tokens // rows):
        at = slice(rows * n, rows * n + rows)
        first = hat[at] * vec_ref[3:4] + vec_ref[4:5]
        hat_two, inverse = normalized(first + (total[at] + vec_ref[0:1]))
        result[at] = (hat_two * vec_ref[1:2] + vec_ref[2:3]).astype(BF16)
        grad = dy[at].astype(F32)
        part = [column_sum(grad * hat_two), column_sum(grad)]
        grad = norm_back(grad, vec_ref[1:2], hat_two, inverse)
        low = grad.astype(BF16)
        total[at] = grad
        glow[at] = low
        part = cat(part + [column_sum(low.astype(F32))], 0)
        two_sums[...] = part if n == 0 else two_sums[...] + part
    store(result, result_out)
    store(glow, glow_out)

    def lower_one(i):
        value = (nt(glow[...], down[cols(i)]) * slope[:, cols(i)].astype(F32)).astype(BF16)
        slope[:, cols(i)] = value
        row_sums[:, cols(i)] = column_sum(value.astype(F32))

    def first_one(i):
        total[...] += nt(slope[:, cols(i)], up[:, cols(i)])

    lower_one(0)
    store(slope.at[:, pl.ds(0, half)], lift_out)
    lower_one(1)
    store(slope.at[:, pl.ds(half, half)], lift_send)
    first_one(0)
    first_one(1)

    for n in range(tokens // rows):
        at = slice(rows * n, rows * n + rows)
        grad = total[at]
        one = norm_back(grad, vec_ref[3:4], hat[at], inv_ref[at])
        low = one.astype(BF16)
        total[at] = one
        branch[at] = low
        part = cat([column_sum(grad * hat[at]), column_sum(grad), column_sum(low.astype(F32))], 0)
        one_sums[...] = part if n == 0 else one_sums[...] + part
    store(total, one_out)
    middle = width // 2
    for n in range(2):
        side = pl.multiple_of(jnp.bitwise_xor(at_ref[2], n) * middle, middle)
        sides[n] = branch[:, pl.ds(side, middle)]
    store(sides.at[0], mine_out)
    store(sides.at[1], send_out)

    head = lax.broadcasted_iota(jnp.int32, (H, width), 1) // HD
    pick = jnp.where(head == lax.broadcasted_iota(jnp.int32, (H, width), 0), 1.0, 0.0).astype(F32)
    for n in range(4):
        part = slice(width // 4 * n, width // 4 * (n + 1))
        grad = nt(branch[...], out[part]).astype(BF16)
        payload[:tokens, part] = grad
        product = grad.astype(F32) * heads[:, part].astype(F32)
        means = lax.dot_general(
            pick[:, part], product, (((1,), (1,)), ((), ())), precision=lax.Precision.HIGHEST, preferred_element_type=F32
        )
        mean_ref[...] = means if n == 0 else mean_ref[...] + means
    rest = cat([log_ref[...], mean_ref[...]], 1)
    for n in range(3):
        term = rest.astype(BF16)
        rest = rest - term.astype(F32)
        payload[tokens + H * n : tokens + H * n + H] = term
    store(payload, pay_out)
    wait_all(stores)


def middle(far, at, up_parts, down_parts, low, row, vectors, logs, inverse, hat, dy, heads, out_full):
    tokens, width = low.shape
    hidden = row.shape[1]
    half = hidden // 2
    shape = jax.ShapeDtypeStruct
    pay_shape = (tokens + 3 * H, width)
    return pl.pallas_call(
        functools.partial(middle_kernel, far, len(up_parts), len(down_parts)),
        in_specs=[SMEM] + [ANY] * (len(up_parts) + len(down_parts)) + [VMEM] * 5 + [ANY] * 4,
        out_specs=[ANY] * 10 + [VMEM] * 4,
        out_shape=[
            shape((tokens, half), BF16),
            shape((tokens, half), BF16),
            shape((tokens, width), BF16),
            shape((tokens, width), BF16),
            shape((tokens, half), BF16),
            shape((tokens, half), BF16),
            shape((tokens, width), F32),
            shape((tokens, width // 2), BF16),
            shape((tokens, width // 2), BF16),
            shape(pay_shape, BF16),
            shape((H, tokens), F32),
            shape((1, hidden), F32),
            shape((3, width), F32),
            shape((3, width), F32),
        ],
        scratch_shapes=[
            pltpu.VMEM((width, hidden), BF16),
            pltpu.VMEM((hidden, width), BF16),
            pltpu.VMEM((width, width), BF16),
            pltpu.VMEM((tokens, width), F32),
            pltpu.VMEM((tokens, width), BF16),
            pltpu.VMEM((tokens, width), BF16),
            pltpu.VMEM((tokens, hidden), BF16),
            pltpu.VMEM((tokens, hidden), BF16),
            pltpu.VMEM((tokens, width), BF16),
            pltpu.VMEM((tokens, width), BF16),
            pltpu.VMEM((tokens, width), F32),
            pltpu.VMEM((tokens, width), BF16),
            pltpu.VMEM((2, tokens, width // 2), BF16),
            pltpu.VMEM(pay_shape, BF16),
            pltpu.SemaphoreType.DMA((copy_count(far, 2),)),
            pltpu.SemaphoreType.DMA((copy_count(far, 2),)),
            pltpu.SemaphoreType.DMA((4,)),
            pltpu.SemaphoreType.DMA((10,)),
        ],
        compiler_params=params(),
        cost_estimate=cost(45),
        name="middle",
    )(at, *up_parts, *down_parts, low, row, vectors, logs, inverse, hat, dy, heads, out_full)


def down_grad_kernel(far, at_ref, act_ref, act_got, glow_ref, glow_got, dw_ref, glows):
    tokens = glow_ref.shape[0]

    @pl.when(pl.program_id(0) == 0)
    def _():
        glows[:tokens] = glow_ref[...]
        glows[tokens:] = glow_got[...]

    dw = tn(cat([act_ref[...], act_got[...]], 0), glows[...]).astype(BF16)
    if far is None:
        dw_ref[...] = dw
        return
    rows = dw.shape[0] // 4
    for j in range(4):
        to = block_place(at_ref, "yx", 0, j // 2, j % 2, far)
        dw_ref[pl.ds(pl.multiple_of(to * rows, rows), rows)] = dw[j * rows : j * rows + rows]


def down_grads(far, at, active, act_got, glow, glow_got):
    tokens, half = active.shape
    width = glow.shape[1]
    chunk = half // 4
    whole = pl.BlockSpec((tokens, width), lambda i: (0, 0))
    block = pl.BlockSpec((tokens, chunk), lambda i: (0, i))
    return pl.pallas_call(
        functools.partial(down_grad_kernel, far),
        grid=(4,),
        in_specs=[SMEM, block, block, whole, whole],
        out_specs=pl.BlockSpec((chunk, width), lambda i: (i, 0)),
        out_shape=jax.ShapeDtypeStruct((half, width), BF16),
        scratch_shapes=[pltpu.VMEM((2 * tokens, width), BF16)],
        compiler_params=params(),
        cost_estimate=cost(8.5),
        name="down_grads",
    )(at, active, act_got, glow, glow_got)


def both_flipped(at_ref, mine_ref, got_ref, flipped, far, heads=False, distant=False):
    tokens = mine_ref.shape[0]
    for core, ref in ((0, mine_ref), (1, got_ref)):
        turned = ref[...].T
        cols = slice(core * tokens, core * tokens + tokens)
        flip = jnp.bitwise_xor(at_ref[2], core) if heads else 0
        half = turned.shape[0] // 2
        if far is None:
            for part in range(2):
                to = jnp.bitwise_xor(flip, part) * half
                flipped[pl.ds(pl.multiple_of(to, half), half), cols] = turned[part * half : part * half + half]
            continue
        rows = turned.shape[0] // (8 * far)
        for z in range(far):
            at_z = jnp.bitwise_xor(z, flip * (far // 2))
            if distant:
                away = jnp.bitwise_xor(at_z, at_ref[3])
                at_z = away % 2 * 2 + away // 2
            for y in range(2):
                for x in range(2):
                    a = ((z * 2 + y) * 2 + x) * 2 * rows
                    to_y, to_x = jnp.bitwise_xor(at_ref[0], y), jnp.bitwise_xor(at_ref[1], x)
                    first = ((1 - to_x) * 2 + to_y) * far + at_z
                    second = ((3 - to_y) * 2 + to_x) * far + at_z
                    for i, to in enumerate((first, second)):
                        to = pl.ds(pl.multiple_of(to * rows, rows), rows)
                        flipped[to, cols] = turned[a + i * rows : a + i * rows + rows]


def quarter_specs(rows, columns, index):
    return [pl.BlockSpec((rows // 4, columns), index)] * 4


def put_quarters(refs, cols, value):
    rows = value.shape[0] // 4
    for i, ref in enumerate(refs):
        ref[:, cols] = value[i * rows : i * rows + rows]


def late_grad_kernel(far, at_ref, low_ref, low_got, heads_ref, heads_got, lift_ref, lift_got, branch_ref, branch_got, *refs):
    quarters, flipped = refs[:4], refs[4]
    step = pl.program_id(0)
    last = pl.num_programs(0) - 1

    @pl.when(step == 0)
    def _():
        both_flipped(at_ref, low_ref, low_got, flipped, far, distant=True)

    @pl.when(step < last)
    def _():
        put_quarters(quarters, slice(None), nn(flipped[...], cat([lift_ref[...], lift_got[...]], 0)).astype(BF16))

    @pl.when(step == last)
    def _():
        both_flipped(at_ref, heads_ref, heads_got, flipped, far, heads=True, distant=True)
        put_quarters(quarters, slice(None), nn(flipped[...], cat([branch_ref[...], branch_got[...]], 0)).astype(BF16))


def late_grads(far, at, low, low_got, heads, heads_got, lift, lift_got, branch, branch_got):
    tokens, width = low.shape
    chunk = branch.shape[1]
    steps = lift.shape[1] // chunk
    whole = lambda shape: pl.BlockSpec(shape, lambda i: (0, 0))
    block = pl.BlockSpec((tokens, chunk), lambda i: (0, jnp.minimum(i, steps - 1)))
    return pl.pallas_call(
        functools.partial(late_grad_kernel, far),
        grid=(steps + 1,),
        in_specs=[SMEM] + [whole((tokens, width))] * 4 + [block, block] + [whole((tokens, chunk))] * 2,
        out_specs=quarter_specs(width, chunk, lambda i: (0, i)),
        out_shape=[jax.ShapeDtypeStruct((width // 4, (steps + 1) * chunk), BF16)] * 4,
        scratch_shapes=[pltpu.VMEM((width, 2 * tokens), BF16)],
        compiler_params=params(),
        cost_estimate=cost(9),
        name="late_grads",
    )(at, low, low_got, heads, heads_got, lift, lift_got, branch, branch_got)


def qkv_grad_kernel(far, at_ref, x_ref, x_got, *refs):
    keeps, gots, refs = refs[:3], refs[3:6], refs[6:]
    note_refs, quarters, flipped = refs[:-5], refs[-5:-1], refs[-1]
    both_flipped(at_ref, x_ref, x_got, flipped, far, distant=True)
    chunk = keeps[0].shape[1]
    for n in range(3):
        dw = nn(flipped[...], cat([keeps[n][...], gots[n][...]], 0)).astype(BF16)
        put_quarters(quarters, slice(n * chunk, n * chunk + chunk), dw)
    for ref in note_refs:
        put_quarters(quarters, slice(3 * chunk, 3 * chunk + ref.shape[1]), ref[...])


def qkv_grads(far, at, x, x_got, keep, got, notes=()):
    tokens, width = x.shape
    columns = 3 * keep[0].shape[1] + sum(v.shape[1] for v in notes)
    return pl.pallas_call(
        functools.partial(qkv_grad_kernel, far),
        in_specs=[SMEM] + [VMEM] * (8 + len(notes)),
        out_shape=[jax.ShapeDtypeStruct((width // 4, columns), BF16)] * 4,
        scratch_shapes=[pltpu.VMEM((width, 2 * tokens), BF16)],
        compiler_params=params(),
        cost_estimate=cost(8.3),
        name="qkv_grads",
    )(at, x, x_got, *keep, *got, *notes)


FAR, Y, X, CORE = "far", "y", "x", "fsdp"
CTX = (FAR, Y, X)
ALL = CTX + (CORE,)


def swap(values, axis):
    return lax.ppermute(values, axis, [(0, 1), (1, 0)])


def swap_both(values):
    return lax.ppermute(values, (Y, X), [(i, 3 - i) for i in range(4)])


def swap_far(values, step):
    return lax.ppermute(values, FAR, [(i, i ^ step) for i in range(lax.axis_size(FAR))])


def together(*arrays):
    return lax.optimization_barrier(arrays)


def choose(core, left, right):
    return jnp.where(core == 0, left, right), jnp.where(core == 0, right, left)


def added(*terms):
    total = terms[0].astype(F32)
    for term in terms[1:]:
        total = total + term.astype(F32)
    return total.astype(BF16)


def own_rows(core, summed):
    mine, send = choose(core, summed[0], summed[1])
    return choose(core, mine, swap(send, CORE))


def color_nexts(keep_x, keep_y, there_x, there_y):
    return added(keep_x[1], there_x[1]), added(keep_y[1], there_y[1])


def color_sums(keep_x, keep_y, there_x, there_y, there_xy, there_yx):
    return jnp.stack([added(keep_x[0], there_x[0], there_xy), added(keep_y[0], there_y[0], there_yx)], 1)


def shards(inputs, segments, cotangent, qkv_weight, query_bias, value_bias, out_weight, out_bias, first_gain, first_shift, up_weight, up_bias, down_weight, down_bias, second_gain, second_shift):
    tokens, width = inputs.shape[1:]
    rows, hidden = up_weight.shape
    piece = down_weight.shape[0]
    near = width // 2
    blocks = lax.axis_size(CTX)
    place = lax.axis_index(CTX)
    core = lax.axis_index(CORE)
    at = jnp.stack([lax.axis_index(Y), lax.axis_index(X), core, lax.axis_index(FAR)]).astype(jnp.int32)
    far = 4 if rows % 32 == 0 and lax.axis_size(FAR) == 4 and piece == HIDDEN_BLOCK else None
    onward = [(i, i + 1) for i in range(blocks - 1)]
    back = [(i + 1, i) for i in range(blocks - 1)]

    def from_before(v):
        return lax.ppermute(v, CTX, onward)

    def from_after(v):
        return lax.ppermute(v, CTX, back)

    def own_first(v):
        return cat(choose(core, v[:, :near], v[:, near:]), 1)

    x = inputs[0]
    vectors = (query_bias, value_bias, out_bias, first_gain, first_shift, down_bias, second_gain, second_shift, up_bias)
    each = query_bias.shape[0]
    if far is None:
        split = lambda w, size: w.reshape(rows, -1, 2, size).swapaxes(0, 2).swapaxes(1, 2).reshape(2, rows, -1)
        sides = cat([split(qkv_weight, near), split(out_weight, near), split(up_weight, piece)], 2)
        mine, send = choose(core, sides[0], sides[1])
        both = cat(choose(core, mine, swap(send, CORE)), 0)
        whole = lambda v: lax.all_gather(v, CTX, axis=0, tiled=True)
        pair = lambda v: [v, swap(v, CORE)]
        qkv_parts = pair(whole(both[:, : 3 * near])) + pair(whole(both[:, 3 * near : 4 * near]))
        up_parts, down_parts = pair(whole(both[:, 4 * near :])), pair(whole(down_weight))
        x_before, x_after = from_before(x), from_after(x)
        table = lax.all_gather(cat(vectors, 0)[None], ALL, axis=0, tiled=True)
    else:
        mine, send, note = prepare(at, qkv_weight, out_weight, up_weight, vectors)
        block, up_block = arrange(at, mine, swap(send, CORE), note, hidden)
        cut = 4 * near
        lines = sum(v.shape[0] for v in vectors) // 128
        pair = jnp.stack([block, swap_far(block, 2)])
        down_pair = jnp.stack([down_weight, swap(down_weight, X)])
        pair, x_before, x_two = together(pair, from_before(x), x)
        wide = jnp.stack([pair, swap_far(pair, 1)]).reshape((4,) + block.shape)
        x_after = from_after(x_two)
        wide, up_block, down_pair, x_after = together(wide, up_block, down_pair, x_after)
        a1, b1, up_hi = swap(wide[:, 0], Y), swap(wide[:, 1], X), swap_far(up_block, 2)
        a1, b1, up_hi = together(a1, b1, up_hi)
        pair_a, pair_b, up_pair = jnp.stack([wide[:, 0], a1]), jnp.stack([wide[:, 1], b1]), jnp.stack([up_block, up_hi])
        a2, b2, up_lo = swap(pair_a, X), swap(pair_b, Y), swap_far(up_pair, 1)
        up_lo, down_pair = together(up_lo, down_pair)
        down_wide = lax.all_gather(down_pair, FAR, axis=1)
        a2, b2, up_lo = together(a2, b2, up_lo)
        first_parts = [pair_a, a2, pair_b, b2]
        qkv_parts = first_parts + [swap(p, CORE) for p in first_parts]
        up_wide = jnp.stack([up_pair, up_lo]).reshape((4,) + up_block.shape)
        up_y = swap(up_wide, Y)
        notes = jnp.stack([jnp.stack([qkv_parts[4 * c + s][:, :, :lines, cut:] for s in range(2)]) for c in range(2)])
        notes = notes.reshape(2, 2, 2, 2, 2, -1).swapaxes(3, 4)
        for axis, index in ((0, core), (1, at[1]), (2, at[0]), (3, at[3] // 2), (4, at[3] % 2)):
            notes = jnp.where(index == 0, notes, jnp.flip(notes, axis))
        table = notes.transpose(3, 4, 2, 1, 0, 5).reshape(2 * blocks, -1)

    rows_of = [table[:, each * i : each * i + each].reshape(1, width).astype(F32) for i in range(8)]
    query_row, value_row, out_row, gain_one, shift_one, down_row, gain_two, shift_two = rows_of
    up_row = table[:, 8 * each :].reshape(blocks, 2, piece).astype(F32)
    up_row = cat(choose(core, up_row[:, 0].reshape(1, -1), up_row[:, 1].reshape(1, -1)), 1)
    bias_own, bias_halo, bias_narrow = mask_biases(segments[0], place, blocks, tokens)
    query_row, value_row, gap = own_first(query_row), own_first(value_row), jnp.zeros((1, near), F32)
    qkv_row = cat([query_row[:, :near], gap, value_row[:, :near], query_row[:, near:], gap, value_row[:, near:]], 1)

    mixed, qkv_full, out_full = project(far, at, qkv_parts, x, qkv_row)
    if far is not None:
        qkv_full, up_y = together(qkv_full, up_y)
        up_pair = jnp.stack([up_wide, up_y])
        up_x, up_pair_core = swap(up_pair, X), swap(up_pair, CORE)
    before, after = project_more(x_before, x_after, qkv_full, qkv_row)
    if far is not None:
        before, down_wide = together(before, down_wide)
        down_y, down_wide_core = swap(down_wide, Y), swap(down_wide, CORE)
    heads, logs = attend(mixed, before, after, bias_own, bias_halo)
    hat, inverse, low = out_project(heads, out_full, x, cat([out_row, gain_one, shift_one], 0))
    low, x_got, heads_got = together(low, swap(x, CORE), swap(heads, CORE))
    if far is not None:
        low, up_x, up_pair_core, down_wide_core, down_y = together(low, up_x, up_pair_core, down_wide_core, down_y)
        up_parts = [up_pair, up_x, up_pair_core, swap(up_x, CORE)]
        down_parts = [down_wide, down_y, down_wide_core, swap(down_y, CORE)]
    low_got = swap(low, CORE)
    (
        active, act_send, result, glow, lift_keep, lift_send, grad_one, branch_mine, branch_send, payload, means, up_bias_part, sums_two, sums_one,
    ) = middle(
        far, at, up_parts, down_parts, low, up_row, cat([down_row, gain_two, shift_two, gain_one, shift_one], 0),
        logs, inverse, hat, cotangent[0], heads, out_full,
    )
    payload, low_got = together(payload, low_got)
    pay_before, pay_after = from_before(payload), from_after(payload)
    act_got, glow_got, lift_got, branch_got = swap(act_send, CORE), swap(glow, CORE), swap(lift_send, CORE), swap(branch_send, CORE)
    down_part = down_grads(far, at, active, act_got, glow, glow_got)
    late = late_grads(far, at, low, low_got, heads, heads_got, lift_keep, lift_got, branch_mine, branch_got)
    dq_keep, dq_send, dkv, dq_sum = own_grads(mixed, before, after, payload, logs, means, bias_own, bias_halo)
    if far is not None:
        down_part = lax.psum_scatter(down_part.reshape(far, 2, 2, piece, width), FAR, scatter_dimension=0, tiled=False)
        by = lambda parts: [v.reshape(2, far, rows, v.shape[1]) for v in parts]
        late_send_x, late_keep_x, late_send_y, late_keep_y = by(late)
        late_x, late_y, pay_before, pay_after, dkv = together(late_send_x, late_send_y, pay_before, pay_after, dkv)
        late_x, late_y = swap(late_x, X), swap(late_y, Y)
    *send, sum_send = halo_grads(mixed, before, after, pay_before, pay_after, bias_narrow, dkv, 1)
    send = [dq_send] + send
    *keep, sum_keep = halo_grads(mixed, before, after, pay_before, pay_after, bias_narrow, dkv, 0)
    if far is not None:
        late_x, late_y, sum_keep = together(late_x, late_y, sum_keep)
    keep, dv_sum = [dq_keep] + keep, cat([sum_keep, sum_send], 1)
    got = [swap(v, CORE) for v in send]
    if far is not None:
        late_xy, late_yx = color_nexts(late_keep_x, late_keep_y, late_x, late_y)
        late_xy, late_yx, *got = together(late_xy, late_yx, *got)
        late_xy, late_yx = swap(late_xy, Y), swap(late_yx, X)
    features = (own_first(dq_sum), own_first(dv_sum), sums_one[2], sums_one[0], sums_one[1], sums_two[2], sums_two[0], sums_two[1])
    small = jnp.stack([v.reshape(blocks, 2, each) for v in features], 2).reshape(blocks, 2, -1)
    sides = choose(core, up_bias_part[:, : hidden // 2], up_bias_part[:, hidden // 2 :])
    small = cat([small, jnp.stack([v.reshape(blocks, piece) for v in sides], 1)], 2)
    if far is None:
        qkv = qkv_grads(far, at, x, x_got, keep, got)
        total = lambda v: lax.psum_scatter(v, CTX, scatter_dimension=0, tiled=True)
        down_sum = total(down_part).astype(F32)
        small_sum = lax.psum_scatter(small.reshape(2 * blocks, -1), ALL, scatter_dimension=0, tiled=True)[0]
        late_sum, qkv_sum = [total(cat(v, 0)).reshape(2, rows, -1) for v in (late, qkv)]
    else:
        small = small.astype(BF16).reshape(far, 2, 2, 2, lines, 128).transpose(3, 2, 1, 0, 4, 5)
        for axis, index in ((1, at[1]), (2, at[0])):
            small = jnp.where(index == 0, small, jnp.flip(small, axis))
        small = jnp.stack([jnp.flip(small[0], 0), jnp.flip(small[1].swapaxes(0, 1), 0)])
        small = small.reshape(2, 2, 2, 2, 2, lines, 128)
        for axis, index in ((3, at[3] // 2), (4, at[3] % 2)):
            small = jnp.where(index == 0, small, jnp.flip(small, axis))
        small = small.swapaxes(3, 4).reshape(8 * far, lines, 128)
        note = jnp.zeros((8 * far, rows, 128), BF16).at[:, :lines].set(small).reshape(width, 128)
        qkv_send_x, qkv_keep_x, qkv_send_y, qkv_keep_y = by(qkv_grads(far, at, x, x_got, keep, got, (note,)))
        qkv_send_x, qkv_send_y, late_xy, late_yx = together(qkv_send_x, qkv_send_y, late_xy, late_yx)
        qkv_x, qkv_y = swap(qkv_send_x, X), swap(qkv_send_y, Y)
        late_sum = color_sums(late_keep_x, late_keep_y, late_x, late_y, late_xy, late_yx)
        late_lo = swap_far(late_sum[2:], 1)
        qkv_x, qkv_y, down_part = together(qkv_x, qkv_y, down_part)
        qkv_xy, qkv_yx = color_nexts(qkv_keep_x, qkv_keep_y, qkv_x, qkv_y)
        qkv_xy, qkv_yx, down_part, *both = together(qkv_xy, qkv_yx, down_part, *keep, *send)
        keep, send = both[:3], both[3:]
        qkv_xy, qkv_yx = swap(qkv_xy, Y), swap(qkv_yx, X)
        down_y, down_x, down_xy = swap(down_part[1, 0], Y), swap(down_part[0, 1], X), swap_both(down_part[1, 1])
        qkv_xy, qkv_yx, late_lo = together(qkv_xy, qkv_yx, late_lo)
        qkv_sum = color_sums(qkv_keep_x, qkv_keep_y, qkv_x, qkv_y, qkv_xy, qkv_yx)
        qkv_sum, late_sum = together(qkv_sum, added(late_sum[:2], late_lo))
        qkv_lo, late_hi = swap_far(qkv_sum[2:], 1), swap_far(late_sum[1], 2)
        qkv_lo, late_hi = together(qkv_lo, late_hi)
        qkv_sum = added(qkv_sum[:2], qkv_lo)
        qkv_sum = added(qkv_sum[0], swap_far(qkv_sum[1], 2))
        late_sum = added(late_sum[0], late_hi)
        late_sum, down_y, down_x, down_xy = together(late_sum, down_y, down_x, down_xy)
        down_sum = down_part[0, 0].astype(F32) + down_y.astype(F32) + down_x.astype(F32) + down_xy.astype(F32)
    inputs_grad = nt(cat([*keep, *send], 1), qkv_full)
    inputs_grad = (grad_one + inputs_grad).astype(BF16)[None]
    wide = hidden // 2
    if far is not None:
        qkv_sum, late_sum = together(qkv_sum, late_sum)
    left, right = own_rows(core, late_sum)
    up_sum = jnp.stack([v[:, :wide].reshape(rows, blocks, piece) for v in (left, right)], 2).reshape(rows, hidden).astype(F32)
    out_sum = cat([left[:, wide:], right[:, wide:]], 1).astype(F32)
    mine, send = choose(core, qkv_sum[0], qkv_sum[1])
    got = swap(send, CORE)
    left, right = choose(core, mine[:, : 3 * near], got[:, : 3 * near])
    if far is not None:
        small_sum = (mine[:lines, 3 * near :].astype(F32) + got[:lines, 3 * near :].astype(F32)).reshape(-1)
    qkv_sum = jnp.stack([v.reshape(rows, 3, near) for v in (left, right)], 2).reshape(rows, 3 * width).astype(F32)
    s = [small_sum[each * i : each * i + each] for i in range(8)]
    return (
        result[None], inputs_grad, qkv_sum, s[0], s[1], out_sum, s[2], s[3], s[4], up_sum, small_sum[8 * each :], down_sum, s[5], s[6], s[7],
    )


def solution(mesh):
    devices = mesh.devices
    split = jax.sharding.Mesh(devices.reshape(devices.shape[0] // 4, 2, 2, devices.shape[1]), ALL)
    rows, vec = P(ALL, None), P(ALL)
    tokens = P(CORE, CTX, None)
    return jax.shard_map(
        shards,
        mesh=split,
        in_specs=(tokens, P(CORE, None), tokens, rows, vec, vec, rows, vec, vec, vec, rows, vec, rows, vec, vec, vec),
        out_specs=(tokens, tokens, rows, vec, vec, rows, vec, vec, vec, rows, vec, rows, vec, vec, vec),
        check_vma=False,
    )
```

```python
import functools

import jax
import jax.numpy as jnp
from jax import lax
from jax.experimental import pallas as pl
from jax.experimental.pallas import tpu as pltpu
from jax.sharding import PartitionSpec as P

H = 16
HD = 64
WINDOW = 1024
HALF = WINDOW // 2
ROWS = 256
NARROW = 128
PAIR = 2 * HD
FILL = -1e30
EPS = 1e-05
HIDDEN_BLOCK = 128
F32 = jnp.float32
BF16 = jnp.bfloat16
VMEM_BYTES = 56 * 1024 * 1024
SMEM = pl.BlockSpec(memory_space=pltpu.SMEM)
ANY = pl.BlockSpec(memory_space=pl.ANY)
VMEM = pl.BlockSpec(memory_space=pltpu.VMEM)


def nn(a, b):
    return lax.dot_general(a, b, (((1,), (0,)), ((), ())), preferred_element_type=F32)


def nt(a, b):
    return lax.dot_general(a, b, (((1,), (1,)), ((), ())), preferred_element_type=F32)


def tn(a, b):
    return lax.dot_general(a, b, (((0,), (0,)), ((), ())), preferred_element_type=F32)


def cat(parts, axis):
    return jnp.concatenate(parts, axis=axis)


def cost(us):
    return pl.CostEstimate(flops=int(us * 1.0e9), bytes_accessed=int(us * 3.5e6), transcendentals=0)


def params():
    return pltpu.CompilerParams(vmem_limit_bytes=VMEM_BYTES)


def head_masks(scale):
    lane = lax.broadcasted_iota(jnp.int32, (1, PAIR), 1)
    first = jnp.where(lane < HD, scale, 0.0).astype(F32)
    second = jnp.where(lane < HD, 0.0, scale).astype(F32)
    return first.astype(BF16), second.astype(BF16)


def stacked(values, masks):
    return cat([values * masks[0], values * masks[1]], 0)


def strip(i, tokens, rows=ROWS):
    return slice(rows * i, rows * i + tokens + rows)


def put_rows(ref, cols, pair):
    head = lax.broadcasted_iota(jnp.int32, (H, 1), 0) - 2 * pl.program_id(0)
    ref[:, cols] = jnp.where(head == 0, pair[0], jnp.where(head == 1, pair[1], ref[:, cols]))


def take_row(values, h, pair=None):
    head = lax.broadcasted_iota(jnp.int32, (H, 1), 0) - 2 * (pl.program_id(0) if pair is None else pair)
    return jnp.sum(jnp.where(head == h, values, 0.0), axis=0, keepdims=True)


def attend_kernel(q_ref, ko_ref, kp_ref, kn_ref, vo_ref, vp_ref, vn_ref, bo_ref, bh_ref, out_ref, lse_ref, kh, vh):
    tokens = q_ref.shape[0]
    kh[:tokens] = kp_ref[...]
    kh[tokens:] = kn_ref[...]
    ones = head_masks(1.0)
    vh[:tokens] = vp_ref[...]
    vh[tokens:] = vn_ref[...]
    vo = stacked(vo_ref[...], ones)
    scaled = head_masks(HD ** -0.5)
    lane = lax.broadcasted_iota(jnp.int32, (ROWS, PAIR), 1)
    for i in range(tokens // ROWS):
        rows = slice(ROWS * i, ROWS * i + ROWS)
        window = strip(i, tokens)
        q = q_ref[rows]
        own_parts, halo_parts, totals, logs = [], [], [], []
        for mask in scaled:
            qm = q * mask
            so = nt(qm, ko_ref[...]) + bo_ref[rows]
            sh = nt(qm, kh[window]) + bh_ref[i]
            peak = jnp.maximum(jnp.max(so, axis=1, keepdims=True), jnp.max(sh, axis=1, keepdims=True))
            po = jnp.exp(so - peak)
            ph = jnp.exp(sh - peak)
            total = jnp.sum(po, axis=1, keepdims=True) + jnp.sum(ph, axis=1, keepdims=True)
            own_parts.append(po.astype(BF16))
            halo_parts.append(ph.astype(BF16))
            totals.append(1.0 / total)
            logs.append((peak + jnp.log(total)).T)
        out = nn(cat(own_parts, 1), vo) + nn(cat(halo_parts, 1), stacked(vh[window], ones))
        out = out * jnp.where(lane < HD, totals[0], totals[1])
        out_ref[rows] = out.astype(BF16)
        put_rows(lse_ref, rows, logs)


def attend(mixed, before, after, bias_own, bias_halo):
    tokens, width = mixed.shape[0], mixed.shape[1] // 3
    pairs = width // PAIR

    near = pairs // 2

    def column(part):
        return pl.BlockSpec((tokens, PAIR), lambda p: (0, (p // near * 3 + part) * near + p % near))

    whole = lambda shape: pl.BlockSpec(shape, lambda p: (0,) * len(shape))
    return pl.pallas_call(
        attend_kernel,
        grid=(pairs,),
        in_specs=[column(0), column(1), column(1), column(1), column(2), column(2), column(2), whole(bias_own.shape), whole(bias_halo.shape)],
        out_specs=[pl.BlockSpec((tokens, PAIR), lambda p: (0, p)), whole((H, tokens))],
        out_shape=[jax.ShapeDtypeStruct((tokens, width), BF16), jax.ShapeDtypeStruct((H, tokens), F32)],
        scratch_shapes=[pltpu.VMEM((2 * tokens, PAIR), BF16), pltpu.VMEM((2 * tokens, PAIR), BF16)],
        compiler_params=params(),
        cost_estimate=cost(0.48),
        name="attend",
    )(mixed, mixed, before, after, mixed, before, after, bias_own, bias_halo)


def own_grad_kernel(q_ref, ko_ref, kp_ref, kn_ref, vo_ref, vp_ref, vn_ref, do_ref, log_ref, mean_ref, bo_ref, bh_ref, dq_keep, dq_send, dkv_ref, sum_ref, kh, vh, dq_ref):
    tokens = q_ref.shape[0]
    kh[:tokens] = kp_ref[...]
    kh[tokens:] = kn_ref[...]
    vh[:tokens] = vp_ref[...]
    vh[tokens:] = vn_ref[...]
    ones = head_masks(1.0)
    scaled = head_masks(HD ** -0.5)
    k_own = ko_ref[...]
    v_own = vo_ref[...]
    k_pair = stacked(k_own, scaled)
    log_rows = [take_row(log_ref[...], h) for h in range(2)]
    mean_rows = [take_row(mean_ref[...], h) for h in range(2)]
    chunk = ROWS
    for c in range(tokens // chunk):
        cols = slice(chunk * c, chunk * c + chunk)
        q = q_ref[cols]
        do = do_ref[cols]
        probs, grads, qs, dos = [], [], [], []
        for h in range(2):
            qm = q * scaled[h]
            dm = do * ones[h]
            st = nt(k_own, qm) + bo_ref[:, cols]
            pt = jnp.exp(st - log_rows[h][:, cols])
            gt = pt * (nt(v_own, dm) - mean_rows[h][:, cols])
            probs.append(pt.astype(BF16))
            grads.append(gt.astype(BF16))
            qs.append(qm)
            dos.append(dm)
        dv = nn(cat(probs, 1), cat(dos, 0))
        dk = nn(cat(grads, 1), cat(qs, 0))
        if c == 0:
            dkv_ref[0, 0] = dk
            dkv_ref[0, 1] = dv
        else:
            dkv_ref[0, 0] += dk
            dkv_ref[0, 1] += dv
        dq_own = tn(cat(grads, 0), k_pair)
        for r in range(chunk // ROWS):
            i = c * (chunk // ROWS) + r
            rows = slice(ROWS * i, ROWS * i + ROWS)
            window = strip(i, tokens)
            halo = []
            for h in range(2):
                qm = q[ROWS * r : ROWS * r + ROWS] * scaled[h]
                dm = do[ROWS * r : ROWS * r + ROWS] * ones[h]
                s = nt(qm, kh[window]) + bh_ref[i]
                p = jnp.exp(s - log_rows[h][:, rows].T)
                halo.append((p * (nt(dm, vh[window]) - mean_rows[h][:, rows].T)).astype(BF16))
            dq = dq_own[ROWS * r : ROWS * r + ROWS] + nn(cat(halo, 1), stacked(kh[window], scaled))
            dq = dq.astype(BF16)
            dq_ref[rows] = dq
            sum_ref[...] = column_sum(dq.astype(F32)) + (sum_ref[...] if i else 0.0)

    @pl.when(pl.program_id(0) < pl.num_programs(0) // 2)
    def _():
        dq_keep[...] = dq_ref[...]

    @pl.when(pl.program_id(0) >= pl.num_programs(0) // 2)
    def _():
        dq_send[...] = dq_ref[...]


def own_grads(mixed, before, after, payload, logs, means, bias_own, bias_halo):
    tokens, width = mixed.shape[0], payload.shape[1]
    pairs = width // PAIR

    near = pairs // 2

    def column(part):
        return pl.BlockSpec((tokens, PAIR), lambda p: (0, (p // near * 3 + part) * near + p % near))

    whole = lambda shape: pl.BlockSpec(shape, lambda p: (0,) * len(shape))
    block = pl.BlockSpec((tokens, PAIR), lambda p: (0, p))
    return pl.pallas_call(
        own_grad_kernel,
        grid=(pairs,),
        in_specs=[column(0), column(1), column(1), column(1), column(2), column(2), column(2), block, whole(logs.shape), whole(means.shape), whole(bias_own.shape), whole(bias_halo.shape)],
        out_specs=[
            pl.BlockSpec((tokens, PAIR), lambda p: (0, jnp.minimum(p, near - 1))),
            pl.BlockSpec((tokens, PAIR), lambda p: (0, jnp.maximum(p - near, 0))),
            pl.BlockSpec((1, 2, tokens, PAIR), lambda p: (p // near, 0, 0, p % near)),
            pl.BlockSpec((1, PAIR), lambda p: (0, p)),
        ],
        out_shape=[
            jax.ShapeDtypeStruct((tokens, width // 2), BF16),
            jax.ShapeDtypeStruct((tokens, width // 2), BF16),
            jax.ShapeDtypeStruct((2, 2, tokens, width // 2), F32),
            jax.ShapeDtypeStruct((1, width), F32),
        ],
        scratch_shapes=[pltpu.VMEM((2 * tokens, PAIR), BF16), pltpu.VMEM((2 * tokens, PAIR), BF16), pltpu.VMEM((tokens, PAIR), BF16)],
        compiler_params=params(),
        cost_estimate=cost(27.5),
        name="own_grads",
    )(mixed, mixed, before, after, mixed, before, after, payload, logs, means, bias_own, bias_halo)


def halo_grad_kernel(half, ko_ref, vo_ref, qp_ref, qn_ref, dp_ref, dn_ref, lp0, lp1, lp2, ln0, ln1, ln2, bh_ref, dkv_in, dk_ref, dv_ref, sum_ref, qh, dh, lh):
    tokens = ko_ref.shape[0]
    qh[:tokens] = qp_ref[...]
    qh[tokens:] = qn_ref[...]
    dh[:tokens] = dp_ref[...]
    dh[tokens:] = dn_ref[...]
    for first, refs in ((0, (lp0, lp1, lp2)), (tokens, (ln0, ln1, ln2))):
        table = refs[0][...].astype(F32) + refs[1][...].astype(F32) + refs[2][...].astype(F32)
        for h in range(2):
            row = take_row(table, h, pl.program_id(0) + half * pl.num_programs(0))
            lh[0, h : h + 1, first : first + tokens] = row[:, :tokens]
            lh[1, h : h + 1, first : first + tokens] = row[:, tokens:]
    ones = head_masks(1.0)
    scaled = head_masks(HD ** -0.5)
    for j in range(tokens // NARROW):
        rows = slice(NARROW * j, NARROW * j + NARROW)
        window = strip(j, tokens, NARROW)
        q = qh[window]
        do = dh[window]
        k = ko_ref[rows]
        v = vo_ref[rows]
        probs, grads, qs, dos = [], [], [], []
        for h in range(2):
            qm = q * scaled[h]
            dm = do * ones[h]
            st = nt(k, qm) + bh_ref[j]
            pt = jnp.exp(st - lh[0, h : h + 1, window])
            gt = pt * (nt(v, dm) - lh[1, h : h + 1, window])
            probs.append(pt.astype(BF16))
            grads.append(gt.astype(BF16))
            qs.append(qm)
            dos.append(dm)
        dk_ref[rows] = (dkv_in[0, 0, rows] + nn(cat(grads, 1), cat(qs, 0))).astype(BF16)
        dv = (dkv_in[0, 1, rows] + nn(cat(probs, 1), cat(dos, 0))).astype(BF16)
        dv_ref[rows] = dv
        sum_ref[...] = column_sum(dv.astype(F32)) + (sum_ref[...] if j else 0.0)


def halo_grads(mixed, before, after, grad_before, grad_after, bias_halo, dkv, half):
    tokens, width = dkv.shape[2], 2 * dkv.shape[3]
    near = width // PAIR // 2

    def column(part):
        return pl.BlockSpec((tokens, PAIR), lambda p: (0, (half * 3 + part) * near + p))

    whole = lambda shape: pl.BlockSpec(shape, lambda p: (0,) * len(shape))
    both = pl.BlockSpec((1, 2, tokens, PAIR), lambda p: (half, 0, 0, p))
    tables = [pl.BlockSpec((H, width), lambda p, k=k: (tokens // H + k, 0)) for k in range(3)]
    block = pl.BlockSpec((tokens, PAIR), lambda p: (0, half * near + p))
    made = pl.BlockSpec((tokens, PAIR), lambda p: (0, p))
    return pl.pallas_call(
        functools.partial(halo_grad_kernel, half),
        grid=(near,),
        in_specs=[column(1), column(2), column(0), column(0), block, block] + tables + tables + [whole(bias_halo.shape), both],
        out_specs=[made, made, pl.BlockSpec((1, PAIR), lambda p: (0, p))],
        out_shape=[jax.ShapeDtypeStruct((tokens, width // 2), BF16)] * 2 + [jax.ShapeDtypeStruct((1, width // 2), F32)],
        scratch_shapes=[
            pltpu.VMEM((2 * tokens, PAIR), BF16),
            pltpu.VMEM((2 * tokens, PAIR), BF16),
            pltpu.VMEM((2, 2, 2 * tokens), F32),
        ],
        compiler_params=params(),
        cost_estimate=cost(0.05),
        name="halo_grads",
    )(mixed, mixed, before, after, grad_before, grad_after, *[grad_before] * 3, *[grad_after] * 3, bias_halo, dkv)


def mask_biases(segments, place, blocks, tokens):
    line = cat([jnp.full((tokens,), -1, jnp.int32), segments, jnp.full((tokens,), -1, jnp.int32)], 0)
    near = lax.dynamic_slice_in_dim(line, place * tokens, 3 * tokens)
    own = near[tokens : 2 * tokens]
    bias_own = jnp.where(own[:, None] == own[None, :], 0.0, FILL).astype(F32)
    halo = cat([near[:tokens], near[2 * tokens :]], 0)
    at = jnp.arange(tokens, dtype=jnp.int32)
    halo_at = cat([at - tokens, at + tokens], 0)
    allowed = (own[:, None] == halo[None, :]) & (jnp.abs(halo_at[None, :] - at[:, None]) < HALF)
    bias = jnp.where(allowed, 0.0, FILL).astype(F32)
    strips = [jnp.stack([bias[r * i : r * i + r, strip(i, tokens, r)] for i in range(tokens // r)]) for r in (ROWS, NARROW)]
    return bias_own, *strips


def normalized(values):
    average = jnp.mean(values, axis=1, keepdims=True)
    centered = values - average
    spread = jnp.mean(centered * centered, axis=1, keepdims=True)
    inverse = lax.rsqrt(spread + EPS)
    return centered * inverse, inverse


def norm_back(grad, gain, hat, inverse):
    scaled = grad * gain
    return inverse * (
        scaled
        - jnp.mean(scaled, axis=1, keepdims=True)
        - hat * jnp.mean(scaled * hat, axis=1, keepdims=True)
    )


def column_sum(values):
    return jnp.sum(values, axis=0, keepdims=True)


def part_blocks(at_ref, order, second, far):
    for first in range(2):
        rel = {order[-2]: first, order[-1]: second}
        y = jnp.bitwise_xor(at_ref[0], rel["y"])
        x = jnp.bitwise_xor(at_ref[1], rel["x"])
        for i in range(far):
            z = jnp.bitwise_xor(at_ref[3], (i % 2) * 2 + i // 2) if order[0] == "z" else i
            yield first, i, (z * 2 + y) * 2 + x


def start_all(copies):
    for copy in copies:
        copy.start()


def wait_all(copies):
    for copy in copies:
        copy.wait()


def block_place(at_ref, order, z, y, x, far):
    where = {"z": (z, far), "y": (jnp.bitwise_xor(at_ref[0], y), 2), "x": (jnp.bitwise_xor(at_ref[1], x), 2)}
    to = 0
    for axis in order:
        to = to * where[axis][1] + where[axis][0]
    return to


def prepare_kernel(at_ref, qkv_ref, out_ref, up_ref, *refs):
    vectors, mine_ref, send_ref, note_ref = refs[:-3], *refs[-3:]
    width = out_ref.shape[1]
    place = 0
    for ref, piece in ((qkv_ref, width // 2), (out_ref, width // 2), (up_ref, HIDDEN_BLOCK)):
        for i in range(0, ref.shape[1], 2 * piece):
            mine_ref[:, place : place + piece] = ref[:, pl.ds(pl.multiple_of(i + at_ref[2] * piece, piece), piece)]
            send_ref[:, place : place + piece] = ref[:, pl.ds(pl.multiple_of(i + (1 - at_ref[2]) * piece, piece), piece)]
            place += piece
    line = cat([v[...].astype(F32) for v in vectors], 1).astype(BF16)
    note_ref[...] = jnp.zeros_like(note_ref)
    for i in range(line.shape[1] // 128):
        note_ref[i : i + 1] = line[:, i * 128 : i * 128 + 128]


def prepare(at, qkv, out, up, vectors):
    rows = qkv.shape[0]
    columns = (qkv.shape[1] + out.shape[1] + up.shape[1]) // 2
    half = jax.ShapeDtypeStruct((rows, columns), BF16)
    return pl.pallas_call(
        prepare_kernel,
        in_specs=[SMEM] + [VMEM] * (3 + len(vectors)),
        out_shape=[half, half, jax.ShapeDtypeStruct((rows, 128), BF16)],
        compiler_params=params(),
        cost_estimate=cost(0.04),
        name="prepare",
    )(at, qkv, out, up, *[v[None] for v in vectors])


def arrange_kernel(at_ref, mine_ref, got_ref, note_ref, block_ref, up_ref):
    rows, cut = mine_ref.shape[0], block_ref.shape[2] - 128
    block_ref[0, :, cut:] = note_ref[...]
    block_ref[1, :, cut:] = jnp.zeros_like(note_ref)

    def lay(first, second):
        for i, ref in ((0, first), (1, second)):
            block_ref[i, :, :cut] = ref[:, :cut]
            up_ref[i * rows : i * rows + rows] = ref[:, cut:]

    @pl.when(at_ref[2] == 0)
    def _():
        lay(mine_ref, got_ref)

    @pl.when(at_ref[2] != 0)
    def _():
        lay(got_ref, mine_ref)


def arrange(at, mine, got, note, hidden):
    rows, columns = mine.shape
    return pl.pallas_call(
        arrange_kernel,
        in_specs=[SMEM] + [VMEM] * 3,
        out_shape=[
            jax.ShapeDtypeStruct((2, rows, columns - hidden // 2 + 128), BF16),
            jax.ShapeDtypeStruct((2 * rows, hidden // 2), BF16),
        ],
        compiler_params=params(),
        cost_estimate=cost(0.04),
        name="arrange",
    )(at, mine, got, note)


def first_copies(refs, qkv, out, sems, at_ref, far):
    width, columns = qkv.shape
    half, near = width // 2, columns // 2
    copies = []

    def add(source, target):
        copies.append(pltpu.make_async_copy(source, target, sems.at[len(copies)]))

    def column(core):
        return pl.ds(pl.multiple_of(jnp.bitwise_xor(at_ref[2], core) * half, half), half)

    for core in range(2):
        if far is None:
            add(refs[core], qkv.at[:, pl.ds(core * near, near)])
            for part in range(2):
                row = pl.ds(pl.multiple_of(jnp.bitwise_xor(at_ref[2], part) * half, half), half)
                add(refs[2 + core].at[pl.ds(part * half, half)], out.at[row, column(core)])
            continue
        rows = width // (8 * far)
        for color, order in enumerate(("zyx", "zxy")):
            for second in range(2):
                ref = refs[core * 4 + color * 2 + second]
                for first, z, block in part_blocks(at_ref, order, second, far):
                    row = (block * 2 + color) * rows
                    add(ref.at[first, z, :, pl.ds(0, near)], qkv.at[pl.ds(pl.multiple_of(row, rows), rows), pl.ds(core * near, near)])
                    row = jnp.bitwise_xor(row, at_ref[2] * half)
                    add(ref.at[first, z, :, pl.ds(near, half)], out.at[pl.ds(pl.multiple_of(row, rows), rows), column(core)])
    return copies


def project_kernel(far, parts, *refs):
    at_ref, refs = refs[0], refs[1:]
    part_refs, refs = refs[:parts], refs[parts:]
    own_ref, row_ref, own_out, qkv_out, out_out, qkv, out, sems, out_sems = refs
    copies = first_copies(part_refs, qkv, out, sems, at_ref, far)
    start_all(copies)
    wait_all(copies)
    keep = [pltpu.make_async_copy(qkv, qkv_out, out_sems.at[0]), pltpu.make_async_copy(out, out_out, out_sems.at[1])]
    start_all(keep)
    chunk = 512

    def body(j, carry):
        cols = pl.ds(pl.multiple_of(j * chunk, chunk), chunk)
        own_out[:, cols] = (nn(own_ref[...], qkv[:, cols]) + row_ref[:, cols]).astype(BF16)
        return carry

    lax.fori_loop(0, qkv.shape[1] // chunk, body, 0)
    wait_all(keep)


def copy_count(far, each):
    return 2 if far is None else 8 * far * each


def project(far, at, parts, x, row):
    tokens, width = x.shape
    columns = row.shape[1]
    mixed = jax.ShapeDtypeStruct((tokens, columns), BF16)
    return pl.pallas_call(
        functools.partial(project_kernel, far, len(parts)),
        in_specs=[SMEM] + [ANY] * len(parts) + [VMEM] * 2,
        out_specs=[VMEM, ANY, ANY],
        out_shape=[mixed, jax.ShapeDtypeStruct((width, columns), BF16), jax.ShapeDtypeStruct((width, width), BF16)],
        scratch_shapes=[
            pltpu.VMEM((width, columns), BF16),
            pltpu.VMEM((width, width), BF16),
            pltpu.SemaphoreType.DMA((6 if far is None else 64 * far,)),
            pltpu.SemaphoreType.DMA((2,)),
        ],
        compiler_params=params(),
        cost_estimate=cost(0.26),
        name="project",
    )(at, *parts, x, row)


def project_more_kernel(before_ref, after_ref, w_ref, row_ref, before_out, after_out):
    for source, target in ((before_ref, before_out), (after_ref, after_out)):
        target[...] = (nn(source[...], w_ref[...]) + row_ref[...]).astype(BF16)


def project_more(before, after, full, row, chunk=512):
    tokens, width = before.shape
    columns = full.shape[1]
    whole = pl.BlockSpec((tokens, width), lambda i: (0, 0))
    block = pl.BlockSpec((tokens, chunk), lambda i: (0, i))
    return pl.pallas_call(
        project_more_kernel,
        grid=(columns // chunk,),
        in_specs=[whole, whole, pl.BlockSpec((width, chunk), lambda i: (0, i)), pl.BlockSpec((1, chunk), lambda i: (0, i))],
        out_specs=[block, block],
        out_shape=[jax.ShapeDtypeStruct((tokens, columns), BF16)] * 2,
        compiler_params=params(),
        cost_estimate=cost(0.214),
        name="project_more",
    )(before, after, full, row)


def out_kernel(heads_ref, w_ref, x_ref, vec_ref, hat_ref, inv_ref, low_ref):
    branch = nn(heads_ref[...], w_ref[...]) + vec_ref[0:1]
    hat, inverse = normalized(x_ref[...].astype(F32) + branch)
    hat_ref[...] = hat
    inv_ref[...] = inverse
    low_ref[...] = (hat * vec_ref[1:2] + vec_ref[2:3]).astype(BF16)


def out_project(heads, out_full, x, vectors):
    tokens, width = heads.shape
    rows = tokens // 2
    block = pl.BlockSpec((rows, width), lambda i: (i, 0))
    return pl.pallas_call(
        out_kernel,
        grid=(2,),
        in_specs=[block, pl.BlockSpec(out_full.shape, lambda i: (0, 0)), block, pl.BlockSpec(vectors.shape, lambda i: (0, 0))],
        out_specs=[block, pl.BlockSpec((rows, 1), lambda i: (i, 0)), block],
        out_shape=[
            jax.ShapeDtypeStruct((tokens, width), F32),
            jax.ShapeDtypeStruct((tokens, 1), F32),
            jax.ShapeDtypeStruct((tokens, width), BF16),
        ],
        compiler_params=params(),
        cost_estimate=cost(0.114),
        name="out_project",
    )(heads, out_full, x, vectors)


def up_copies(refs, full, sems, at_ref, far):
    width, half = full.shape[0], full.shape[1] // 2
    copies = []
    for core in range(2):
        cols = pl.ds(core * half, half)
        if far is None:
            copies.append(pltpu.make_async_copy(refs[core], full.at[:, cols], sems.at[core]))
            continue
        rows = width // (4 * far)
        for second in range(2):
            ref = refs[core * 2 + second]
            for first, z, block in part_blocks(at_ref, "zyx", second, far):
                to = full.at[pl.ds(pl.multiple_of(block * rows, rows), rows), cols]
                copies.append(pltpu.make_async_copy(ref.at[first, z], to, sems.at[len(copies)]))
    return copies


def down_copies(refs, full, sems, at_ref, far):
    half = full.shape[0] // 2
    copies = []
    for core in range(2):
        if far is None:
            copies.append(pltpu.make_async_copy(refs[core], full.at[pl.ds(core * half, half)], sems.at[core]))
            continue
        rows = half // (4 * far)
        for second in range(2):
            ref = refs[core * 2 + second]
            for first, z, block in part_blocks(at_ref, "xy", second, far):
                to = full.at[pl.ds(pl.multiple_of(core * half + block * rows, rows), rows)]
                copies.append(pltpu.make_async_copy(ref.at[first, z], to, sems.at[len(copies)]))
    return copies


def middle_kernel(far, ups, downs, *refs):
    at_ref, refs = refs[0], refs[1:]
    up_refs, down_refs, refs = refs[:ups], refs[ups : ups + downs], refs[ups + downs :]
    low_ref, row_ref, vec_ref, log_ref, inv_ref, hat_in, dy_in, heads_in, out_in = refs[:9]
    act_out, act_send, result_out, glow_out, lift_out, lift_send, one_out, mine_out, send_out, pay_out, mean_ref, row_sums, two_sums, one_sums = refs[9:23]
    up, down, out, hat, dy, heads, act, slope, result, glow, total, branch, sides, payload, up_sems, down_sems, in_sems, out_sems = refs[23:]
    tokens, width = low_ref.shape
    half = up.shape[1] // 2
    chunk = half // 2
    steps = 2 * half // chunk
    from_up = up_copies(up_refs, up, up_sems, at_ref, far)
    from_down = down_copies(down_refs, down, down_sems, at_ref, far)
    loads = [pltpu.make_async_copy(*pair, in_sems.at[i]) for i, pair in enumerate(((hat_in, hat), (dy_in, dy), (out_in, out), (heads_in, heads)))]
    start_all(from_up)
    start_all(from_down)
    start_all(loads)
    stores = []

    def store(source, target):
        copy = pltpu.make_async_copy(source, target, out_sems.at[len(stores)])
        stores.append(copy)
        copy.start()

    def cols(i):
        return pl.ds(pl.multiple_of(i * chunk, chunk), chunk)

    def raise_one(i):
        lifted = nn(low_ref[...], up[:, cols(i)]) + row_ref[:, cols(i)]
        phi = 0.5 * (1.0 + lax.erf(lifted * (0.5 ** 0.5)))
        density = jnp.exp(lifted * lifted * -0.5) * 0.3989422804014327
        act[:, cols(i)] = (lifted * phi).astype(BF16)
        slope[:, cols(i)] = (phi + lifted * density).astype(BF16)

    def settle_one(i):
        total[...] += nn(act[:, cols(i)], down[cols(i)])

    half_up, half_down = len(from_up) // 2, len(from_down) // 2
    wait_all(from_up[:half_up])
    raise_one(0)
    raise_one(1)
    wait_all(from_up[half_up:])
    wait_all(from_down[:half_down])
    total[...] = nn(act[:, cols(0)], down[cols(0)])

    def both(i, carry):
        raise_one(i)
        settle_one(i - 1)
        return carry

    both(2, 0)
    wait_all(from_down[half_down:])
    both(3, 0)
    settle_one(steps - 1)
    store(act.at[:, pl.ds(0, half)], act_out)
    store(act.at[:, pl.ds(half, half)], act_send)
    wait_all(loads)

    rows = 128
    for n in range(tokens // rows):
        at = slice(rows * n, rows * n + rows)
        first = hat[at] * vec_ref[3:4] + vec_ref[4:5]
        hat_two, inverse = normalized(first + (total[at] + vec_ref[0:1]))
        result[at] = (hat_two * vec_ref[1:2] + vec_ref[2:3]).astype(BF16)
        grad = dy[at].astype(F32)
        part = [column_sum(grad * hat_two), column_sum(grad)]
        grad = norm_back(grad, vec_ref[1:2], hat_two, inverse)
        low = grad.astype(BF16)
        total[at] = grad
        glow[at] = low
        part = cat(part + [column_sum(low.astype(F32))], 0)
        two_sums[...] = part if n == 0 else two_sums[...] + part
    store(result, result_out)
    store(glow, glow_out)

    def lower_one(i):
        value = (nt(glow[...], down[cols(i)]) * slope[:, cols(i)].astype(F32)).astype(BF16)
        slope[:, cols(i)] = value
        row_sums[:, cols(i)] = column_sum(value.astype(F32))

    def first_one(i):
        total[...] += nt(slope[:, cols(i)], up[:, cols(i)])

    lower_one(0)

    def back(i, carry):
        lower_one(i)
        first_one(i - 1)
        return carry

    lax.fori_loop(1, steps, back, 0)
    store(slope.at[:, pl.ds(0, half)], lift_out)
    store(slope.at[:, pl.ds(half, half)], lift_send)
    first_one(steps - 1)

    for n in range(tokens // rows):
        at = slice(rows * n, rows * n + rows)
        grad = total[at]
        one = norm_back(grad, vec_ref[3:4], hat[at], inv_ref[at])
        low = one.astype(BF16)
        total[at] = one
        branch[at] = low
        part = cat([column_sum(grad * hat[at]), column_sum(grad), column_sum(low.astype(F32))], 0)
        one_sums[...] = part if n == 0 else one_sums[...] + part
    store(total, one_out)
    middle = width // 2
    for n in range(2):
        side = pl.multiple_of(jnp.bitwise_xor(at_ref[2], n) * middle, middle)
        sides[n] = branch[:, pl.ds(side, middle)]
    store(sides.at[0], mine_out)
    store(sides.at[1], send_out)

    head = lax.broadcasted_iota(jnp.int32, (H, width), 1) // HD
    pick = jnp.where(head == lax.broadcasted_iota(jnp.int32, (H, width), 0), 1.0, 0.0).astype(F32)
    for n in range(4):
        part = slice(width // 4 * n, width // 4 * (n + 1))
        grad = nt(branch[...], out[part]).astype(BF16)
        payload[:tokens, part] = grad
        product = grad.astype(F32) * heads[:, part].astype(F32)
        means = lax.dot_general(
            pick[:, part], product, (((1,), (1,)), ((), ())), precision=lax.Precision.HIGHEST, preferred_element_type=F32
        )
        mean_ref[...] = means if n == 0 else mean_ref[...] + means
    rest = cat([log_ref[...], mean_ref[...]], 1)
    for n in range(3):
        term = rest.astype(BF16)
        rest = rest - term.astype(F32)
        payload[tokens + H * n : tokens + H * n + H] = term
    store(payload, pay_out)
    wait_all(stores)


def middle(far, at, up_parts, down_parts, low, row, vectors, logs, inverse, hat, dy, heads, out_full):
    tokens, width = low.shape
    hidden = row.shape[1]
    half = hidden // 2
    shape = jax.ShapeDtypeStruct
    pay_shape = (tokens + 3 * H, width)
    return pl.pallas_call(
        functools.partial(middle_kernel, far, len(up_parts), len(down_parts)),
        in_specs=[SMEM] + [ANY] * (len(up_parts) + len(down_parts)) + [VMEM] * 5 + [ANY] * 4,
        out_specs=[ANY] * 10 + [VMEM] * 4,
        out_shape=[
            shape((tokens, half), BF16),
            shape((tokens, half), BF16),
            shape((tokens, width), BF16),
            shape((tokens, width), BF16),
            shape((tokens, half), BF16),
            shape((tokens, half), BF16),
            shape((tokens, width), F32),
            shape((tokens, width // 2), BF16),
            shape((tokens, width // 2), BF16),
            shape(pay_shape, BF16),
            shape((H, tokens), F32),
            shape((1, hidden), F32),
            shape((3, width), F32),
            shape((3, width), F32),
        ],
        scratch_shapes=[
            pltpu.VMEM((width, hidden), BF16),
            pltpu.VMEM((hidden, width), BF16),
            pltpu.VMEM((width, width), BF16),
            pltpu.VMEM((tokens, width), F32),
            pltpu.VMEM((tokens, width), BF16),
            pltpu.VMEM((tokens, width), BF16),
            pltpu.VMEM((tokens, hidden), BF16),
            pltpu.VMEM((tokens, hidden), BF16),
            pltpu.VMEM((tokens, width), BF16),
            pltpu.VMEM((tokens, width), BF16),
            pltpu.VMEM((tokens, width), F32),
            pltpu.VMEM((tokens, width), BF16),
            pltpu.VMEM((2, tokens, width // 2), BF16),
            pltpu.VMEM(pay_shape, BF16),
            pltpu.SemaphoreType.DMA((copy_count(far, 2),)),
            pltpu.SemaphoreType.DMA((copy_count(far, 2),)),
            pltpu.SemaphoreType.DMA((4,)),
            pltpu.SemaphoreType.DMA((10,)),
        ],
        compiler_params=params(),
        cost_estimate=cost(45),
        name="middle",
    )(at, *up_parts, *down_parts, low, row, vectors, logs, inverse, hat, dy, heads, out_full)


def down_grad_kernel(far, at_ref, act_ref, act_got, glow_ref, glow_got, dw_ref, glows):
    tokens = glow_ref.shape[0]

    @pl.when(pl.program_id(0) == 0)
    def _():
        glows[:tokens] = glow_ref[...]
        glows[tokens:] = glow_got[...]

    dw = tn(cat([act_ref[...], act_got[...]], 0), glows[...]).astype(BF16)
    if far is None:
        dw_ref[...] = dw
        return
    rows = dw.shape[0] // 4
    for j in range(4):
        to = block_place(at_ref, "yx", 0, j // 2, j % 2, far)
        dw_ref[pl.ds(pl.multiple_of(to * rows, rows), rows)] = dw[j * rows : j * rows + rows]


def down_grads(far, at, active, act_got, glow, glow_got):
    tokens, half = active.shape
    width = glow.shape[1]
    chunk = half // 4
    whole = pl.BlockSpec((tokens, width), lambda i: (0, 0))
    block = pl.BlockSpec((tokens, chunk), lambda i: (0, i))
    return pl.pallas_call(
        functools.partial(down_grad_kernel, far),
        grid=(4,),
        in_specs=[SMEM, block, block, whole, whole],
        out_specs=pl.BlockSpec((chunk, width), lambda i: (i, 0)),
        out_shape=jax.ShapeDtypeStruct((half, width), BF16),
        scratch_shapes=[pltpu.VMEM((2 * tokens, width), BF16)],
        compiler_params=params(),
        cost_estimate=cost(8.5),
        name="down_grads",
    )(at, active, act_got, glow, glow_got)


def both_flipped(at_ref, mine_ref, got_ref, flipped, far, heads=False, distant=False):
    tokens = mine_ref.shape[0]
    for core, ref in ((0, mine_ref), (1, got_ref)):
        turned = ref[...].T
        cols = slice(core * tokens, core * tokens + tokens)
        flip = jnp.bitwise_xor(at_ref[2], core) if heads else 0
        half = turned.shape[0] // 2
        if far is None:
            for part in range(2):
                to = jnp.bitwise_xor(flip, part) * half
                flipped[pl.ds(pl.multiple_of(to, half), half), cols] = turned[part * half : part * half + half]
            continue
        rows = turned.shape[0] // (8 * far)
        for z in range(far):
            at_z = jnp.bitwise_xor(z, flip * (far // 2))
            if distant:
                away = jnp.bitwise_xor(at_z, at_ref[3])
                at_z = away % 2 * 2 + away // 2
            for y in range(2):
                for x in range(2):
                    a = ((z * 2 + y) * 2 + x) * 2 * rows
                    to_y, to_x = jnp.bitwise_xor(at_ref[0], y), jnp.bitwise_xor(at_ref[1], x)
                    first = ((1 - to_x) * 2 + to_y) * far + at_z
                    second = ((3 - to_y) * 2 + to_x) * far + at_z
                    for i, to in enumerate((first, second)):
                        to = pl.ds(pl.multiple_of(to * rows, rows), rows)
                        flipped[to, cols] = turned[a + i * rows : a + i * rows + rows]


def quarter_specs(rows, columns, index):
    return [pl.BlockSpec((rows // 4, columns), index)] * 4


def put_quarters(refs, cols, value):
    rows = value.shape[0] // 4
    for i, ref in enumerate(refs):
        ref[:, cols] = value[i * rows : i * rows + rows]


def late_grad_kernel(far, at_ref, low_ref, low_got, heads_ref, heads_got, lift_ref, lift_got, branch_ref, branch_got, *refs):
    quarters, flipped = refs[:4], refs[4]
    step = pl.program_id(0)
    last = pl.num_programs(0) - 1

    @pl.when(step == 0)
    def _():
        both_flipped(at_ref, low_ref, low_got, flipped, far, distant=True)

    @pl.when(step < last)
    def _():
        put_quarters(quarters, slice(None), nn(flipped[...], cat([lift_ref[...], lift_got[...]], 0)).astype(BF16))

    @pl.when(step == last)
    def _():
        both_flipped(at_ref, heads_ref, heads_got, flipped, far, heads=True, distant=True)
        put_quarters(quarters, slice(None), nn(flipped[...], cat([branch_ref[...], branch_got[...]], 0)).astype(BF16))


def late_grads(far, at, low, low_got, heads, heads_got, lift, lift_got, branch, branch_got):
    tokens, width = low.shape
    chunk = branch.shape[1]
    steps = lift.shape[1] // chunk
    whole = lambda shape: pl.BlockSpec(shape, lambda i: (0, 0))
    block = pl.BlockSpec((tokens, chunk), lambda i: (0, jnp.minimum(i, steps - 1)))
    return pl.pallas_call(
        functools.partial(late_grad_kernel, far),
        grid=(steps + 1,),
        in_specs=[SMEM] + [whole((tokens, width))] * 4 + [block, block] + [whole((tokens, chunk))] * 2,
        out_specs=quarter_specs(width, chunk, lambda i: (0, i)),
        out_shape=[jax.ShapeDtypeStruct((width // 4, (steps + 1) * chunk), BF16)] * 4,
        scratch_shapes=[pltpu.VMEM((width, 2 * tokens), BF16)],
        compiler_params=params(),
        cost_estimate=cost(9),
        name="late_grads",
    )(at, low, low_got, heads, heads_got, lift, lift_got, branch, branch_got)


def qkv_grad_kernel(far, at_ref, x_ref, x_got, *refs):
    keeps, gots, refs = refs[:3], refs[3:6], refs[6:]
    note_refs, quarters, flipped = refs[:-5], refs[-5:-1], refs[-1]
    both_flipped(at_ref, x_ref, x_got, flipped, far, distant=True)
    chunk = keeps[0].shape[1]
    for n in range(3):
        dw = nn(flipped[...], cat([keeps[n][...], gots[n][...]], 0)).astype(BF16)
        put_quarters(quarters, slice(n * chunk, n * chunk + chunk), dw)
    for ref in note_refs:
        put_quarters(quarters, slice(3 * chunk, 3 * chunk + ref.shape[1]), ref[...])


def qkv_grads(far, at, x, x_got, keep, got, notes=()):
    tokens, width = x.shape
    columns = 3 * keep[0].shape[1] + sum(v.shape[1] for v in notes)
    return pl.pallas_call(
        functools.partial(qkv_grad_kernel, far),
        in_specs=[SMEM] + [VMEM] * (8 + len(notes)),
        out_shape=[jax.ShapeDtypeStruct((width // 4, columns), BF16)] * 4,
        scratch_shapes=[pltpu.VMEM((width, 2 * tokens), BF16)],
        compiler_params=params(),
        cost_estimate=cost(8.3),
        name="qkv_grads",
    )(at, x, x_got, *keep, *got, *notes)


FAR, Y, X, CORE = "far", "y", "x", "fsdp"
CTX = (FAR, Y, X)
ALL = CTX + (CORE,)


def swap(values, axis):
    return lax.ppermute(values, axis, [(0, 1), (1, 0)])


def swap_both(values):
    return lax.ppermute(values, (Y, X), [(i, 3 - i) for i in range(4)])


def swap_far(values, step):
    return lax.ppermute(values, FAR, [(i, i ^ step) for i in range(lax.axis_size(FAR))])


def together(*arrays):
    return lax.optimization_barrier(arrays)


def choose(core, left, right):
    return jnp.where(core == 0, left, right), jnp.where(core == 0, right, left)


def added(*terms):
    total = terms[0].astype(F32)
    for term in terms[1:]:
        total = total + term.astype(F32)
    return total.astype(BF16)


def own_rows(core, summed):
    mine, send = choose(core, summed[0], summed[1])
    return choose(core, mine, swap(send, CORE))


def color_nexts(keep_x, keep_y, there_x, there_y):
    return added(keep_x[1], there_x[1]), added(keep_y[1], there_y[1])


def color_sums(keep_x, keep_y, there_x, there_y, there_xy, there_yx):
    return jnp.stack([added(keep_x[0], there_x[0], there_xy), added(keep_y[0], there_y[0], there_yx)], 1)


def shards(inputs, segments, cotangent, qkv_weight, query_bias, value_bias, out_weight, out_bias, first_gain, first_shift, up_weight, up_bias, down_weight, down_bias, second_gain, second_shift):
    tokens, width = inputs.shape[1:]
    rows, hidden = up_weight.shape
    piece = down_weight.shape[0]
    near = width // 2
    blocks = lax.axis_size(CTX)
    place = lax.axis_index(CTX)
    core = lax.axis_index(CORE)
    at = jnp.stack([lax.axis_index(Y), lax.axis_index(X), core, lax.axis_index(FAR)]).astype(jnp.int32)
    far = 4 if rows % 32 == 0 and lax.axis_size(FAR) == 4 and piece == HIDDEN_BLOCK else None
    onward = [(i, i + 1) for i in range(blocks - 1)]
    back = [(i + 1, i) for i in range(blocks - 1)]

    def from_before(v):
        return lax.ppermute(v, CTX, onward)

    def from_after(v):
        return lax.ppermute(v, CTX, back)

    def own_first(v):
        return cat(choose(core, v[:, :near], v[:, near:]), 1)

    x = inputs[0]
    vectors = (query_bias, value_bias, out_bias, first_gain, first_shift, down_bias, second_gain, second_shift, up_bias)
    each = query_bias.shape[0]
    if far is None:
        split = lambda w, size: w.reshape(rows, -1, 2, size).swapaxes(0, 2).swapaxes(1, 2).reshape(2, rows, -1)
        sides = cat([split(qkv_weight, near), split(out_weight, near), split(up_weight, piece)], 2)
        mine, send = choose(core, sides[0], sides[1])
        both = cat(choose(core, mine, swap(send, CORE)), 0)
        whole = lambda v: lax.all_gather(v, CTX, axis=0, tiled=True)
        pair = lambda v: [v, swap(v, CORE)]
        qkv_parts = pair(whole(both[:, : 3 * near])) + pair(whole(both[:, 3 * near : 4 * near]))
        up_parts, down_parts = pair(whole(both[:, 4 * near :])), pair(whole(down_weight))
        x_before, x_after = from_before(x), from_after(x)
        table = lax.all_gather(cat(vectors, 0)[None], ALL, axis=0, tiled=True)
    else:
        mine, send, note = prepare(at, qkv_weight, out_weight, up_weight, vectors)
        block, up_block = arrange(at, mine, swap(send, CORE), note, hidden)
        cut = 4 * near
        lines = sum(v.shape[0] for v in vectors) // 128
        pair = jnp.stack([block, swap_far(block, 2)])
        down_pair = jnp.stack([down_weight, swap(down_weight, X)])
        pair, x_before, x_two = together(pair, from_before(x), x)
        wide = jnp.stack([pair, swap_far(pair, 1)]).reshape((4,) + block.shape)
        x_after = from_after(x_two)
        wide, up_block, down_pair, x_after = together(wide, up_block, down_pair, x_after)
        a1, b1, up_hi = swap(wide[:, 0], Y), swap(wide[:, 1], X), swap_far(up_block, 2)
        a1, b1, up_hi = together(a1, b1, up_hi)
        pair_a, pair_b, up_pair = jnp.stack([wide[:, 0], a1]), jnp.stack([wide[:, 1], b1]), jnp.stack([up_block, up_hi])
        a2, b2, up_lo = swap(pair_a, X), swap(pair_b, Y), swap_far(up_pair, 1)
        up_lo, down_pair = together(up_lo, down_pair)
        down_wide = lax.all_gather(down_pair, FAR, axis=1)
        a2, b2, up_lo = together(a2, b2, up_lo)
        first_parts = [pair_a, a2, pair_b, b2]
        qkv_parts = first_parts + [swap(p, CORE) for p in first_parts]
        up_wide = jnp.stack([up_pair, up_lo]).reshape((4,) + up_block.shape)
        up_y = swap(up_wide, Y)
        notes = jnp.stack([jnp.stack([qkv_parts[4 * c + s][:, :, :lines, cut:] for s in range(2)]) for c in range(2)])
        notes = notes.reshape(2, 2, 2, 2, 2, -1).swapaxes(3, 4)
        for axis, index in ((0, core), (1, at[1]), (2, at[0]), (3, at[3] // 2), (4, at[3] % 2)):
            notes = jnp.where(index == 0, notes, jnp.flip(notes, axis))
        table = notes.transpose(3, 4, 2, 1, 0, 5).reshape(2 * blocks, -1)

    rows_of = [table[:, each * i : each * i + each].reshape(1, width).astype(F32) for i in range(8)]
    query_row, value_row, out_row, gain_one, shift_one, down_row, gain_two, shift_two = rows_of
    up_row = table[:, 8 * each :].reshape(blocks, 2, piece).astype(F32)
    up_row = cat(choose(core, up_row[:, 0].reshape(1, -1), up_row[:, 1].reshape(1, -1)), 1)
    bias_own, bias_halo, bias_narrow = mask_biases(segments[0], place, blocks, tokens)
    query_row, value_row, gap = own_first(query_row), own_first(value_row), jnp.zeros((1, near), F32)
    qkv_row = cat([query_row[:, :near], gap, value_row[:, :near], query_row[:, near:], gap, value_row[:, near:]], 1)

    mixed, qkv_full, out_full = project(far, at, qkv_parts, x, qkv_row)
    if far is not None:
        qkv_full, up_y = together(qkv_full, up_y)
        up_pair = jnp.stack([up_wide, up_y])
        up_x, up_pair_core = swap(up_pair, X), swap(up_pair, CORE)
    before, after = project_more(x_before, x_after, qkv_full, qkv_row)
    if far is not None:
        before, down_wide = together(before, down_wide)
        down_y, down_wide_core = swap(down_wide, Y), swap(down_wide, CORE)
    heads, logs = attend(mixed, before, after, bias_own, bias_halo)
    hat, inverse, low = out_project(heads, out_full, x, cat([out_row, gain_one, shift_one], 0))
    low, x_got, heads_got = together(low, swap(x, CORE), swap(heads, CORE))
    if far is not None:
        low, up_x, up_pair_core, down_wide_core, down_y = together(low, up_x, up_pair_core, down_wide_core, down_y)
        up_parts = [up_pair, up_x, up_pair_core, swap(up_x, CORE)]
        down_parts = [down_wide, down_y, down_wide_core, swap(down_y, CORE)]
    low_got = swap(low, CORE)
    (
        active, act_send, result, glow, lift_keep, lift_send, grad_one, branch_mine, branch_send, payload, means, up_bias_part, sums_two, sums_one,
    ) = middle(
        far, at, up_parts, down_parts, low, up_row, cat([down_row, gain_two, shift_two, gain_one, shift_one], 0),
        logs, inverse, hat, cotangent[0], heads, out_full,
    )
    payload, low_got = together(payload, low_got)
    pay_before, pay_after = from_before(payload), from_after(payload)
    act_got, glow_got, lift_got, branch_got = swap(act_send, CORE), swap(glow, CORE), swap(lift_send, CORE), swap(branch_send, CORE)
    down_part = down_grads(far, at, active, act_got, glow, glow_got)
    late = late_grads(far, at, low, low_got, heads, heads_got, lift_keep, lift_got, branch_mine, branch_got)
    dq_keep, dq_send, dkv, dq_sum = own_grads(mixed, before, after, payload, logs, means, bias_own, bias_halo)
    if far is not None:
        down_part = lax.psum_scatter(down_part.reshape(far, 2, 2, piece, width), FAR, scatter_dimension=0, tiled=False)
        by = lambda parts: [v.reshape(2, far, rows, v.shape[1]) for v in parts]
        late_send_x, late_keep_x, late_send_y, late_keep_y = by(late)
        late_x, late_y, pay_before, pay_after, dkv = together(late_send_x, late_send_y, pay_before, pay_after, dkv)
        late_x, late_y = swap(late_x, X), swap(late_y, Y)
    *send, sum_send = halo_grads(mixed, before, after, pay_before, pay_after, bias_narrow, dkv, 1)
    send = [dq_send] + send
    *keep, sum_keep = halo_grads(mixed, before, after, pay_before, pay_after, bias_narrow, dkv, 0)
    if far is not None:
        late_x, late_y, sum_keep = together(late_x, late_y, sum_keep)
    keep, dv_sum = [dq_keep] + keep, cat([sum_keep, sum_send], 1)
    got = [swap(v, CORE) for v in send]
    if far is not None:
        late_xy, late_yx = color_nexts(late_keep_x, late_keep_y, late_x, late_y)
        late_xy, late_yx, *got = together(late_xy, late_yx, *got)
        late_xy, late_yx = swap(late_xy, Y), swap(late_yx, X)
    features = (own_first(dq_sum), own_first(dv_sum), sums_one[2], sums_one[0], sums_one[1], sums_two[2], sums_two[0], sums_two[1])
    small = jnp.stack([v.reshape(blocks, 2, each) for v in features], 2).reshape(blocks, 2, -1)
    sides = choose(core, up_bias_part[:, : hidden // 2], up_bias_part[:, hidden // 2 :])
    small = cat([small, jnp.stack([v.reshape(blocks, piece) for v in sides], 1)], 2)
    if far is None:
        qkv = qkv_grads(far, at, x, x_got, keep, got)
        total = lambda v: lax.psum_scatter(v, CTX, scatter_dimension=0, tiled=True)
        down_sum = total(down_part).astype(F32)
        small_sum = lax.psum_scatter(small.reshape(2 * blocks, -1), ALL, scatter_dimension=0, tiled=True)[0]
        late_sum, qkv_sum = [total(cat(v, 0)).reshape(2, rows, -1) for v in (late, qkv)]
    else:
        small = small.astype(BF16).reshape(far, 2, 2, 2, lines, 128).transpose(3, 2, 1, 0, 4, 5)
        for axis, index in ((1, at[1]), (2, at[0])):
            small = jnp.where(index == 0, small, jnp.flip(small, axis))
        small = jnp.stack([jnp.flip(small[0], 0), jnp.flip(small[1].swapaxes(0, 1), 0)])
        small = small.reshape(2, 2, 2, 2, 2, lines, 128)
        for axis, index in ((3, at[3] // 2), (4, at[3] % 2)):
            small = jnp.where(index == 0, small, jnp.flip(small, axis))
        small = small.swapaxes(3, 4).reshape(8 * far, lines, 128)
        note = jnp.zeros((8 * far, rows, 128), BF16).at[:, :lines].set(small).reshape(width, 128)
        qkv_send_x, qkv_keep_x, qkv_send_y, qkv_keep_y = by(qkv_grads(far, at, x, x_got, keep, got, (note,)))
        qkv_send_x, qkv_send_y, late_xy, late_yx = together(qkv_send_x, qkv_send_y, late_xy, late_yx)
        qkv_x, qkv_y = swap(qkv_send_x, X), swap(qkv_send_y, Y)
        late_sum = color_sums(late_keep_x, late_keep_y, late_x, late_y, late_xy, late_yx)
        late_lo = swap_far(late_sum[2:], 1)
        qkv_x, qkv_y, down_part = together(qkv_x, qkv_y, down_part)
        qkv_xy, qkv_yx = color_nexts(qkv_keep_x, qkv_keep_y, qkv_x, qkv_y)
        qkv_xy, qkv_yx, down_part, *both = together(qkv_xy, qkv_yx, down_part, *keep, *send)
        keep, send = both[:3], both[3:]
        qkv_xy, qkv_yx = swap(qkv_xy, Y), swap(qkv_yx, X)
        down_y, down_x, down_xy = swap(down_part[1, 0], Y), swap(down_part[0, 1], X), swap_both(down_part[1, 1])
        qkv_xy, qkv_yx, late_lo = together(qkv_xy, qkv_yx, late_lo)
        qkv_sum = color_sums(qkv_keep_x, qkv_keep_y, qkv_x, qkv_y, qkv_xy, qkv_yx)
        qkv_sum, late_sum = together(qkv_sum, added(late_sum[:2], late_lo))
        qkv_lo, late_hi = swap_far(qkv_sum[2:], 1), swap_far(late_sum[1], 2)
        qkv_lo, late_hi = together(qkv_lo, late_hi)
        qkv_sum = added(qkv_sum[:2], qkv_lo)
        qkv_sum = added(qkv_sum[0], swap_far(qkv_sum[1], 2))
        late_sum = added(late_sum[0], late_hi)
        late_sum, down_y, down_x, down_xy = together(late_sum, down_y, down_x, down_xy)
        down_sum = down_part[0, 0].astype(F32) + down_y.astype(F32) + down_x.astype(F32) + down_xy.astype(F32)
    inputs_grad = nt(cat([*keep, *send], 1), qkv_full)
    inputs_grad = (grad_one + inputs_grad).astype(BF16)[None]
    wide = hidden // 2
    if far is not None:
        qkv_sum, late_sum = together(qkv_sum, late_sum)
    left, right = own_rows(core, late_sum)
    up_sum = jnp.stack([v[:, :wide].reshape(rows, blocks, piece) for v in (left, right)], 2).reshape(rows, hidden).astype(F32)
    out_sum = cat([left[:, wide:], right[:, wide:]], 1).astype(F32)
    mine, send = choose(core, qkv_sum[0], qkv_sum[1])
    got = swap(send, CORE)
    left, right = choose(core, mine[:, : 3 * near], got[:, : 3 * near])
    if far is not None:
        small_sum = (mine[:lines, 3 * near :].astype(F32) + got[:lines, 3 * near :].astype(F32)).reshape(-1)
    qkv_sum = jnp.stack([v.reshape(rows, 3, near) for v in (left, right)], 2).reshape(rows, 3 * width).astype(F32)
    s = [small_sum[each * i : each * i + each] for i in range(8)]
    return (
        result[None], inputs_grad, qkv_sum, s[0], s[1], out_sum, s[2], s[3], s[4], up_sum, small_sum[8 * each :], down_sum, s[5], s[6], s[7],
    )


def solution(mesh):
    devices = mesh.devices
    split = jax.sharding.Mesh(devices.reshape(devices.shape[0] // 4, 2, 2, devices.shape[1]), ALL)
    rows, vec = P(ALL, None), P(ALL)
    tokens = P(CORE, CTX, None)
    return jax.shard_map(
        shards,
        mesh=split,
        in_specs=(tokens, P(CORE, None), tokens, rows, vec, vec, rows, vec, vec, vec, rows, vec, rows, vec, vec, vec),
        out_specs=(tokens, tokens, rows, vec, vec, rows, vec, vec, vec, rows, vec, rows, vec, vec, vec),
        check_vma=False,
    )
```
